32 devices in a mesh: wide: 8 (over z, x), narrow: 4 (over y, core).
Axes of the slice: x: 2, y: 2, z: 4, core: 2. Of those that a mesh axis runs over, the one named last changes fastest.
Arguments:
- tokens: bfloat16 [32768, 768], P(('wide', 'narrow')), may hold values from -6 to 6
- cotangent: bfloat16 [32768, 768], P(('wide', 'narrow')), may hold values from -6 to 6
- pair_lengths: int32 [64, 4], P(('wide', 'narrow')), may hold values from 1 to 256, 512 in all within a row
- w_query: float32 [768, 768], P(('wide', 'narrow')), may hold values from -0.21875 to 0.21875
- w_key: float32 [768, 768], P(('wide', 'narrow')), may hold values from -0.21875 to 0.21875
- w_value: float32 [768, 768], P(('wide', 'narrow')), may hold values from -0.21875 to 0.21875
- w_output: float32 [768, 768], P(('wide', 'narrow')), may hold values from -0.875 to 0.875
- w_up: float32 [768, 3072], P(('wide', 'narrow')), may hold values from -0.21875 to 0.21875
- w_down: float32 [3072, 768], P(('wide', 'narrow')), may hold values from -0.109375 to 0.109375
- b_query: float32 [768], P(('wide', 'narrow')), may hold values from -3 to 3
- b_value: float32 [768], P(('wide', 'narrow')), may hold values from -3 to 3
- b_output: float32 [768], P(('wide', 'narrow')), may hold values from -3 to 3
- b_up: float32 [3072], P(('wide', 'narrow')), may hold values from -3 to 3
- b_down: float32 [768], P(('wide', 'narrow')), may hold values from -3 to 3
- first_gain: float32 [768], P(('wide', 'narrow')), may hold values from 0.5 to 1.5
- first_shift: float32 [768], P(('wide', 'narrow')), may hold values from -3 to 3
- second_gain: float32 [768], P(('wide', 'narrow')), may hold values from 0.5 to 1.5
- second_shift: float32 [768], P(('wide', 'narrow')), may hold values from -3 to 3
- bucket_bias: float32 [256, 12], P(('wide', 'narrow')), may hold values from -4 to 4
Outputs:
- layer_out: bfloat16 [32768, 768], P(('wide', 'narrow'))
- grad_tokens: bfloat16 [32768, 768], P(('wide', 'narrow'))
- grad_w_query: float32 [768, 768], P(('wide', 'narrow'))
- grad_w_key: float32 [768, 768], P(('wide', 'narrow'))
- grad_w_value: float32 [768, 768], P(('wide', 'narrow'))
- grad_w_output: float32 [768, 768], P(('wide', 'narrow'))
- grad_w_up: float32 [768, 3072], P(('wide', 'narrow'))
- grad_w_down: float32 [3072, 768], P(('wide', 'narrow'))
- grad_b_query: float32 [768], P(('wide', 'narrow'))
- grad_b_value: float32 [768], P(('wide', 'narrow'))
- grad_b_output: float32 [768], P(('wide', 'narrow'))
- grad_b_up: float32 [3072], P(('wide', 'narrow'))
- grad_b_down: float32 [768], P(('wide', 'narrow'))
- grad_first_gain: float32 [768], P(('wide', 'narrow'))
- grad_first_shift: float32 [768], P(('wide', 'narrow'))
- grad_second_gain: float32 [768], P(('wide', 'narrow'))
- grad_second_shift: float32 [768], P(('wide', 'narrow'))
- grad_bucket_bias: float32 [256, 12], P(('wide', 'narrow'))
The draws below stay inside these ranges and needn't reach their ends.
Inputs may be any that keep to these rules, and one draw needn't show every extreme that they name: `pair_lengths`: each row's 4 lengths sum to 512, and the longest pair of every row has exactly 256 tokens.
All inputs are finite; a program needn't handle non-finite values.
Results may differ from the reference program's by a relative error of at most 0.014.
The reference program's roundings to bfloat16 on the way count: a program that leaves them out, or rounds other values in their place, can miss the bound.
Values may be sent and summed in bfloat16 or wider, within the bound.
No kernel may reach another device: no remote copies, remote signals or barrier semaphores. Data moves between devices by JAX's collectives and lax.ppermute only.
A program may use at most 192 MiB of HBM per device.

```python
import math
import jax
import jax.numpy as jnp
import numpy as np
from jax import lax

D = 768
HEADS = 12
FF = 3072
BUCKETS = 256
ROW_LEN = 512
PAIRS = 4
PAIR_MAX = 256
HEAD_DIM = 64
ROWS = 64
TOKENS = 32768


def steps_of(key, dims, cuts, least, largest):
    def one(dim, parts):
        draws = jax.random.uniform(jax.random.fold_in(jax.random.fold_in(key, 6), dim), (parts,), jnp.float32, least / len(cuts), largest / len(cuts))
        return jnp.repeat(jnp.exp(draws), dims[dim] // parts).reshape((-1,) + (1,) * (len(dims) - dim - 1))

    level = one(*cuts[0])
    for cut in cuts[1:]:
        level = level * one(*cut)
    return level


def split_up(count, total, bound, slope):
    loads = [(1 << 20) // math.isqrt(grade ** slope) + 1 for grade in range(2, count + 1)]
    rest, given = total - bound - (count - 1), [1] * (count - 1)
    while rest > 0:
        free = [i for i in range(count - 1) if given[i] < bound]
        whole, left = sum([loads[i] for i in free]), rest
        for i in free:
            more = min(bound - given[i], max(1, left * loads[i] // whole), rest)
            given[i] = given[i] + more
            rest = rest - more
    return np.array([bound] + given)


def ragged(key, number_of, total, limit, slope):
    if number_of == 2:
        one = jax.random.randint(key, (), max(1, total - limit), min(limit, total - 1) + 1)
        return jnp.stack([one, total - one])
    tallies = jnp.asarray(split_up(number_of, total, limit, slope), jnp.int32)
    pairs = (number_of - 1) // 2
    donor, receiver = tallies[1:1 + 2 * pairs:2], tallies[2:2 + 2 * pairs:2]
    margin = jnp.minimum(donor - 1, limit - receiver)
    passed = jax.random.randint(jax.random.fold_in(key, 1), (pairs,), 0, 1 << 20) % (margin + 1)
    tallies = tallies.at[1:1 + 2 * pairs:2].set(donor - passed).at[2:2 + 2 * pairs:2].set(receiver + passed)
    return tallies[jax.random.permutation(jax.random.fold_in(key, 2), number_of)]


def normal_values(rng, shape, scale, limit, shards=(), held_as=jnp.bfloat16):
    loudness = steps_of(rng, shape, shards, -0.22, 0.18) if shards else 1.0
    values = jax.random.normal(rng, shape, jnp.float32) * scale * loudness
    return jnp.minimum(jnp.maximum(values, -limit), limit).astype(held_as)


def setup_inputs(seed: int = 0) -> dict:
    key_list = jax.random.split(jax.random.key(seed), 20)
    tokens = normal_values(key_list[0], (TOKENS, D), 1.0, 6.0, ((0, 32),))
    cotangent = normal_values(key_list[1], (TOKENS, D), 1.0, 6.0, ((0, 32),))
    pair_lengths = jax.vmap(lambda own: ragged(own, PAIRS, ROW_LEN, PAIR_MAX, 2))(jax.random.split(key_list[2], ROWS)).reshape((ROWS, PAIRS)).astype(jnp.int32)
    w_query = normal_values(key_list[3], (D, D), D ** -0.5, 0.21875, ((0, 32),), jnp.float32)
    w_key = normal_values(key_list[4], (D, D), D ** -0.5, 0.21875, ((0, 32),), jnp.float32)
    w_value = normal_values(key_list[5], (D, D), D ** -0.5, 0.21875, ((0, 32),), jnp.float32)
    w_output = normal_values(key_list[6], (D, D), (D // 16) ** -0.5, 0.875, ((0, 32),), jnp.float32)
    w_up = normal_values(key_list[7], (D, FF), D ** -0.5, 0.21875, ((0, 32),), jnp.float32)
    w_down = normal_values(key_list[8], (FF, D), FF ** -0.5, 0.109375, ((0, 32),), jnp.float32)
    b_query = normal_values(key_list[9], (D,), 0.5, 3.0, ((0, 32),), jnp.float32)
    b_value = normal_values(key_list[10], (D,), 0.5, 3.0, ((0, 32),), jnp.float32)
    b_output = normal_values(key_list[11], (D,), 0.5, 3.0, ((0, 32),), jnp.float32)
    b_up = normal_values(key_list[12], (FF,), 0.5, 3.0, ((0, 32),), jnp.float32)
    b_down = normal_values(key_list[13], (D,), 0.5, 3.0, ((0, 32),), jnp.float32)
    first_gain = jnp.clip(1.0 + 0.1 * jax.random.normal(key_list[14], (D,), jnp.float32), 0.5, 1.5)
    first_shift = normal_values(key_list[15], (D,), 0.5, 3.0, ((0, 32),), jnp.float32)
    second_gain = jnp.clip(1.0 + 0.1 * jax.random.normal(key_list[16], (D,), jnp.float32), 0.5, 1.5)
    second_shift = normal_values(key_list[17], (D,), 0.5, 3.0, ((0, 32),), jnp.float32)
    bucket_bias = normal_values(key_list[18], (BUCKETS, HEADS), 1.0, 4.0, ((0, 32),), jnp.float32)
    return dict(tokens=tokens, cotangent=cotangent, pair_lengths=pair_lengths, w_query=w_query, w_key=w_key, w_value=w_value, w_output=w_output, w_up=w_up, w_down=w_down, b_query=b_query, b_value=b_value, b_output=b_output, b_up=b_up, b_down=b_down, first_gain=first_gain, first_shift=first_shift, second_gain=second_gain, second_shift=second_shift, bucket_bias=bucket_bias)


@jax.custom_vjp
def low(v):
    return lax.optimization_barrier(v.astype(jnp.bfloat16)).astype(jnp.float32)

@jax.custom_vjp
def low_back(v):
    return v

def low_keep(v):
    return (low(v), None)

def low_pass(kept, grad):
    return (grad,)

def back_keep(v):
    return (v, None)

def back_low(kept, grad):
    return (low(grad),)
low.defvjp(low_keep, low_pass)
low_back.defvjp(back_keep, back_low)
highest = lax.Precision.HIGHEST
epsilon = 1e-05

def row_layout(row_lengths):
    place = jnp.arange(ROW_LEN, dtype=jnp.int32)
    ending = jnp.cumsum(row_lengths).astype(jnp.int32)
    after = (place[:, None] >= ending[None, :]).astype(jnp.int32)
    segment = lax.optimization_barrier(jnp.sum(after, axis=1)).astype(jnp.int32)
    start = lax.optimization_barrier(jnp.sum(after * row_lengths[None, :], axis=1)).astype(jnp.int32)
    position = place - start
    middle = BUCKETS // 2
    bucket = (jnp.clip(position[None, :] - position[:, None], -middle, middle - 1) + middle).astype(jnp.int32)
    allowed = segment[:, None] == segment[None, :]
    return (bucket, allowed)

def normalize(value, gain, shift):
    center = value - lax.optimization_barrier(jnp.mean(value, axis=-1, keepdims=True))
    inverse = lax.rsqrt(lax.optimization_barrier(jnp.mean(center * center, axis=-1, keepdims=True)) + epsilon)
    return center * inverse * gain + shift

def attend_row(table, query, keys, values, bucket, allowed):
    length = query.shape[0]
    query_heads = query.reshape(length, HEADS, -1)
    key_heads = keys.reshape(length, HEADS, -1)
    value_heads = values.reshape(length, HEADS, -1)
    raw = low_back(jnp.einsum('ihd,jhd->hij', query_heads, key_heads, precision=highest))
    bias = jnp.transpose(table[bucket], (2, 0, 1))
    scores = jnp.where(allowed[None], raw * (1.0 / math.sqrt(HEAD_DIM)) + bias, -1e+30)
    highest_score = lax.optimization_barrier(jnp.max(scores, axis=-1, keepdims=True))
    exponent = jnp.exp(scores - highest_score)
    probs = exponent / lax.optimization_barrier(jnp.sum(exponent, axis=-1, keepdims=True))
    mixed = jnp.einsum('hij,jhd->ihd', low(probs), value_heads, precision=highest)
    return mixed.reshape(length, -1)
checked_row = jax.checkpoint(attend_row)

def project(value, weight):
    return jnp.dot(value, weight, precision=highest)

def layer_forward(params, inputs, bucket, allowed):
    w_query, w_key, w_value, w_output, w_up, w_down, b_query, b_value, b_output, b_up, b_down, first_gain, first_shift, second_gain, second_shift, bucket_bias = tuple((low(entry) for entry in params))
    row_count = bucket.shape[0]
    width = inputs.shape[1]
    source = low(inputs)
    query = low(low_back(project(source, w_query)) + b_query)
    keys = low(low_back(project(source, w_key)))
    values = low(low_back(project(source, w_value)) + b_value)

    def by_row(entry):
        return entry.reshape(row_count, -1, width)
    attended = lax.map(lambda entry: checked_row(bucket_bias, *entry), (by_row(query), by_row(keys), by_row(values), bucket, allowed))
    mixed = low(low_back(attended.reshape(inputs.shape)))
    first = inputs + low_back(project(mixed, w_output)) + b_output
    normed = normalize(first, first_gain, first_shift)
    hidden = low_back(project(low(normed), w_up)) + b_up
    active = low(jax.nn.gelu(hidden, approximate=False))
    second = normed + low_back(project(active, w_down)) + b_down
    return normalize(second, second_gain, second_shift)

def reference(tokens, cotangent, pair_lengths, w_query, w_key, w_value, w_output, w_up, w_down, b_query, b_value, b_output, b_up, b_down, first_gain, first_shift, second_gain, second_shift, bucket_bias):
    params = (w_query, w_key, w_value, w_output, w_up, w_down, b_query, b_value, b_output, b_up, b_down, first_gain, first_shift, second_gain, second_shift, bucket_bias)
    total_tokens = tokens.shape[0]
    width = tokens.shape[1]
    row_count = pair_lengths.shape[0]
    group = math.gcd(row_count, max(1, 4096 // ROW_LEN))
    blocks = row_count // group
    inputs = tokens.astype(jnp.float32).reshape(blocks, group * ROW_LEN, width)
    upstream = cotangent.astype(jnp.float32).reshape(blocks, group * ROW_LEN, width)
    lengths = pair_lengths.reshape(blocks, group, -1)

    def group_step(totals, entry):
        block_in, block_grad, block_lengths = entry
        bucket, allowed = jax.vmap(row_layout)(block_lengths)

        def forward(values, weights):
            return layer_forward(weights, values, bucket, allowed)
        result, pullback = jax.vjp(forward, block_in, params)
        grad_values, grad_weights = pullback(block_grad)
        totals = jax.tree.map(lambda left, right: left + right, totals, grad_weights)
        return (totals, (result.astype(jnp.bfloat16), grad_values.astype(jnp.bfloat16)))
    start = jax.tree.map(jnp.zeros_like, params)
    totals, (outputs, grad_inputs) = lax.scan(group_step, start, (inputs, upstream, lengths))
    return (outputs.reshape(total_tokens, width), grad_inputs.reshape(total_tokens, width), totals[0], totals[1], totals[2], totals[3], totals[4], totals[5], totals[6], totals[7], totals[8], totals[9], totals[10], totals[11], totals[12], totals[13], totals[14], totals[15])
```

```python
from functools import partial
import math

import jax
import jax.numpy as jnp
from jax import lax
from jax.experimental import pallas as pl
from jax.experimental.pallas import tpu as pltpu
from jax.sharding import PartitionSpec as P

WIDE, NARROW = "wide", "narrow"
AXES = (WIDE, NARROW)
Z, X, Y, CORE = range(4)
ROW_LEN = 512
MIB = 1 << 20
bf16, f32 = jnp.bfloat16, jnp.float32
NN = (((1,), (0,)), ((), ()))
NT = (((1,), (1,)), ((), ()))
TN = (((0,), (0,)), ((), ()))


def dot(left, right, dims=NN):
    return lax.dot_general(left, right, dims, preferred_element_type=f32)


def shape_of(shape, dtype):
    return jax.ShapeDtypeStruct(shape, dtype)


def toeplitz(line, ref, head):
    base = jnp.concatenate([pltpu.roll(line, s, 1) if s else line for s in range(8)], axis=0)
    for c in range(16):
        turned = pltpu.roll(base, 8 * c, 1) if c else base
        for b in range(ROW_LEN // 128):
            cut = ROW_LEN - 128 * b
            piece = jnp.concatenate([turned[:, cut:], turned[:, :cut]], axis=1) if b else turned
            first = 128 * b + 8 * c
            ref[head, first : first + 8, :] = piece


def diagonals(ref, head):
    total = None
    for c in range(16):
        turned = None
        for b in range(ROW_LEN // 128):
            first = 128 * b + 8 * c
            piece = ref[head, first : first + 8, :]
            if b:
                piece = jnp.concatenate([piece[:, 128 * b :], piece[:, : 128 * b]], axis=1)
            turned = piece if turned is None else turned + piece
        if c:
            turned = pltpu.roll(turned, ROW_LEN - 8 * c, 1)
        total = turned if total is None else total + turned
    out = total[0:1]
    for s in range(1, 8):
        out = out + pltpu.roll(total[s : s + 1], ROW_LEN - s, 1)
    return out


def forward_kernel(line_ref, segc_ref, segr_ref, qkv_ref, o_ref, p_ref, bias, mask):
    g, r = pl.program_id(0), pl.program_id(1)

    @pl.when(g == 0)
    def _():
        mask[r] = jnp.where(segc_ref[0] == segr_ref[0], 0.0, -1e30)

    @pl.when(r == 0)
    def _():
        for h in range(2):
            toeplitz(line_ref[0, h : h + 1, :], bias, h)

    q, k, v = qkv_ref[:, 0:128], qkv_ref[:, 128:256], qkv_ref[:, 256:384]
    lane = lax.broadcasted_iota(jnp.int32, (ROW_LEN, 128), 1)
    outs = []
    for h in range(2):
        mine = (lane < 64) if h == 0 else (lane >= 64)
        qh = jnp.where(mine, q.astype(f32) * 0.125, 0.0).astype(bf16)
        s = dot(qh, k, NT) + bias[h] + mask[r]
        e = jnp.exp(s - jnp.max(s, axis=1, keepdims=True))
        p = (e * (1.0 / jnp.sum(e, axis=1, keepdims=True))).astype(bf16)
        p_ref[0, h] = p
        outs.append(dot(p, v))
    o_ref[...] = jnp.where(lane < 64, outs[0], outs[1]).astype(bf16)


def attend_forward(lines, segc, segr, qkv):
    pairs, rows = lines.shape[0], segc.shape[0]
    by_pair = lambda g, r: (g, 0, 0)
    by_row = lambda g, r: (r, 0, 0)
    return pl.pallas_call(
        forward_kernel,
        grid=(pairs, rows),
        in_specs=[
            pl.BlockSpec((1, 2, ROW_LEN), by_pair),
            pl.BlockSpec((1, ROW_LEN, 1), by_row),
            pl.BlockSpec((1, 1, ROW_LEN), by_row),
            pl.BlockSpec((ROW_LEN, 384), lambda g, r: (r, g)),
        ],
        out_specs=[
            pl.BlockSpec((ROW_LEN, 128), lambda g, r: (r, g)),
            pl.BlockSpec((1, 2, ROW_LEN, ROW_LEN), lambda g, r: (r, g, 0, 0)),
        ],
        out_shape=[
            shape_of((rows * ROW_LEN, 128 * pairs), bf16),
            shape_of((rows, 2 * pairs, ROW_LEN, ROW_LEN), bf16),
        ],
        scratch_shapes=[pltpu.VMEM((2, ROW_LEN, ROW_LEN), f32), pltpu.VMEM((rows, ROW_LEN, ROW_LEN), f32)],
        compiler_params=pltpu.CompilerParams(vmem_limit_bytes=40 * MIB),
        cost_estimate=pl.CostEstimate(flops=pairs * rows * 10**9, bytes_accessed=pairs * rows * 2 * MIB, transcendentals=0),
    )(lines, segc, segr, qkv)


def backward_kernel(qkv_ref, do_ref, o_ref, p_ref, d_ref, line_ref, sums_ref, acc):
    r, last = pl.program_id(1), pl.num_programs(1) - 1
    q, k, v = qkv_ref[:, 0:128], qkv_ref[:, 128:256], qkv_ref[:, 256:384]
    lane = lax.broadcasted_iota(jnp.int32, (ROW_LEN, 128), 1)
    qt = (q.astype(f32) * 0.125).T.astype(bf16)
    do = do_ref[...].astype(f32)
    dot_t = do.T.astype(bf16)
    prod = do * o_ref[...].astype(f32)
    dqs, dks, dvs = [], [], []
    for h in range(2):
        mine = (lane < 64) if h == 0 else (lane >= 64)
        doh = jnp.where(mine, do, 0.0).astype(bf16)
        delta = jnp.sum(jnp.where(mine, prod, 0.0), axis=1, keepdims=True)
        p = p_ref[0, h]
        ds = p.astype(f32) * (dot(doh, v, NT) - delta)

        @pl.when(r == 0)
        def _():
            acc[h] = ds

        @pl.when(r > 0)
        def _():
            acc[h] += ds

        dsb = ds.astype(bf16)
        half = slice(64 * h, 64 * h + 64)
        dqs.append(dot(dsb, k))
        dks.append(dot(qt[half, :], dsb))
        dvs.append(dot(dot_t[half, :], p))
    dq = jnp.where(lane < 64, dqs[0], dqs[1]) * 0.125
    dk = jnp.concatenate(dks, axis=0).T
    dv = jnp.concatenate(dvs, axis=0).T
    d_ref[:, 0:128] = dq.astype(bf16)
    d_ref[:, 128:256] = dk.astype(bf16)
    d_ref[:, 256:384] = dv.astype(bf16)
    sums = jnp.concatenate([jnp.sum(dq, axis=0, keepdims=True), jnp.sum(dv, axis=0, keepdims=True)], axis=0)

    @pl.when(r == 0)
    def _():
        sums_ref[0] = sums

    @pl.when(r > 0)
    def _():
        sums_ref[0] += sums

    @pl.when(r == last)
    def _():
        for h in range(2):
            line_ref[0, h : h + 1, :] = diagonals(acc, h)


def attend_backward(first, pairs, qkv, do, o, p):
    rows = p.shape[0]
    narrow = pl.BlockSpec((ROW_LEN, 128), lambda g, r: (r, g))
    return pl.pallas_call(
        backward_kernel,
        grid=(pairs, rows),
        in_specs=[
            pl.BlockSpec((ROW_LEN, 384), lambda g, r: (r, g + first)),
            pl.BlockSpec((ROW_LEN, 128), lambda g, r: (r, g + first)),
            pl.BlockSpec((ROW_LEN, 128), lambda g, r: (r, g + first)),
            pl.BlockSpec((1, 2, ROW_LEN, ROW_LEN), lambda g, r: (r, g + first, 0, 0)),
        ],
        out_specs=[
            pl.BlockSpec((ROW_LEN, 384), lambda g, r: (r, g)),
            pl.BlockSpec((1, 2, ROW_LEN), lambda g, r: (g, 0, 0)),
            pl.BlockSpec((1, 2, 128), lambda g, r: (g, 0, 0)),
        ],
        out_shape=[
            shape_of((rows * ROW_LEN, 384 * pairs), bf16),
            shape_of((pairs, 2, ROW_LEN), f32),
            shape_of((pairs, 2, 128), f32),
        ],
        scratch_shapes=[pltpu.VMEM((2, ROW_LEN, ROW_LEN), f32)],
        compiler_params=pltpu.CompilerParams(vmem_limit_bytes=40 * MIB),
        cost_estimate=pl.CostEstimate(flops=pairs * rows * 10**9, bytes_accessed=pairs * rows * 2 * MIB, transcendentals=0),
    )(qkv, do, o, p)


def normalize(value, gain, shift):
    center = value - jnp.mean(value, axis=1, keepdims=True)
    inverse = lax.rsqrt(jnp.mean(center * center, axis=1, keepdims=True) + 1e-5)
    normed = center * inverse
    return normed, inverse, normed * gain + shift


def normalize_back(upstream, normed, inverse, gain):
    scaled = upstream * gain
    return inverse * (
        scaled
        - jnp.mean(scaled, axis=1, keepdims=True)
        - normed * jnp.mean(scaled * normed, axis=1, keepdims=True)
    )


def column_sum(value):
    return jnp.sum(value, axis=0, keepdims=True)


def middle_kernel(
    chunk,
    o_ref, x_ref, c_ref, wo_ref, wu_ref, wd_ref, vec_ref, bu_ref,
    out_ref, dh1_ref, dy1_ref, do_ref, a_ref, g_ref, dy2_ref, dz_ref, vsum_ref, usum_ref,
    slope,
):
    step = pl.program_id(0)
    b_out, b_down, gain1, shift1, gain2, shift2 = [vec_ref[i : i + 1, :] for i in range(6)]
    hidden = wu_ref.shape[1]
    first = x_ref[...].astype(f32) + dot(o_ref[...], wo_ref[...]) + b_out
    n1, r1, a = normalize(first, gain1, shift1)
    ab = a.astype(bf16)
    a_ref[...] = ab
    second = a + b_down
    for f in range(0, hidden, chunk):
        cols = slice(f, f + chunk)
        z = dot(ab, wu_ref[:, cols]) + bu_ref[:, cols]
        mass = 0.5 * (1.0 + lax.erf(z * (1.0 / math.sqrt(2.0))))
        slope[:, cols] = mass + z * jnp.exp(-0.5 * z * z) * (1.0 / math.sqrt(2.0 * math.pi))
        active = (z * mass).astype(bf16)
        g_ref[:, cols] = active
        second = second + dot(active, wd_ref[cols, :])
    n2, r2, out = normalize(second, gain2, shift2)
    out_ref[...] = out.astype(bf16)
    c = c_ref[...].astype(f32)
    dh2 = normalize_back(c, n2, r2, gain2)
    dy2 = dh2.astype(bf16)
    dy2_ref[...] = dy2
    da = dh2
    parts = []
    for f in range(0, hidden, chunk):
        cols = slice(f, f + chunk)
        dz = dot(dy2, wd_ref[cols, :], NT) * slope[:, cols]
        parts.append(column_sum(dz))
        dzb = dz.astype(bf16)
        dz_ref[:, cols] = dzb
        da = da + dot(dzb, wu_ref[:, cols], NT)
    dh1 = normalize_back(da, n1, r1, gain1)
    dh1_ref[...] = dh1
    dy1 = dh1.astype(bf16)
    dy1_ref[...] = dy1
    do_ref[...] = dot(dy1, wo_ref[...], NT).astype(bf16)
    sums = [column_sum(t) for t in (dh1, dh2, da * n1, da, c * n2, c)]
    vsum = jnp.concatenate(sums + [jnp.zeros((2, c.shape[1]), f32)], axis=0)
    usum = jnp.concatenate(parts, axis=1)

    @pl.when(step == 0)
    def _():
        vsum_ref[...] = vsum
        usum_ref[...] = usum

    @pl.when(step > 0)
    def _():
        vsum_ref[...] += vsum
        usum_ref[...] += usum


def middle(o, x, c, wo, wu, wd, vec, bu, block=256, chunk=1024):
    tokens, width = x.shape
    hidden = wu.shape[1]
    by_token = lambda n: pl.BlockSpec((block, n), lambda i: (i, 0))
    whole = lambda a: pl.BlockSpec(a.shape, lambda i: (0, 0), pipeline_mode=pl.Buffered(1))
    return pl.pallas_call(
        partial(middle_kernel, chunk),
        grid=(tokens // block,),
        in_specs=[by_token(width)] * 3 + [whole(a) for a in (wo, wu, wd, vec, bu)],
        out_specs=[by_token(width)] * 5
        + [by_token(hidden), by_token(width), by_token(hidden)]
        + [pl.BlockSpec((8, width), lambda i: (0, 0)), pl.BlockSpec((1, hidden), lambda i: (0, 0))],
        out_shape=[
            shape_of((tokens, width), bf16),
            shape_of((tokens, width), f32),
            shape_of((tokens, width), bf16),
            shape_of((tokens, width), bf16),
            shape_of((tokens, width), bf16),
            shape_of((tokens, hidden), bf16),
            shape_of((tokens, width), bf16),
            shape_of((tokens, hidden), bf16),
            shape_of((8, width), f32),
            shape_of((1, hidden), f32),
        ],
        scratch_shapes=[pltpu.VMEM((block, hidden), f32)],
        compiler_params=pltpu.CompilerParams(vmem_limit_bytes=58 * MIB),
        cost_estimate=pl.CostEstimate(flops=4 * 10**10, bytes_accessed=40 * MIB, transcendentals=0),
    )(o, x, c, wo, wu, wd, vec, bu)


class Links:
    def __init__(self, mesh):
        wide, narrow = mesh.shape[WIDE], mesh.shape[NARROW]
        self.sizes = (wide // 2, 2, narrow // 2, 2)
        w, n = lax.axis_index(WIDE), lax.axis_index(NARROW)
        self.place = (w // 2, w % 2, n // 2, n % 2)
        self.core = self.place[CORE]
        self.chips = wide * narrow // 2

    def number(self, at):
        return ((at[Z] * self.sizes[X] + at[X]) * self.sizes[Y] + at[Y]) * 2 + at[CORE]

    def fetch(self, value, axis, step):
        pairs = []
        for z in range(self.sizes[Z]):
            for x in range(self.sizes[X]):
                for y in range(self.sizes[Y]):
                    for c in range(2):
                        here = (z, x, y, c)
                        there = list(here)
                        there[axis] = (there[axis] + step) % self.sizes[axis]
                        pairs.append((self.number(there), self.number(here)))
        return lax.ppermute(value, AXES, pairs)

    def spread(self, value, axis, at=0):
        others = [self.fetch(value, axis, k) for k in range(1, self.sizes[axis])]
        return jnp.stack([value] + others, axis=at)

    def fold(self, value, axis, at):
        size, me = self.sizes[axis], self.place[axis]
        total = lax.dynamic_index_in_dim(value, me, at, keepdims=False)
        got = []
        for k in range(1, size):
            block = lax.dynamic_index_in_dim(value, (me + k) % size, at, keepdims=False)
            got.append(self.fetch(block.astype(bf16), axis, size - k))
        for piece in got:
            total = total + piece.astype(f32)
        return total

    def gather(self, left, right):
        even = self.core == 0
        kept, sent = jnp.where(even, left, right), jnp.where(even, right, left)
        got = self.fetch(sent, CORE, 1)
        both = jnp.stack([jnp.where(even, kept, got), jnp.where(even, got, kept)])
        both = self.spread(both, Z, 1)
        first = self.spread(self.spread(both[0], X), Y)
        second = self.spread(self.spread(both[1], Y), X)
        rest = (self.chips,) + left.shape
        mine = jnp.stack([first.reshape(rest), second.reshape(rest)])
        return mine, self.fetch(mine, CORE, 1)

    def order(self):
        chip = jnp.arange(self.chips, dtype=jnp.int32)
        sz, sx, sy = self.sizes[:3]
        kz = (chip // (sx * sy) - self.place[Z]) % sz
        kx = (chip // sy - self.place[X]) % sx
        ky = (chip - self.place[Y]) % sy
        return jnp.concatenate(
            [(ky * sx + kx) * sz + kz, (kx * sy + ky) * sz + kz, self.core.reshape(1)]
        ).astype(jnp.int32)

    def scatter(self, pieces):
        even = self.core == 0
        left, right = [jnp.concatenate(side, axis=-1) for side in pieces]
        kept = jnp.where(even, left, right)
        sent = jnp.where(even, right, left).astype(bf16)
        total = kept + self.fetch(sent, CORE, 1).astype(f32)
        total = total.reshape(self.sizes + total.shape[1:])
        first = self.fold(self.fold(total[:, :, :, 0], Y, 2), X, 1)
        second = self.fold(self.fold(total[:, :, :, 1], X, 1), Y, 1)
        both = self.fold(jnp.stack([first, second], axis=1), Z, 0)
        own = jnp.where(even, both[0], both[1])
        got = self.fetch(jnp.where(even, both[1], both[0]), CORE, 1)
        return jnp.where(even, own, got), jnp.where(even, got, own)


def unpack_kernel(cuts, chips, order_ref, *refs):
    mine, theirs, outs = refs[0:2], refs[2:4], refs[4:]
    core = order_ref[2 * chips]

    def write(left, right):
        for d in range(2):
            rows = jnp.concatenate([left[d][0, 0], right[d][0, 0]], axis=1)
            for out, cut in zip(outs, cuts):
                each = len(cut)
                for i, (start, stop) in enumerate(cut):
                    if isinstance(start, tuple):
                        out[d * each + i] = jnp.concatenate([rows[:, s:t] for s, t in (start, stop)], axis=1)
                    else:
                        out[d * each + i] = rows[:, start:stop]

    @pl.when(core == 0)
    def _():
        write(mine, theirs)

    @pl.when(core == 1)
    def _():
        write(theirs, mine)


def unpack(order, mine, theirs, cuts):
    unused, chips, rows, columns = mine.shape
    block = (1, 1, rows, columns)
    a = pl.BlockSpec(block, lambda i, order: (0, order[i], 0, 0))
    b = pl.BlockSpec(block, lambda i, order: (1, order[i + chips], 0, 0))

    def width(entry):
        start, stop = entry
        return sum(t - s for s, t in entry) if isinstance(start, tuple) else stop - start

    shapes = [(2 * len(cut), rows, width(cut[0])) for cut in cuts]
    return pl.pallas_call(
        partial(unpack_kernel, cuts, chips),
        grid_spec=pltpu.PrefetchScalarGridSpec(
            num_scalar_prefetch=1,
            grid=(chips,),
            in_specs=[a, b, a, b],
            out_specs=[pl.BlockSpec(s, lambda i, order: (i, 0, 0)) for s in shapes],
        ),
        out_shape=[shape_of((chips * s[0],) + s[1:], mine.dtype) for s in shapes],
        compiler_params=pltpu.CompilerParams(vmem_limit_bytes=24 * MIB),
        cost_estimate=pl.CostEstimate(flops=0, bytes_accessed=4 * mine.size * 2, transcendentals=0),
    )(order, mine, mine, theirs, theirs)


def segments(lengths):
    place = jnp.arange(ROW_LEN, dtype=jnp.int32)
    ending = jnp.cumsum(lengths, axis=1)
    return jnp.sum((place[None, :, None] >= ending[:, None, :]).astype(jnp.int32), axis=2)


def interleaved(q, k, v):
    rows = q.shape[0]
    return jnp.stack([t.reshape(rows, -1, 128) for t in (q, k, v)], axis=2).reshape(rows, -1)


def separate(qkv):
    rows = qkv.shape[0]
    parts = qkv.reshape(rows, -1, 3, 128)
    return [parts[:, :, i].reshape(rows, -1) for i in range(3)]


def per_device(
    mesh, tokens, cotangent, pair_lengths, w_query, w_key, w_value, w_output, w_up, w_down, b_query, b_value,
    b_output, b_up, b_down, first_gain, first_shift, second_gain, second_shift, bucket_bias,
):
    links = Links(mesh)
    devices = 2 * links.chips
    rows, width = w_query.shape
    hidden = w_up.shape[1]
    heads = bucket_bias.shape[1]
    buckets = bucket_bias.shape[0] * devices
    ratio = hidden // width
    low = lambda t: t.astype(bf16)

    column = lambda t: t.reshape(rows, -1)
    small = [column(t) for t in (b_query, b_value, b_output, b_down, first_gain, first_shift, second_gain, second_shift, b_up, bucket_bias)]
    small = low(jnp.concatenate(small, axis=1))
    small = jnp.pad(small, ((0, 0), (0, 128 - small.shape[1])))
    square = interleaved(low(w_query), low(w_key), low(w_value))
    half = square.shape[1] // 2
    order = links.order()

    got = links.gather(
        jnp.concatenate([square[:, :half], small], axis=1),
        jnp.concatenate([square[:, half:], jnp.zeros_like(small)], axis=1),
    )
    w_half, h_half = width // 2, hidden // 2
    up_low, out_low = low(w_up), low(w_output)
    got_up = links.gather(
        jnp.concatenate([out_low[:, :w_half], up_low[:, :h_half]], axis=1),
        jnp.concatenate([out_low[:, w_half:], up_low[:, h_half:]], axis=1),
    )
    down_low = low(w_down)
    got_down = links.gather(down_low[:, :w_half], down_low[:, w_half:])

    side = half + 128
    full, small = unpack(order, *got, [[((0, half), (side, side + half))], [(half, side)]])
    full = full.reshape(width, 2 * half)
    small = small.reshape(width, 128).astype(f32)
    table = small[:, 12:16].reshape(buckets, heads).T
    ends = [jnp.broadcast_to(table[:, i : i + 1], (heads, 128)) for i in (buckets - 1, 0)]
    middle_bucket = buckets // 2
    lines = jnp.concatenate([table[:, middle_bucket:], *ends, table[:, :middle_bucket]], axis=1)
    lines = lines.reshape(heads // 2, 2, ROW_LEN)
    vectors = small[:, :8].T
    zero = jnp.zeros((width,), f32)
    bias = interleaved(vectors[0:1], zero[None], vectors[1:2])
    segment = segments(pair_lengths)

    qkv = low(dot(tokens, full) + bias)
    mixed, probs = attend_forward(lines, segment[:, :, None], segment[:, None, :], qkv)

    out_cut = [((0, w_half), (w_half + h_half, 2 * w_half + h_half))]
    up_cut = [((w_half, w_half + h_half), (2 * w_half + h_half, 2 * w_half + 2 * h_half))]
    full_out, full_up = unpack(order, *got_up, [out_cut, up_cut])
    (full_down,) = unpack(order, *got_down, [[(0, width)]])
    result, dh1, dy1, do, settled, active, dy2, dz, vsum, usum = middle(
        mixed,
        tokens,
        cotangent,
        full_out.reshape(width, width),
        full_up.reshape(width, hidden),
        full_down.reshape(hidden, width),
        vectors[2:],
        small[:, 8:12].reshape(1, hidden),
    )
    by_device = lambda t: t.reshape(devices, -1, t.shape[-1])
    grad_down = by_device(dot(active, dy2, TN))
    down_sum = links.scatter([[grad_down[..., :w_half]], [grad_down[..., w_half:]]])
    grad_up = by_device(dot(settled, dz, TN))
    grad_out = by_device(dot(mixed, dy1, TN))
    up_sum = links.scatter(
        [
            [grad_out[..., :w_half], grad_up[..., :h_half]],
            [grad_out[..., w_half:], grad_up[..., h_half:]],
        ]
    )
    half_pairs = heads // 4
    grads = [attend_backward(first, half_pairs, qkv, do, mixed, probs) for first in (0, half_pairs)]
    d_left, d_right = grads[0][0], grads[1][0]
    sums = jnp.concatenate([g[2] for g in grads], axis=0)
    g_query, g_value = sums[:, 0].reshape(width), sums[:, 1].reshape(width)
    line = jnp.concatenate([g[1] for g in grads], axis=0).reshape(heads, ROW_LEN)
    upper, lower = line[:, :middle_bucket], line[:, ROW_LEN - middle_bucket :]
    upper = upper.at[:, -1].add(jnp.sum(line[:, middle_bucket : ROW_LEN // 2], axis=1))
    lower = lower.at[:, 0].add(jnp.sum(line[:, ROW_LEN // 2 : ROW_LEN - middle_bucket], axis=1))
    g_table = jnp.concatenate([lower, upper], axis=1).T.reshape(width, -1)
    tall = [t.reshape(width, -1) for t in (g_query, g_value, vsum[0], vsum[1], vsum[2], vsum[3], vsum[4], vsum[5], usum[0])]
    g_small = jnp.concatenate(tall + [g_table], axis=1)
    g_small = by_device(jnp.pad(g_small, ((0, 0), (0, 128 - g_small.shape[1]))))
    g_left, g_right = by_device(dot(tokens, d_left, TN)), by_device(dot(tokens, d_right, TN))
    square_sum = links.scatter([[g_left, g_small], [g_right, jnp.zeros_like(g_small)]])
    grad_tokens = low(dh1 + dot(d_left, full[:, :half], NT) + dot(d_right, full[:, half:], NT))

    left, right = square_sum
    out_query, out_key, out_value = separate(jnp.concatenate([left[:, :half], right[:, :half]], axis=1))
    own = left[:, half:]
    flat = [own[:, i] for i in range(8)]
    whole = lambda pair, start, stop: jnp.concatenate([pair[0][:, start:stop], pair[1][:, start:stop]], axis=1)
    return (
        result,
        grad_tokens,
        out_query,
        out_key,
        out_value,
        whole(up_sum, 0, w_half),
        whole(up_sum, w_half, w_half + h_half),
        whole(down_sum, 0, w_half),
        flat[0],
        flat[1],
        flat[2],
        own[:, 8:12].reshape(-1),
        flat[3],
        flat[4],
        flat[5],
        flat[6],
        flat[7],
        own[:, 12:16].reshape(-1, heads),
    )


def solution(mesh):
    split, line = P(AXES, None), P(AXES)
    return jax.shard_map(
        partial(per_device, mesh),
        mesh=mesh,
        in_specs=(split,) * 9 + (line,) * 9 + (split,),
        out_specs=(split,) * 8 + (line,) * 9 + (split,),
        check_vma=False,
    )
```

```python
from functools import partial
import math

import jax
import jax.numpy as jnp
from jax import lax
from jax.experimental import pallas as pl
from jax.experimental.pallas import tpu as pltpu
from jax.sharding import PartitionSpec as P

WIDE, NARROW = "wide", "narrow"
AXES = (WIDE, NARROW)
Z, X, Y, CORE = range(4)
ROW_LEN = 512
MIB = 1 << 20
bf16, f32 = jnp.bfloat16, jnp.float32
NN = (((1,), (0,)), ((), ()))
NT = (((1,), (1,)), ((), ()))
TN = (((0,), (0,)), ((), ()))


def dot(left, right, dims=NN):
    return lax.dot_general(left, right, dims, preferred_element_type=f32)


def shape_of(shape, dtype):
    return jax.ShapeDtypeStruct(shape, dtype)


def toeplitz(line, ref, head):
    base = jnp.concatenate([pltpu.roll(line, s, 1) if s else line for s in range(8)], axis=0)
    for c in range(16):
        turned = pltpu.roll(base, 8 * c, 1) if c else base
        for b in range(ROW_LEN // 128):
            cut = ROW_LEN - 128 * b
            piece = jnp.concatenate([turned[:, cut:], turned[:, :cut]], axis=1) if b else turned
            first = 128 * b + 8 * c
            ref[head, first : first + 8, :] = piece


def diagonals(ref, head):
    total = None
    for c in range(16):
        turned = None
        for b in range(ROW_LEN // 128):
            first = 128 * b + 8 * c
            piece = ref[head, first : first + 8, :]
            if b:
                piece = jnp.concatenate([piece[:, 128 * b :], piece[:, : 128 * b]], axis=1)
            turned = piece if turned is None else turned + piece
        if c:
            turned = pltpu.roll(turned, ROW_LEN - 8 * c, 1)
        total = turned if total is None else total + turned
    out = total[0:1]
    for s in range(1, 8):
        out = out + pltpu.roll(total[s : s + 1], ROW_LEN - s, 1)
    return out


def forward_kernel(first_ref, line_ref, segc_ref, segr_ref, qkv_ref, *refs):
    o_ref, p_ref, bias, mask = refs[-4:]
    g, r = pl.program_id(0), pl.program_id(1)

    @pl.when(g == 0)
    def _():
        mask[r] = jnp.where(segc_ref[0] == segr_ref[0], 0.0, -1e30)

    @pl.when(r == 0)
    def _():
        for h in range(2):
            toeplitz(line_ref[0, h : h + 1, :], bias, h)

    q, k, v = qkv_ref[:, 0:128], qkv_ref[:, 128:256], qkv_ref[:, 256:384]
    lane = lax.broadcasted_iota(jnp.int32, (ROW_LEN, 128), 1)
    outs = []
    for h in range(2):
        mine = (lane < 64) if h == 0 else (lane >= 64)
        qh = jnp.where(mine, q.astype(f32) * 0.125, 0.0).astype(bf16)
        s = dot(qh, k, NT) + bias[h] + mask[r]
        e = jnp.exp(s - jnp.max(s, axis=1, keepdims=True))
        p = (e * (1.0 / jnp.sum(e, axis=1, keepdims=True))).astype(bf16)
        p_ref[0, h] = p
        outs.append(dot(p, v))
    o_ref[...] = jnp.where(lane < 64, outs[0], outs[1]).astype(bf16)


def attend_forward(first, lines, segc, segr, qkv, after=()):
    pairs, rows = qkv.shape[1] // 384, segc.shape[0]
    return pl.pallas_call(
        forward_kernel,
        grid_spec=pltpu.PrefetchScalarGridSpec(
            num_scalar_prefetch=1,
            grid=(pairs, rows),
            in_specs=[
                pl.BlockSpec((1, 2, ROW_LEN), lambda g, r, first: (g + first[0], 0, 0)),
                pl.BlockSpec((1, ROW_LEN, 1), lambda g, r, first: (r, 0, 0)),
                pl.BlockSpec((1, 1, ROW_LEN), lambda g, r, first: (r, 0, 0)),
                pl.BlockSpec((ROW_LEN, 384), lambda g, r, first: (r, g)),
            ]
            + [pl.BlockSpec(memory_space=pl.ANY)] * len(after),
            out_specs=[
                pl.BlockSpec((ROW_LEN, 128), lambda g, r, first: (r, g)),
                pl.BlockSpec((1, 2, ROW_LEN, ROW_LEN), lambda g, r, first: (r, g, 0, 0)),
            ],
            scratch_shapes=[pltpu.VMEM((2, ROW_LEN, ROW_LEN), f32), pltpu.VMEM((rows, ROW_LEN, ROW_LEN), f32)],
        ),
        out_shape=[
            shape_of((rows * ROW_LEN, 128 * pairs), bf16),
            shape_of((rows, 2 * pairs, ROW_LEN, ROW_LEN), bf16),
        ],
        compiler_params=pltpu.CompilerParams(vmem_limit_bytes=36 * MIB),
        cost_estimate=pl.CostEstimate(flops=pairs * rows * 2 * 10**9, bytes_accessed=pairs * rows * 2 * MIB, transcendentals=0),
    )(first, lines, segc, segr, qkv, *after)


def backward_kernel(qkv_ref, do_ref, o_ref, p_ref, *refs):
    d_ref, line_ref, sums_ref, acc = refs[-4:]
    r, last = pl.program_id(1), pl.num_programs(1) - 1
    q, k, v = qkv_ref[:, 0:128], qkv_ref[:, 128:256], qkv_ref[:, 256:384]
    lane = lax.broadcasted_iota(jnp.int32, (ROW_LEN, 128), 1)
    qt = (q.astype(f32) * 0.125).T.astype(bf16)
    do = do_ref[...].astype(f32)
    dot_t = do.T.astype(bf16)
    prod = do * o_ref[...].astype(f32)
    dqs, dks, dvs = [], [], []
    for h in range(2):
        mine = (lane < 64) if h == 0 else (lane >= 64)
        doh = jnp.where(mine, do, 0.0).astype(bf16)
        delta = jnp.sum(jnp.where(mine, prod, 0.0), axis=1, keepdims=True)
        p = p_ref[0, h]
        ds = p.astype(f32) * (dot(doh, v, NT) - delta)

        @pl.when(r == 0)
        def _():
            acc[h] = ds

        @pl.when(r > 0)
        def _():
            acc[h] += ds

        dsb = ds.astype(bf16)
        half = slice(64 * h, 64 * h + 64)
        dqs.append(dot(dsb, k))
        dks.append(dot(qt[half, :], dsb))
        dvs.append(dot(dot_t[half, :], p))
    dq = jnp.where(lane < 64, dqs[0], dqs[1]) * 0.125
    dk = jnp.concatenate(dks, axis=0).T
    dv = jnp.concatenate(dvs, axis=0).T
    d_ref[:, 0:128] = dq.astype(bf16)
    d_ref[:, 128:256] = dk.astype(bf16)
    d_ref[:, 256:384] = dv.astype(bf16)
    sums = jnp.concatenate([jnp.sum(dq, axis=0, keepdims=True), jnp.sum(dv, axis=0, keepdims=True)], axis=0)

    @pl.when(r == 0)
    def _():
        sums_ref[0] = sums

    @pl.when(r > 0)
    def _():
        sums_ref[0] += sums

    @pl.when(r == last)
    def _():
        for h in range(2):
            line_ref[0, h : h + 1, :] = diagonals(acc, h)


def attend_backward(qkv, do, o, p, after=()):
    rows, pairs = p.shape[0], qkv.shape[1] // 384
    half = pl.BlockSpec((ROW_LEN, 128), lambda g, r: (r, g))
    wide = pl.BlockSpec((ROW_LEN, 384), lambda g, r: (r, g))
    return pl.pallas_call(
        backward_kernel,
        grid=(pairs, rows),
        in_specs=[wide, half, half, pl.BlockSpec((1, 2, ROW_LEN, ROW_LEN), lambda g, r: (r, g, 0, 0))]
        + [pl.BlockSpec(memory_space=pl.ANY)] * len(after),
        out_specs=[
            wide,
            pl.BlockSpec((1, 2, ROW_LEN), lambda g, r: (g, 0, 0)),
            pl.BlockSpec((1, 2, 128), lambda g, r: (g, 0, 0)),
        ],
        out_shape=[
            shape_of((rows * ROW_LEN, 384 * pairs), bf16),
            shape_of((pairs, 2, ROW_LEN), f32),
            shape_of((pairs, 2, 128), f32),
        ],
        scratch_shapes=[pltpu.VMEM((2, ROW_LEN, ROW_LEN), f32)],
        compiler_params=pltpu.CompilerParams(vmem_limit_bytes=36 * MIB),
        cost_estimate=pl.CostEstimate(flops=pairs * rows * 2 * 10**9, bytes_accessed=pairs * rows * 2 * MIB, transcendentals=0),
    )(qkv, do, o, p, *after)


def normalize(value, gain, shift):
    center = value - jnp.mean(value, axis=1, keepdims=True)
    inverse = lax.rsqrt(jnp.mean(center * center, axis=1, keepdims=True) + 1e-5)
    normed = center * inverse
    return normed, inverse, normed * gain + shift


def normalize_back(upstream, normed, inverse, gain):
    scaled = upstream * gain
    return inverse * (
        scaled
        - jnp.mean(scaled, axis=1, keepdims=True)
        - normed * jnp.mean(scaled * normed, axis=1, keepdims=True)
    )


def column_sum(value):
    return jnp.sum(value, axis=0, keepdims=True)


def middle_kernel(
    blocks, order_ref,
    om_ref, ot_ref, x_ref, c_ref, vec_ref, bu_ref, uma_ref, umb_ref, uta_ref, utb_ref, dma_ref, dmb_ref, dta_ref, dtb_ref,
    *refs,
):
    (
        out_ref, dh1_ref, a_ref, g_ref, dom_ref, dot_ref, dy1m_ref, dy1t_ref, dy2m_ref, dy2t_ref, dzm_ref, dzt_ref,
        vsum_ref, usum_ref, wo, wu, wd, slope, dy, sems,
    ) = refs[-20:]
    step = pl.program_id(0)
    width, hidden = wu.shape
    core = order_ref[2 * blocks]
    w_half, h_half = width // 2, hidden // 2

    def cols(size, side, first=0, count=None):
        return pl.ds(pl.multiple_of(side * size + first, 128), size if count is None else count)

    @pl.when(step == 0)
    def _():
        up_left = uma_ref.shape[2]
        up_right = h_half - up_left
        rows, deep = uma_ref.shape[1], dma_ref.shape[1]

        def moves(k):
            i, j = order_ref[k], order_ref[blocks + k]
            at, first, second = place(k, rows), place(2 * k, deep), place(2 * k + 1, deep)
            found = []
            for side, ua, ub, da, db in ((core, uma_ref, umb_ref, dma_ref, dmb_ref), (1 - core, uta_ref, utb_ref, dta_ref, dtb_ref)):
                found += [
                    (ub.at[j, :, up_right : up_right + w_half], wo.at[at, cols(w_half, side)]),
                    (ua.at[i], wu.at[at, cols(h_half, side, 0, up_left)]),
                    (ub.at[j, :, 0:up_right], wu.at[at, cols(h_half, side, up_left, up_right)]),
                    (da.at[i], wd.at[first, cols(w_half, side)]),
                    (db.at[j], wd.at[second, cols(w_half, side)]),
                ]
            return found

        copies(moves, sems, blocks)

    rows_of = lambda side: cols(w_half, side)
    b_out, b_down, gain1, shift1, gain2, shift2 = [vec_ref[i : i + 1, :] for i in range(2, 8)]
    first = x_ref[...].astype(f32) + dot(om_ref[...], wo[rows_of(core), :]) + dot(ot_ref[...], wo[rows_of(1 - core), :]) + b_out
    n1, r1, a = normalize(first, gain1, shift1)
    ab = a.astype(bf16)
    a_ref[...] = ab
    second = a + b_down
    chunk = h_half // 2
    for f in range(0, hidden, chunk):
        at = slice(f, f + chunk)
        z = dot(ab, wu[:, at]) + bu_ref[:, at]
        mass = 0.5 * (1.0 + lax.erf(z * (1.0 / math.sqrt(2.0))))
        slope[:, at] = mass + z * jnp.exp(-0.5 * z * z) * (1.0 / math.sqrt(2.0 * math.pi))
        active = (z * mass).astype(bf16)
        g_ref[:, at] = active
        second = second + dot(active, wd[at, :])
    n2, r2, out = normalize(second, gain2, shift2)
    out_ref[...] = out.astype(bf16)
    c = c_ref[...].astype(f32)
    dh2 = normalize_back(c, n2, r2, gain2)
    dy2 = dh2.astype(bf16)
    dy[...] = dy2
    dy2m_ref[...] = dy[:, cols(w_half, core)]
    dy2t_ref[...] = dy[:, cols(w_half, 1 - core)]
    da = dh2
    parts = []
    for side, dz_ref in ((core, dzm_ref), (1 - core, dzt_ref)):
        for f in range(0, h_half, chunk):
            at = cols(h_half, side, f, chunk)
            dz = dot(dy2, wd[at, :], NT) * slope[:, at]
            parts.append((at, column_sum(dz)))
            dzb = dz.astype(bf16)
            dz_ref[:, f : f + chunk] = dzb
            da = da + dot(dzb, wu[:, at], NT)
    dh1 = normalize_back(da, n1, r1, gain1)
    dh1_ref[...] = dh1
    dy1 = dh1.astype(bf16)
    dy[...] = dy1
    dy1m_ref[...] = dy[:, cols(w_half, core)]
    dy1t_ref[...] = dy[:, cols(w_half, 1 - core)]
    dom_ref[...] = dot(dy1, wo[rows_of(core), :], NT).astype(bf16)
    dot_ref[...] = dot(dy1, wo[rows_of(1 - core), :], NT).astype(bf16)
    sums = [column_sum(t) for t in (dh1, dh2, da * n1, da, c * n2, c)]
    vsum = jnp.concatenate(sums + [jnp.zeros((2, c.shape[1]), f32)], axis=0)

    @pl.when(step == 0)
    def _():
        vsum_ref[...] = vsum
        for at, part in parts:
            usum_ref[:, at] = part

    @pl.when(step > 0)
    def _():
        vsum_ref[...] += vsum
        for at, part in parts:
            usum_ref[:, at] += part


def middle(order, om, ot, x, c, vec, bu, up, down, after=(), block=256):
    tokens, width = x.shape
    hidden = bu.shape[1]
    blocks = up[0].shape[0]
    by_token = lambda n: pl.BlockSpec((block, n), lambda i, order: (i, 0))
    fixed = lambda s: pl.BlockSpec(s, lambda i, order: (0, 0))
    half, h_half = width // 2, hidden // 2
    outs = [(width, bf16), (width, f32), (width, bf16), (hidden, bf16)] + [(half, bf16)] * 6 + [(h_half, bf16)] * 2
    return pl.pallas_call(
        partial(middle_kernel, blocks),
        grid_spec=pltpu.PrefetchScalarGridSpec(
            num_scalar_prefetch=1,
            grid=(tokens // block,),
            in_specs=[by_token(half)] * 2
            + [by_token(width)] * 2
            + [fixed(vec.shape), fixed(bu.shape)]
            + [pl.BlockSpec(memory_space=pl.ANY)] * (8 + len(after)),
            out_specs=[by_token(n) for n, _ in outs] + [fixed((8, width)), fixed((1, hidden))],
            scratch_shapes=[
                pltpu.VMEM((width, width), bf16),
                pltpu.VMEM((width, hidden), bf16),
                pltpu.VMEM((hidden, width), bf16),
                pltpu.VMEM((block, hidden), f32),
                pltpu.VMEM((block, width), bf16),
                pltpu.SemaphoreType.DMA((10, blocks)),
            ],
        ),
        out_shape=[shape_of((tokens, n), t) for n, t in outs] + [shape_of((8, width), f32), shape_of((1, hidden), f32)],
        compiler_params=pltpu.CompilerParams(vmem_limit_bytes=50 * MIB),
        cost_estimate=pl.CostEstimate(flops=4 * 10**10, bytes_accessed=40 * MIB, transcendentals=0),
    )(order, om, ot, x, c, vec, bu, *up, *down, *after)


def copies(moves, sems, count):
    def each(k, act):
        for i, (source, target) in enumerate(moves(k)):
            act(pltpu.make_async_copy(source, target, sems.at[i, k]))

    lax.fori_loop(0, count, lambda k, c: (each(k, lambda copy: copy.start()), c)[1], 0)
    lax.fori_loop(0, count, lambda k, c: (each(k, lambda copy: copy.wait()), c)[1], 0)


def place(k, rows):
    return pl.ds(pl.multiple_of(k * rows, rows), rows)


def project_kernel(blocks, order_ref, x_ref, bias_ref, a_ref, b_ref, *refs):
    out_ref, weight, sems = refs[-3:]
    rows = a_ref.shape[1]
    left = a_ref.shape[2]
    right = weight.shape[1] - left

    @pl.when(pl.program_id(0) == 0)
    def _():
        def moves(k):
            at = place(k, rows)
            return [
                (a_ref.at[order_ref[k]], weight.at[at, 0:left]),
                (b_ref.at[order_ref[blocks + k], :, 0:right], weight.at[at, left : left + right]),
            ]

        copies(moves, sems, blocks)

    out_ref[...] = (dot(x_ref[...], weight[...]) + bias_ref[...]).astype(bf16)


def project(order, flip, x, bias, a, b, after=(), block=512):
    tokens, width = x.shape
    blocks, outs = a.shape[0], bias.shape[1] // 2
    half = lambda i, order: (0, 1 - order[2 * blocks] if flip else order[2 * blocks])
    return pl.pallas_call(
        partial(project_kernel, blocks),
        grid_spec=pltpu.PrefetchScalarGridSpec(
            num_scalar_prefetch=1,
            grid=(tokens // block,),
            in_specs=[
                pl.BlockSpec((block, width), lambda i, order: (i, 0)),
                pl.BlockSpec((1, outs), half),
            ]
            + [pl.BlockSpec(memory_space=pl.ANY)] * (2 + len(after)),
            out_specs=pl.BlockSpec((block, outs), lambda i, order: (i, 0)),
            scratch_shapes=[pltpu.VMEM((width, outs), bf16), pltpu.SemaphoreType.DMA((2, blocks))],
        ),
        out_shape=shape_of((tokens, outs), bf16),
        compiler_params=pltpu.CompilerParams(vmem_limit_bytes=24 * MIB),
        cost_estimate=pl.CostEstimate(flops=2 * tokens * width * outs, bytes_accessed=8 * MIB, transcendentals=0),
    )(order, x, bias, a, b, *after)


def token_kernel(blocks, order_ref, base_ref, dm_ref, dt_ref, ma_ref, mb_ref, ta_ref, tb_ref, *refs):
    out_ref, mine, theirs, sems = refs[-4:]
    rows, left = ma_ref.shape[1:]
    right = mine.shape[1] - left

    @pl.when(pl.program_id(0) == 0)
    def _():
        def moves(k):
            at, i, j = place(k, rows), order_ref[k], order_ref[blocks + k]
            return [
                (ma_ref.at[i], mine.at[at, 0:left]),
                (mb_ref.at[j, :, 0:right], mine.at[at, left : left + right]),
                (ta_ref.at[i], theirs.at[at, 0:left]),
                (tb_ref.at[j, :, 0:right], theirs.at[at, left : left + right]),
            ]

        copies(moves, sems, blocks)

    total = base_ref[...] + dot(dm_ref[...], mine[...], NT) + dot(dt_ref[...], theirs[...], NT)
    out_ref[...] = total.astype(bf16)


def token_gradient(order, base, dm, dt, gathered, after=(), block=256):
    tokens, width = base.shape
    blocks, outs = gathered[0].shape[0], dm.shape[1]
    by_token = lambda n: pl.BlockSpec((block, n), lambda i, order: (i, 0))
    return pl.pallas_call(
        partial(token_kernel, blocks),
        grid_spec=pltpu.PrefetchScalarGridSpec(
            num_scalar_prefetch=1,
            grid=(tokens // block,),
            in_specs=[by_token(width), by_token(outs), by_token(outs)]
            + [pl.BlockSpec(memory_space=pl.ANY)] * (4 + len(after)),
            out_specs=by_token(width),
            scratch_shapes=[pltpu.VMEM((width, outs), bf16)] * 2 + [pltpu.SemaphoreType.DMA((4, blocks))],
        ),
        out_shape=shape_of((tokens, width), bf16),
        compiler_params=pltpu.CompilerParams(vmem_limit_bytes=24 * MIB),
        cost_estimate=pl.CostEstimate(flops=4 * tokens * width * outs, bytes_accessed=14 * MIB, transcendentals=0),
    )(order, base, dm, dt, *gathered, *after)


TABLE_AT, UP_AT = 8, 32


def small_block(vectors, table, up):
    rows = vectors[0].shape[0]
    tall = jnp.stack(vectors, axis=1)
    table = jnp.pad(table, ((0, rows - table.shape[0]), (0, UP_AT - TABLE_AT - table.shape[1])))
    up = jnp.pad(up[None], ((0, rows - 1), (0, 128 - UP_AT - up.shape[0])))
    return jnp.concatenate([tall, table, up], axis=1)


def spread_kernel(devices, order_ref, b_ref, line_ref, vec_ref, up_ref, bias_ref, full, tab):
    blocks, rows = b_ref.shape[0:2]
    width, heads = vec_ref.shape[1], line_ref.shape[0]
    for k in range(blocks):
        full[rows * k : rows * k + rows, :] = b_ref[order_ref[blocks + k]].astype(f32)
    each, per, ups = width // devices, tab.shape[0] // devices, up_ref.shape[1] // devices
    vec_ref[...] = full[...].T[0:8, :]
    for d in range(devices):
        tab[per * d : per * d + per, :] = full[each * d : each * d + per, :]
        up_ref[:, ups * d : ups * d + ups] = full[each * d : each * d + 1, UP_AT : UP_AT + ups]
    table = tab[...].T[TABLE_AT : TABLE_AT + heads, :]
    buckets = table.shape[1]
    half, rest = buckets // 2, (ROW_LEN - buckets) // 2
    ends = [jnp.broadcast_to(table[:, i : i + 1], (heads, rest)) for i in (buckets - 1, 0)]
    line_ref[...] = jnp.concatenate([table[:, half:], *ends, table[:, :half]], axis=1)
    for g in range(heads // 2):
        bias_ref[:, 384 * g : 384 * g + 128] = vec_ref[0:1, 128 * g : 128 * g + 128]
        bias_ref[:, 384 * g + 128 : 384 * g + 256] = jnp.zeros((1, 128), f32)
        bias_ref[:, 384 * g + 256 : 384 * g + 384] = vec_ref[1:2, 128 * g : 128 * g + 128]


def spread_small(order, b, devices, width, heads, buckets, hidden):
    blocks, rows = b.shape[0:2]
    last = b.shape[2] // 128 - 1
    fixed = lambda i, order: (0, 0)
    shapes = [(heads, ROW_LEN), (8, width), (1, hidden), (1, 3 * width)]
    return pl.pallas_call(
        partial(spread_kernel, devices),
        grid_spec=pltpu.PrefetchScalarGridSpec(
            num_scalar_prefetch=1,
            grid=(1,),
            in_specs=[pl.BlockSpec((blocks, rows, 128), lambda i, order: (0, 0, last))],
            out_specs=[pl.BlockSpec(s, fixed) for s in shapes],
            scratch_shapes=[pltpu.VMEM((width, 128), f32), pltpu.VMEM((buckets, 128), f32)],
        ),
        out_shape=[shape_of(s, f32) for s in shapes],
        compiler_params=pltpu.CompilerParams(vmem_limit_bytes=8 * MIB),
        cost_estimate=pl.CostEstimate(flops=10**6, bytes_accessed=MIB, transcendentals=0),
    )(order, b)


def collect_kernel(devices, buckets, core_ref, vsum_ref, usum_ref, ms_ref, ts_ref, ml_ref, tl_ref, out_ref, tall, sums, lines):
    core = core_ref[0]
    width = vsum_ref.shape[1]
    pairs = ms_ref.shape[0]
    sums[core], sums[1 - core] = ms_ref[...], ts_ref[...]
    lines[core], lines[1 - core] = ml_ref[...], tl_ref[...]
    tall[...] = jnp.zeros_like(tall)
    tall[2:8, :] = vsum_ref[0:6, :]
    for side in range(2):
        for g in range(pairs):
            at = 128 * (side * pairs + g)
            tall[0:2, at : at + 128] = sums[side, g]
    out_ref[...] = tall[...].T
    line = jnp.concatenate([lines[0], lines[1]], axis=0)
    heads = line.shape[0]
    half, middle = buckets // 2, ROW_LEN // 2
    far = jnp.sum(line[:, half:middle], axis=1, keepdims=True)
    near = jnp.sum(line[:, middle : ROW_LEN - half], axis=1, keepdims=True)
    place = lax.broadcasted_iota(jnp.int32, (heads, half), 1)
    upper = line[:, :half] + jnp.where(place == half - 1, far, 0.0)
    lower = line[:, ROW_LEN - half :] + jnp.where(place == 0, near, 0.0)
    table = jnp.concatenate([lower, upper], axis=1)
    below = jnp.zeros((128 - TABLE_AT - heads, buckets), f32)
    table = jnp.concatenate([jnp.zeros((TABLE_AT, buckets), f32), table, below], axis=0).T
    each, per, ups = width // devices, buckets // devices, usum_ref.shape[1] // devices
    for d in range(devices):
        out_ref[each * d : each * d + per, :] += table[per * d : per * d + per, :]
        out_ref[each * d : each * d + 1, UP_AT : UP_AT + ups] = usum_ref[:, ups * d : ups * d + ups]


def collect_small(core, devices, buckets, vsum, usum, mine, theirs):
    width = vsum.shape[1]
    pairs = mine[1].shape[0]
    flat = lambda t: t.reshape(2 * pairs, ROW_LEN)
    args = [vsum, usum, mine[1], theirs[1], flat(mine[0]), flat(theirs[0])]
    whole = lambda t: pl.BlockSpec(t.shape, lambda i, core: (0,) * t.ndim)
    return pl.pallas_call(
        partial(collect_kernel, devices, buckets),
        grid_spec=pltpu.PrefetchScalarGridSpec(
            num_scalar_prefetch=1,
            grid=(1,),
            in_specs=[whole(t) for t in args],
            out_specs=pl.BlockSpec((width, 128), lambda i, core: (0, 0)),
            scratch_shapes=[
                pltpu.VMEM((128, width), f32),
                pltpu.VMEM((2, pairs, 2, 128), f32),
                pltpu.VMEM((2, 2 * pairs, ROW_LEN), f32),
            ],
        ),
        out_shape=shape_of((width, 128), f32),
        compiler_params=pltpu.CompilerParams(vmem_limit_bytes=8 * MIB),
        cost_estimate=pl.CostEstimate(flops=10**6, bytes_accessed=MIB, transcendentals=0),
    )(core, *args)


class Links:
    def __init__(self, mesh):
        wide, narrow = mesh.shape[WIDE], mesh.shape[NARROW]
        self.sizes = (wide // 2, 2, narrow // 2, 2)
        w, n = lax.axis_index(WIDE), lax.axis_index(NARROW)
        self.place = (w // 2, w % 2, n // 2, n % 2)
        self.core = self.place[CORE]
        self.chips = wide * narrow // 2

    def number(self, at):
        return ((at[Z] * self.sizes[X] + at[X]) * self.sizes[Y] + at[Y]) * 2 + at[CORE]

    def fetch(self, value, axis, step):
        pairs = []
        for z in range(self.sizes[Z]):
            for x in range(self.sizes[X]):
                for y in range(self.sizes[Y]):
                    for c in range(2):
                        here = (z, x, y, c)
                        there = list(here)
                        there[axis] = (there[axis] + step) % self.sizes[axis]
                        pairs.append((self.number(there), self.number(here)))
        return lax.ppermute(value, AXES, pairs)

    def spread(self, value, axis):
        others = [self.fetch(value, axis, k) for k in range(1, self.sizes[axis])]
        return jnp.stack([value] + others)

    def swapped(self, left, right):
        even = self.core == 0
        kept, sent = jnp.where(even, left, right), jnp.where(even, right, left)
        got = self.fetch(sent, CORE, 1)
        return jnp.where(even, kept, got), jnp.where(even, got, kept)

    def along_z(self, a, b):
        cut = a.shape[1]
        both = self.spread(jnp.concatenate([a, b], axis=1), Z)
        return both[:, :, :cut], both[:, :, cut:]

    def plane_1(self, a, b):
        return self.spread(a, X), self.spread(b, Y)

    def plane_2(self, a, b):
        a, b = self.spread(a, Y), self.spread(b, X)
        return a.reshape((self.chips,) + a.shape[3:]), b.reshape((self.chips,) + b.shape[3:])

    def order(self):
        chip = jnp.arange(self.chips, dtype=jnp.int32)
        sz, sx, sy = self.sizes[:3]
        kz = (chip // (sx * sy) - self.place[Z]) % sz
        kx = (chip // sy - self.place[X]) % sx
        ky = (chip - self.place[Y]) % sy
        return jnp.concatenate(
            [(ky * sx + kx) * sz + kz, (kx * sy + ky) * sz + kz, self.core.reshape(1)]
        ).astype(jnp.int32)

    def fold(self, block_of, axis):
        size, me = self.sizes[axis], self.place[axis]
        got = []
        for k in range(1, size):
            got.append(self.fetch(block_of((me + k) % size).astype(bf16), axis, size - k))
        total = block_of(me)
        for piece in got:
            total = total + piece.astype(f32)
        return total

    def fold_1(self, kept, got):
        take = lambda t, i, at: lax.dynamic_index_in_dim(t, i, at, keepdims=False).astype(f32)
        a = self.fold(lambda i: take(kept[0], i, 2) + take(got[0], i, 2), Y)
        b = self.fold(lambda i: take(kept[1], i, 1) + take(got[1], i, 1), X)
        return a, b

    def fold_2(self, a, b):
        take = lambda t, i: lax.dynamic_index_in_dim(t, i, 1, keepdims=False)
        return self.fold(lambda i: take(a, i), X), self.fold(lambda i: take(b, i), Y)

    def fold_z(self, a, b, axis):
        cut = a.shape[axis]
        total = self.fold(lambda i: lax.dynamic_index_in_dim(jnp.concatenate([a, b], axis=axis), i, 0, keepdims=False), Z)
        return total

    def finish(self, total):
        rows = total.shape[0] // 2
        even = self.core == 0
        own = jnp.where(even, total[:rows], total[rows:])
        got = self.fetch(jnp.where(even, total[rows:], total[:rows]), CORE, 1)
        return jnp.where(even, own, got), jnp.where(even, got, own)


def segments(lengths):
    place = jnp.arange(ROW_LEN, dtype=jnp.int32)
    ending = jnp.cumsum(lengths, axis=1)
    return jnp.sum((place[None, :, None] >= ending[:, None, :]).astype(jnp.int32), axis=2)


def interleaved(q, k, v):
    rows = q.shape[0]
    return jnp.stack([t.reshape(rows, -1, 128) for t in (q, k, v)], axis=2).reshape(rows, -1)


def separate(qkv):
    rows = qkv.shape[0]
    parts = qkv.reshape(rows, -1, 3, 128)
    return [parts[:, :, i].reshape(rows, -1) for i in range(3)]


def per_device(
    mesh, tokens, cotangent, pair_lengths, w_query, w_key, w_value, w_output, w_up, w_down, b_query, b_value,
    b_output, b_up, b_down, first_gain, first_shift, second_gain, second_shift, bucket_bias,
):
    links = Links(mesh)
    devices = 2 * links.chips
    rows, width = w_query.shape
    hidden = w_up.shape[1]
    heads = bucket_bias.shape[1]
    buckets = bucket_bias.shape[0] * devices
    w_half, h_half = width // 2, hidden // 2
    low = lambda t: t.astype(bf16)
    barrier = lax.optimization_barrier
    core = links.core
    even = core == 0
    order = links.order()
    if (2 * rows) % 16 or w_down.shape[0] % 16:
        found = order

        def blocks(a, b):
            a, b = jnp.take(a, found[: links.chips], axis=0), jnp.take(b, found[links.chips : 2 * links.chips], axis=0)
            return a.reshape(1, -1, a.shape[2]), b.reshape(1, -1, b.shape[2])

        order = jnp.concatenate([jnp.zeros((2,), jnp.int32), core.reshape(1)])
    else:
        blocks = lambda a, b: (a, b)

    def deep(a, b):
        if order.shape[0] > 3:
            return a, b
        a, b = jnp.take(a, found[: links.chips], axis=0), jnp.take(b, found[links.chips : 2 * links.chips], axis=0)
        full = jnp.stack([a, b], axis=1).reshape(2, -1, a.shape[2])
        return full[0:1], full[1:2]

    small = low(
        small_block(
            [b_query, b_value, b_output, b_down, first_gain, first_shift, second_gain, second_shift], bucket_bias, b_up
        )
    )
    square = interleaved(low(w_query), low(w_key), low(w_value))
    half = square.shape[1] // 2
    cut = (half + 128) // 256 * 128
    first_rows, second_rows = links.swapped(
        jnp.concatenate([square[:, :half], small], axis=1), jnp.concatenate([square[:, half:], small], axis=1)
    )
    pair = jnp.concatenate([first_rows, second_rows], axis=0)
    sa, sb = links.along_z(pair[:, :cut], pair[:, cut:])
    up_low, out_low, down_low = low(w_up), low(w_output), low(w_down)
    first_rows, second_rows = links.swapped(
        jnp.concatenate([up_low[:, :h_half], out_low[:, :w_half]], axis=1),
        jnp.concatenate([up_low[:, h_half:], out_low[:, w_half:]], axis=1),
    )
    up_pair = jnp.concatenate([first_rows, second_rows], axis=0)
    up_cut = (h_half + w_half + 128) // 256 * 128
    down_pair = links.swapped(down_low[:, :w_half], down_low[:, w_half:])

    sa, sb, up_pair, *down_pair = barrier((sa, sb, up_pair, *down_pair))
    plane = links.plane_1(sa, sb)
    ua, ub = links.along_z(up_pair[:, :up_cut], up_pair[:, up_cut:])
    mine_a, mine_b, ua, ub, *down_pair = barrier((*links.plane_2(*plane), ua, ub, *down_pair))

    theirs = (links.fetch(mine_a, CORE, 1), links.fetch(mine_b, CORE, 1))
    up_plane = links.plane_1(ua, ub)
    down_z = links.spread(jnp.concatenate(down_pair, axis=1), Z)
    mine = blocks(mine_a, mine_b)
    theirs = blocks(*theirs)
    lines, vectors, up_bias, bias = spread_small(order, mine[1], devices, width, heads, buckets, hidden)
    lines = lines.reshape(heads // 2, 2, ROW_LEN)
    segment = segments(pair_lengths)
    segc, segr = segment[:, :, None], segment[:, None, :]
    pairs = heads // 4
    first_m, first_t = (core * pairs).reshape(1), ((1 - core) * pairs).reshape(1)
    qkv_m = project(order, False, tokens, bias, *mine)
    qkv_t = project(order, True, tokens, bias, *theirs)
    qkv_m, qkv_t, up_1, up_2, down_z = barrier((qkv_m, qkv_t, *up_plane, down_z))

    up_mine = links.plane_2(up_1, up_2)
    down_plane = links.plane_1(down_z[:, :, :w_half], down_z[:, :, w_half:])
    o_m, p_m = attend_forward(first_m, lines, segc, segr, qkv_m)
    o_t, p_t = attend_forward(first_t, lines, segc, segr, qkv_t)
    o_m, o_t, up_a, up_b, down_1, down_2 = barrier((o_m, o_t, *up_mine, *down_plane))

    up_theirs = (links.fetch(up_a, CORE, 1), links.fetch(up_b, CORE, 1))
    down_mine = links.plane_2(down_1, down_2)
    down_theirs = (links.fetch(down_mine[0], CORE, 1), links.fetch(down_mine[1], CORE, 1))

    result, dh1, settled, active, do_m, do_t, dy1_m, dy1_t, dy2_m, dy2_t, dz_m, dz_t, vsum, usum = middle(
        order,
        o_m,
        o_t,
        tokens,
        cotangent,
        vectors,
        up_bias,
        blocks(up_a, up_b) + blocks(*up_theirs),
        deep(*down_mine) + deep(*down_theirs),
    )

    by_chip = lambda t: t.reshape(links.sizes[:3] + (-1, t.shape[1]))

    def by_row(t):
        t = t.reshape(links.sizes[:3] + (2, -1, t.shape[1]))
        return t[:, :, :, 0], t[:, :, :, 1]

    def exchange(ab):
        return tuple(links.fetch(low(t), CORE, 1) for t in ab)

    o_both = jnp.where(even, jnp.concatenate([o_m, o_t], axis=1), jnp.concatenate([o_t, o_m], axis=1))

    def up_parts(dz, dy1):
        up, out = dot(settled, dz, TN), dot(o_both, dy1, TN)
        return by_chip(up[:, :up_cut]), by_chip(jnp.concatenate([up[:, up_cut:], out], axis=1))

    def square_parts(d):
        g = dot(tokens, d, TN)
        return by_chip(g[:, :cut]), by_chip(jnp.concatenate([g[:, cut:], g_small], axis=1))

    def together(*groups):
        sizes = [len(g) for g in groups]
        flat = barrier(tuple(t for g in groups for t in g))
        out = []
        for size in sizes:
            out.append(flat[:size])
            flat = flat[size:]
        return out

    down_got = exchange(by_row(dot(active, dy2_t, TN)))
    down_kept = by_row(dot(active, dy2_m, TN))
    down_got, down_kept, (do_t, dz_t, dy1_t) = together(down_got, down_kept, (do_t, dz_t, dy1_t))
    fold = links.fold_1(down_kept, down_got)
    grads_t = attend_backward(qkv_t, do_t, o_t, p_t)
    fold, grads_t, (dz_t, dy1_t) = together(fold, grads_t, (dz_t, dy1_t))
    fold = links.fold_2(*fold)
    up_got = exchange(up_parts(dz_t, dy1_t))
    up_kept = up_parts(dz_m, dy1_m)
    down_fold, up_got, up_kept, (do_m,) = together(fold, up_got, up_kept, (do_m,))
    down_total = links.fold_z(*down_fold, 1)
    fold = links.fold_1(up_kept, up_got)
    grads_m = attend_backward(qkv_m, do_m, o_m, p_m)
    fold, grads_m, (down_total,), grads_t = together(fold, grads_m, (down_total,), grads_t)
    fold = links.fold_2(*fold)
    g_small = collect_small(core.reshape(1), devices, buckets, vsum, usum, grads_m[1:], grads_t[1:])
    square_got = exchange(square_parts(grads_t[0]))
    square_kept = square_parts(grads_m[0])
    up_fold, square_got, square_kept, (d_m, d_t) = together(fold, square_got, square_kept, (grads_m[0], grads_t[0]))
    up_total = links.fold_z(*up_fold, 2)
    fold = links.fold_1(square_kept, square_got)
    grad_tokens = token_gradient(order, dh1, d_m, d_t, mine + theirs)
    fold, (up_total, grad_tokens) = together(fold, (up_total, grad_tokens))
    square_total = links.fold_z(*links.fold_2(*fold), 2)

    down_l, down_r = links.finish(down_total)
    up_l, up_r = links.finish(up_total)
    own_small = jnp.where(even, square_total[:rows, half:], square_total[rows:, half:])
    left, right = links.finish(square_total[:, :half])
    out_query, out_key, out_value = separate(jnp.concatenate([left, right], axis=1))
    flat = [own_small[:, i] for i in range(8)]
    whole = lambda start, stop: jnp.concatenate([up_l[:, start:stop], up_r[:, start:stop]], axis=1)
    table_rows = bucket_bias.shape[0]
    return (
        result,
        grad_tokens,
        out_query,
        out_key,
        out_value,
        whole(h_half, h_half + w_half),
        whole(0, h_half),
        jnp.concatenate([down_l, down_r], axis=1),
        flat[0],
        flat[1],
        flat[2],
        own_small[0, UP_AT : UP_AT + b_up.shape[0]],
        flat[3],
        flat[4],
        flat[5],
        flat[6],
        flat[7],
        own_small[:table_rows, TABLE_AT : TABLE_AT + heads],
    )


def solution(mesh):
    split, line = P(AXES, None), P(AXES)
    return jax.shard_map(
        partial(per_device, mesh),
        mesh=mesh,
        in_specs=(split,) * 9 + (line,) * 9 + (split,),
        out_specs=(split,) * 8 + (line,) * 9 + (split,),
        check_vma=False,
    )
```

```python
from functools import partial
import math

import jax
import jax.numpy as jnp
from jax import lax
from jax.experimental import pallas as pl
from jax.experimental.pallas import tpu as pltpu
from jax.sharding import PartitionSpec as P

WIDE, NARROW = "wide", "narrow"
AXES = (WIDE, NARROW)
Z, X, Y, CORE = range(4)
ROW_LEN = 512
MIB = 1 << 20
bf16, f32 = jnp.bfloat16, jnp.float32
NN = (((1,), (0,)), ((), ()))
NT = (((1,), (1,)), ((), ()))
TN = (((0,), (0,)), ((), ()))


def dot(left, right, dims=NN):
    return lax.dot_general(left, right, dims, preferred_element_type=f32)


def shape_of(shape, dtype):
    return jax.ShapeDtypeStruct(shape, dtype)


def toeplitz(line, ref, head):
    base = jnp.concatenate([pltpu.roll(line, s, 1) if s else line for s in range(8)], axis=0)
    for c in range(16):
        turned = pltpu.roll(base, 8 * c, 1) if c else base
        for b in range(ROW_LEN // 128):
            cut = ROW_LEN - 128 * b
            piece = jnp.concatenate([turned[:, cut:], turned[:, :cut]], axis=1) if b else turned
            first = 128 * b + 8 * c
            ref[head, first : first + 8, :] = piece


def diagonals(ref, head):
    total = None
    for c in range(16):
        turned = None
        for b in range(ROW_LEN // 128):
            first = 128 * b + 8 * c
            piece = ref[head, first : first + 8, :]
            if b:
                piece = jnp.concatenate([piece[:, 128 * b :], piece[:, : 128 * b]], axis=1)
            turned = piece if turned is None else turned + piece
        if c:
            turned = pltpu.roll(turned, ROW_LEN - 8 * c, 1)
        total = turned if total is None else total + turned
    out = total[0:1]
    for s in range(1, 8):
        out = out + pltpu.roll(total[s : s + 1], ROW_LEN - s, 1)
    return out


def forward_kernel(first_ref, line_ref, segc_ref, segr_ref, qkv_ref, *refs):
    o_ref, p_ref, bias, mask = refs[-4:]
    g, r = pl.program_id(0), pl.program_id(1)

    @pl.when(g == 0)
    def _():
        mask[r] = jnp.where(segc_ref[0] == segr_ref[0], 0.0, -1e30)

    @pl.when(r == 0)
    def _():
        for h in range(2):
            toeplitz(line_ref[0, h : h + 1, :], bias, h)

    q, k, v = qkv_ref[:, 0:128], qkv_ref[:, 128:256], qkv_ref[:, 256:384]
    lane = lax.broadcasted_iota(jnp.int32, (ROW_LEN, 128), 1)
    outs = []
    for h in range(2):
        mine = (lane < 64) if h == 0 else (lane >= 64)
        qh = jnp.where(mine, q.astype(f32) * 0.125, 0.0).astype(bf16)
        s = dot(qh, k, NT) + bias[h] + mask[r]
        e = jnp.exp(s - jnp.max(s, axis=1, keepdims=True))
        p = (e * (1.0 / jnp.sum(e, axis=1, keepdims=True))).astype(bf16)
        p_ref[0, h] = p
        outs.append(dot(p, v))
    o_ref[...] = jnp.where(lane < 64, outs[0], outs[1]).astype(bf16)


def attend_forward(first, lines, segc, segr, qkv, after=()):
    pairs, rows = qkv.shape[1] // 384, segc.shape[0]
    return pl.pallas_call(
        forward_kernel,
        grid_spec=pltpu.PrefetchScalarGridSpec(
            num_scalar_prefetch=1,
            grid=(pairs, rows),
            in_specs=[
                pl.BlockSpec((1, 2, ROW_LEN), lambda g, r, first: (g + first[0], 0, 0)),
                pl.BlockSpec((1, ROW_LEN, 1), lambda g, r, first: (r, 0, 0)),
                pl.BlockSpec((1, 1, ROW_LEN), lambda g, r, first: (r, 0, 0)),
                pl.BlockSpec((ROW_LEN, 384), lambda g, r, first: (r, g)),
            ]
            + [pl.BlockSpec(memory_space=pl.ANY)] * len(after),
            out_specs=[
                pl.BlockSpec((ROW_LEN, 128), lambda g, r, first: (r, g)),
                pl.BlockSpec((1, 2, ROW_LEN, ROW_LEN), lambda g, r, first: (r, g, 0, 0)),
            ],
            scratch_shapes=[pltpu.VMEM((2, ROW_LEN, ROW_LEN), f32), pltpu.VMEM((rows, ROW_LEN, ROW_LEN), f32)],
        ),
        out_shape=[
            shape_of((rows * ROW_LEN, 128 * pairs), bf16),
            shape_of((rows, 2 * pairs, ROW_LEN, ROW_LEN), bf16),
        ],
        compiler_params=pltpu.CompilerParams(vmem_limit_bytes=60 * MIB),
        cost_estimate=pl.CostEstimate(flops=pairs * rows * 2 * 10**9, bytes_accessed=pairs * rows * 2 * MIB, transcendentals=0),
    )(first, lines, segc, segr, qkv, *after)


def backward_kernel(*refs):
    ins, outs, acc = (refs[0:4], refs[4:8]), (refs[-7:-4], refs[-4:-1]), refs[-1]
    for side in range(2):

        @pl.when(pl.program_id(0) == side)
        def _():
            backward_step(*ins[side], *outs[side], acc)


def backward_step(qkv_ref, do_ref, o_ref, p_ref, d_ref, line_ref, sums_ref, acc):
    r, last = pl.program_id(2), pl.num_programs(2) - 1
    q, k, v = qkv_ref[:, 0:128], qkv_ref[:, 128:256], qkv_ref[:, 256:384]
    lane = lax.broadcasted_iota(jnp.int32, (ROW_LEN, 128), 1)
    qt = (q.astype(f32) * 0.125).T.astype(bf16)
    do = do_ref[...].astype(f32)
    dot_t = do.T.astype(bf16)
    prod = do * o_ref[...].astype(f32)
    dqs, dks, dvs = [], [], []
    for h in range(2):
        mine = (lane < 64) if h == 0 else (lane >= 64)
        doh = jnp.where(mine, do, 0.0).astype(bf16)
        delta = jnp.sum(jnp.where(mine, prod, 0.0), axis=1, keepdims=True)
        p = p_ref[0, h]
        ds = p.astype(f32) * (dot(doh, v, NT) - delta)

        @pl.when(r == 0)
        def _():
            acc[h] = ds

        @pl.when(r > 0)
        def _():
            acc[h] += ds

        dsb = ds.astype(bf16)
        half = slice(64 * h, 64 * h + 64)
        dqs.append(dot(dsb, k))
        dks.append(dot(qt[half, :], dsb))
        dvs.append(dot(dot_t[half, :], p))
    dq = jnp.where(lane < 64, dqs[0], dqs[1]) * 0.125
    dk = jnp.concatenate(dks, axis=0).T
    dv = jnp.concatenate(dvs, axis=0).T
    d_ref[:, 0:128] = dq.astype(bf16)
    d_ref[:, 128:256] = dk.astype(bf16)
    d_ref[:, 256:384] = dv.astype(bf16)
    sums = jnp.concatenate([jnp.sum(dq, axis=0, keepdims=True), jnp.sum(dv, axis=0, keepdims=True)], axis=0)

    @pl.when(r == 0)
    def _():
        sums_ref[0] = sums

    @pl.when(r > 0)
    def _():
        sums_ref[0] += sums

    @pl.when(r == last)
    def _():
        for h in range(2):
            line_ref[0, h : h + 1, :] = diagonals(acc, h)


def attend_backward(first, second, after=()):
    rows, pairs = first[3].shape[0], first[0].shape[1] // 384
    ends = ((0, 0), (pairs - 1, rows - 1))

    def block(shape, at, side):
        def index(s, g, r):
            mine = s == side
            return at(jnp.where(mine, g, ends[1 - side][0]), jnp.where(mine, r, ends[1 - side][1]))

        return pl.BlockSpec(shape, index)

    both = lambda shape, at: [block(shape, at, side) for side in range(2)]
    by_row, by_pair = lambda g, r: (r, g), lambda g, r: (g, 0, 0)
    wide, half = both((ROW_LEN, 384), by_row), both((ROW_LEN, 128), by_row)
    probs = both((1, 2, ROW_LEN, ROW_LEN), lambda g, r: (r, g, 0, 0))
    lines, sums = both((1, 2, ROW_LEN), by_pair), both((1, 2, 128), by_pair)
    shapes = [
        shape_of((rows * ROW_LEN, 384 * pairs), bf16),
        shape_of((pairs, 2, ROW_LEN), f32),
        shape_of((pairs, 2, 128), f32),
    ]
    done = pl.pallas_call(
        backward_kernel,
        grid=(2, pairs, rows),
        in_specs=[spec for i in range(2) for spec in (wide[i], half[i], half[i], probs[i])]
        + [pl.BlockSpec(memory_space=pl.ANY)] * len(after),
        out_specs=[spec for i in range(2) for spec in (wide[i], lines[i], sums[i])],
        out_shape=shapes * 2,
        scratch_shapes=[pltpu.VMEM((2, ROW_LEN, ROW_LEN), f32)],
        compiler_params=pltpu.CompilerParams(vmem_limit_bytes=60 * MIB),
        cost_estimate=pl.CostEstimate(flops=pairs * rows * 4 * 10**9, bytes_accessed=pairs * rows * 4 * MIB, transcendentals=0),
    )(*first, *second, *after)
    return done[:3], done[3:]


def normalize(value, gain, shift):
    center = value - jnp.mean(value, axis=1, keepdims=True)
    inverse = lax.rsqrt(jnp.mean(center * center, axis=1, keepdims=True) + 1e-5)
    normed = center * inverse
    return normed, inverse, normed * gain + shift


def normalize_back(upstream, normed, inverse, gain):
    scaled = upstream * gain
    return inverse * (
        scaled
        - jnp.mean(scaled, axis=1, keepdims=True)
        - normed * jnp.mean(scaled * normed, axis=1, keepdims=True)
    )


def column_sum(value):
    return jnp.sum(value, axis=0, keepdims=True)


def middle_kernel(
    blocks, order_ref,
    om_ref, ot_ref, x_ref, c_ref, vec_ref, bu_ref, uma_ref, umb_ref, uta_ref, utb_ref, dm_ref, dt_ref,
    *refs,
):
    (
        out_ref, dh1_ref, a_ref, g_ref, dom_ref, dot_ref, dy1m_ref, dy1t_ref, dy2m_ref, dy2t_ref, dzm_ref, dzt_ref,
        vsum_ref, usum_ref, wo, wu, wd, slope, dy, sems,
    ) = refs[-20:]
    step = pl.program_id(0)
    width, hidden = wu.shape
    core = order_ref[2 * blocks]
    w_half, h_half = width // 2, hidden // 2

    def cols(size, side, first=0, count=None):
        return pl.ds(pl.multiple_of(side * size + first, 128), size if count is None else count)

    up_left = uma_ref.shape[2]
    up_right = h_half - up_left
    rows, deep = uma_ref.shape[1], dm_ref.shape[1]
    sides = ((core, uma_ref, umb_ref, dm_ref), (1 - core, uta_ref, utb_ref, dt_ref))

    def out_moves(k):
        j, at = order_ref[blocks + k], place(k, rows)
        return [(ub.at[j, :, up_right : up_right + w_half], wo.at[at, cols(w_half, s)]) for s, ua, ub, d in sides]

    def up_moves(k):
        i, j, at = order_ref[k], order_ref[blocks + k], place(k, rows)
        first = [(ua.at[i], wu.at[at, cols(h_half, s, 0, up_left)]) for s, ua, ub, d in sides]
        second = [(ub.at[j, :, 0:up_right], wu.at[at, cols(h_half, s, up_left, up_right)]) for s, ua, ub, d in sides]
        return first + second

    def down_moves(k):
        found = []
        for n in range(2):
            i, at = order_ref[(2 + n) * blocks + 1 + k], place(2 * k + n, deep)
            found += [(d.at[i], wd.at[at, cols(w_half, s)]) for s, ua, ub, d in sides]
        return found

    groups = ((out_moves, 0), (up_moves, 2), (down_moves, 6))

    @pl.when(step == 0)
    def _():
        for moves, first in groups:
            copies(moves, sems, blocks, first, wait=False)

    def ready(group):
        @pl.when(step == 0)
        def _():
            copies(groups[group][0], sems, blocks, groups[group][1], start=False)

    ready(0)
    rows_of = lambda side: cols(w_half, side)
    b_out, b_down, gain1, shift1, gain2, shift2 = [vec_ref[i : i + 1, :] for i in range(2, 8)]
    first = x_ref[...].astype(f32) + dot(om_ref[...], wo[rows_of(core), :]) + dot(ot_ref[...], wo[rows_of(1 - core), :]) + b_out
    n1, r1, a = normalize(first, gain1, shift1)
    ab = a.astype(bf16)
    a_ref[...] = ab
    second = a + b_down
    chunk = h_half // 2
    ready(1)
    for f in range(0, hidden, chunk):
        at = slice(f, f + chunk)
        z = dot(ab, wu[:, at]) + bu_ref[:, at]
        mass = 0.5 * (1.0 + lax.erf(z * (1.0 / math.sqrt(2.0))))
        slope[:, at] = mass + z * jnp.exp(-0.5 * z * z) * (1.0 / math.sqrt(2.0 * math.pi))
        active = (z * mass).astype(bf16)
        g_ref[:, at] = active
        if f == 0:
            ready(2)
        second = second + dot(active, wd[at, :])
    n2, r2, out = normalize(second, gain2, shift2)
    out_ref[...] = out.astype(bf16)
    c = c_ref[...].astype(f32)
    dh2 = normalize_back(c, n2, r2, gain2)
    dy2 = dh2.astype(bf16)
    dy[...] = dy2
    dy2m_ref[...] = dy[:, cols(w_half, core)]
    dy2t_ref[...] = dy[:, cols(w_half, 1 - core)]
    da = dh2
    parts = []
    for side, dz_ref in ((core, dzm_ref), (1 - core, dzt_ref)):
        for f in range(0, h_half, chunk):
            at = cols(h_half, side, f, chunk)
            dz = dot(dy2, wd[at, :], NT) * slope[:, at]
            parts.append((at, column_sum(dz)))
            dzb = dz.astype(bf16)
            dz_ref[:, f : f + chunk] = dzb
            da = da + dot(dzb, wu[:, at], NT)
    dh1 = normalize_back(da, n1, r1, gain1)
    dh1_ref[...] = dh1
    dy1 = dh1.astype(bf16)
    dy[...] = dy1
    dy1m_ref[...] = dy[:, cols(w_half, core)]
    dy1t_ref[...] = dy[:, cols(w_half, 1 - core)]
    dom_ref[...] = dot(dy1, wo[rows_of(core), :], NT).astype(bf16)
    dot_ref[...] = dot(dy1, wo[rows_of(1 - core), :], NT).astype(bf16)
    sums = [column_sum(t) for t in (dh1, dh2, da * n1, da, c * n2, c)]
    vsum = jnp.concatenate(sums + [jnp.zeros((2, c.shape[1]), f32)], axis=0)

    @pl.when(step == 0)
    def _():
        vsum_ref[...] = vsum
        for at, part in parts:
            usum_ref[:, at] = part

    @pl.when(step > 0)
    def _():
        vsum_ref[...] += vsum
        for at, part in parts:
            usum_ref[:, at] += part


def middle(order, om, ot, x, c, vec, bu, up, down, after=(), block=256):
    tokens, width = x.shape
    hidden = bu.shape[1]
    blocks = up[0].shape[0]
    by_token = lambda n: pl.BlockSpec((block, n), lambda i, order: (i, 0))
    fixed = lambda s: pl.BlockSpec(s, lambda i, order: (0, 0))
    half, h_half = width // 2, hidden // 2
    outs = [(width, bf16), (width, f32), (width, bf16), (hidden, bf16)] + [(half, bf16)] * 6 + [(h_half, bf16)] * 2
    return pl.pallas_call(
        partial(middle_kernel, blocks),
        grid_spec=pltpu.PrefetchScalarGridSpec(
            num_scalar_prefetch=1,
            grid=(tokens // block,),
            in_specs=[by_token(half)] * 2
            + [by_token(width)] * 2
            + [fixed(vec.shape), fixed(bu.shape)]
            + [pl.BlockSpec(memory_space=pl.ANY)] * (6 + len(after)),
            out_specs=[by_token(n) for n, _ in outs] + [fixed((8, width)), fixed((1, hidden))],
            scratch_shapes=[
                pltpu.VMEM((width, width), bf16),
                pltpu.VMEM((width, hidden), bf16),
                pltpu.VMEM((hidden, width), bf16),
                pltpu.VMEM((block, hidden), f32),
                pltpu.VMEM((block, width), bf16),
                pltpu.SemaphoreType.DMA((10, blocks)),
            ],
        ),
        out_shape=[shape_of((tokens, n), t) for n, t in outs] + [shape_of((8, width), f32), shape_of((1, hidden), f32)],
        compiler_params=pltpu.CompilerParams(vmem_limit_bytes=50 * MIB),
        cost_estimate=pl.CostEstimate(flops=4 * 10**10, bytes_accessed=40 * MIB, transcendentals=0),
    )(order, om, ot, x, c, vec, bu, *up, *down, *after)


def copies(moves, sems, count, first=0, start=True, wait=True):
    def each(k, act):
        for i, (source, target) in enumerate(moves(k)):
            act(pltpu.make_async_copy(source, target, sems.at[first + i, k]))

    if start:
        lax.fori_loop(0, count, lambda k, c: (each(k, lambda copy: copy.start()), c)[1], 0)
    if wait:
        lax.fori_loop(0, count, lambda k, c: (each(k, lambda copy: copy.wait()), c)[1], 0)


def place(k, rows):
    return pl.ds(pl.multiple_of(k * rows, rows), rows)


def project_kernel(blocks, order_ref, x_ref, bias_ref, w_ref, *refs):
    out_ref, weight, sems = refs[-3:]
    rows, left = w_ref.shape[1:]
    right = weight.shape[1] - left

    @pl.when(pl.program_id(0) == 0)
    def _():
        def moves(k):
            at = place(k, rows)
            return [
                (w_ref.at[order_ref[k]], weight.at[at, 0:left]),
                (w_ref.at[blocks + order_ref[blocks + k], :, 0:right], weight.at[at, left : left + right]),
            ]

        copies(moves, sems, blocks)

    out_ref[...] = (dot(x_ref[...], weight[...]) + bias_ref[...]).astype(bf16)


def project(order, flip, x, bias, gathered, after=(), block=512):
    tokens, width = x.shape
    blocks, outs = gathered.shape[0] // 2, bias.shape[1] // 2
    half = lambda i, order: (0, 1 - order[2 * blocks] if flip else order[2 * blocks])
    return pl.pallas_call(
        partial(project_kernel, blocks),
        grid_spec=pltpu.PrefetchScalarGridSpec(
            num_scalar_prefetch=1,
            grid=(tokens // block,),
            in_specs=[
                pl.BlockSpec((block, width), lambda i, order: (i, 0)),
                pl.BlockSpec((1, outs), half),
            ]
            + [pl.BlockSpec(memory_space=pl.ANY)] * (1 + len(after)),
            out_specs=pl.BlockSpec((block, outs), lambda i, order: (i, 0)),
            scratch_shapes=[pltpu.VMEM((width, outs), bf16), pltpu.SemaphoreType.DMA((2, blocks))],
        ),
        out_shape=shape_of((tokens, outs), bf16),
        compiler_params=pltpu.CompilerParams(vmem_limit_bytes=60 * MIB),
        cost_estimate=pl.CostEstimate(flops=2 * tokens * width * outs, bytes_accessed=8 * MIB, transcendentals=0),
    )(order, x, bias, gathered, *after)


def token_kernel(blocks, order_ref, base_ref, dm_ref, dt_ref, wm_ref, wt_ref, *refs):
    out_ref, mine, theirs, sems = refs[-4:]
    rows, left = wm_ref.shape[1:]
    right = mine.shape[1] - left

    @pl.when(pl.program_id(0) == 0)
    def _():
        def moves(k):
            at, i, j = place(k, rows), order_ref[k], blocks + order_ref[blocks + k]
            return [
                (wm_ref.at[i], mine.at[at, 0:left]),
                (wm_ref.at[j, :, 0:right], mine.at[at, left : left + right]),
                (wt_ref.at[i], theirs.at[at, 0:left]),
                (wt_ref.at[j, :, 0:right], theirs.at[at, left : left + right]),
            ]

        copies(moves, sems, blocks)

    total = base_ref[...] + dot(dm_ref[...], mine[...], NT) + dot(dt_ref[...], theirs[...], NT)
    out_ref[...] = total.astype(bf16)


def token_gradient(order, base, dm, dt, gathered, after=(), block=256):
    tokens, width = base.shape
    blocks, outs = gathered[0].shape[0] // 2, dm.shape[1]
    by_token = lambda n: pl.BlockSpec((block, n), lambda i, order: (i, 0))
    return pl.pallas_call(
        partial(token_kernel, blocks),
        grid_spec=pltpu.PrefetchScalarGridSpec(
            num_scalar_prefetch=1,
            grid=(tokens // block,),
            in_specs=[by_token(width), by_token(outs), by_token(outs)]
            + [pl.BlockSpec(memory_space=pl.ANY)] * (2 + len(after)),
            out_specs=by_token(width),
            scratch_shapes=[pltpu.VMEM((width, outs), bf16)] * 2 + [pltpu.SemaphoreType.DMA((4, blocks))],
        ),
        out_shape=shape_of((tokens, width), bf16),
        compiler_params=pltpu.CompilerParams(vmem_limit_bytes=24 * MIB),
        cost_estimate=pl.CostEstimate(flops=4 * tokens * width * outs, bytes_accessed=14 * MIB, transcendentals=0),
    )(order, base, dm, dt, *gathered, *after)


TABLE_AT, UP_AT = 8, 32


def spread_kernel(devices, order_ref, b_ref, line_ref, vec_ref, up_ref, bias_ref, full, tab):
    blocks, rows = b_ref.shape[0:2]
    width, heads = vec_ref.shape[1], 2 * line_ref.shape[0]
    for k in range(blocks):
        full[rows * k : rows * k + rows, :] = b_ref[order_ref[blocks + k]].astype(f32)
    each, per, ups = width // devices, tab.shape[0] // devices, up_ref.shape[1] // devices
    vec_ref[...] = full[...].T[0:8, :]
    for d in range(devices):
        tab[per * d : per * d + per, :] = full[each * d : each * d + per, :]
        up_ref[:, ups * d : ups * d + ups] = full[each * d : each * d + 1, UP_AT : UP_AT + ups]
    table = tab[...].T[TABLE_AT : TABLE_AT + heads, :]
    buckets = table.shape[1]
    half, rest = buckets // 2, (ROW_LEN - buckets) // 2
    ends = [jnp.broadcast_to(table[:, i : i + 1], (heads, rest)) for i in (buckets - 1, 0)]
    lines = jnp.concatenate([table[:, half:], *ends, table[:, :half]], axis=1)
    for g in range(heads // 2):
        line_ref[g] = lines[2 * g : 2 * g + 2, :]
    for g in range(heads // 2):
        bias_ref[:, 384 * g : 384 * g + 128] = vec_ref[0:1, 128 * g : 128 * g + 128]
        bias_ref[:, 384 * g + 128 : 384 * g + 256] = jnp.zeros((1, 128), f32)
        bias_ref[:, 384 * g + 256 : 384 * g + 384] = vec_ref[1:2, 128 * g : 128 * g + 128]


def spread_small(order, b, devices, width, heads, buckets, hidden):
    blocks, rows = b.shape[0] // 2, b.shape[1]
    last = b.shape[2] // 128 - 1
    fixed = lambda s: pl.BlockSpec(s, lambda i, order: (0,) * len(s))
    shapes = [(heads // 2, 2, ROW_LEN), (8, width), (1, hidden), (1, 3 * width)]
    return pl.pallas_call(
        partial(spread_kernel, devices),
        grid_spec=pltpu.PrefetchScalarGridSpec(
            num_scalar_prefetch=1,
            grid=(1,),
            in_specs=[pl.BlockSpec((blocks, rows, 128), lambda i, order: (1, 0, last))],
            out_specs=[fixed(s) for s in shapes],
            scratch_shapes=[pltpu.VMEM((width, 128), f32), pltpu.VMEM((buckets, 128), f32)],
        ),
        out_shape=[shape_of(s, f32) for s in shapes],
        compiler_params=pltpu.CompilerParams(vmem_limit_bytes=8 * MIB),
        cost_estimate=pl.CostEstimate(flops=10**6, bytes_accessed=MIB, transcendentals=0),
    )(order, b)


def collect_kernel(devices, buckets, core_ref, vsum_ref, usum_ref, ms_ref, ts_ref, ml_ref, tl_ref, out_ref, tall, sums, lines):
    core = core_ref[0]
    width = vsum_ref.shape[1]
    pairs = ms_ref.shape[0]
    sums[core], sums[1 - core] = ms_ref[...], ts_ref[...]
    for g in range(pairs):
        lines[core, 2 * g : 2 * g + 2, :] = ml_ref[g]
        lines[1 - core, 2 * g : 2 * g + 2, :] = tl_ref[g]
    tall[...] = jnp.zeros_like(tall)
    tall[2:8, :] = vsum_ref[0:6, :]
    for side in range(2):
        for g in range(pairs):
            at = 128 * (side * pairs + g)
            tall[0:2, at : at + 128] = sums[side, g]
    out_ref[...] = tall[...].T
    line = jnp.concatenate([lines[0], lines[1]], axis=0)
    heads = line.shape[0]
    half, middle = buckets // 2, ROW_LEN // 2
    far = jnp.sum(line[:, half:middle], axis=1, keepdims=True)
    near = jnp.sum(line[:, middle : ROW_LEN - half], axis=1, keepdims=True)
    place = lax.broadcasted_iota(jnp.int32, (heads, half), 1)
    upper = line[:, :half] + jnp.where(place == half - 1, far, 0.0)
    lower = line[:, ROW_LEN - half :] + jnp.where(place == 0, near, 0.0)
    table = jnp.concatenate([lower, upper], axis=1)
    below = jnp.zeros((128 - TABLE_AT - heads, buckets), f32)
    table = jnp.concatenate([jnp.zeros((TABLE_AT, buckets), f32), table, below], axis=0).T
    each, per, ups = width // devices, buckets // devices, usum_ref.shape[1] // devices
    for d in range(devices):
        out_ref[each * d : each * d + per, :] += table[per * d : per * d + per, :]
        out_ref[each * d : each * d + 1, UP_AT : UP_AT + ups] = usum_ref[:, ups * d : ups * d + ups]


def collect_small(core, devices, buckets, vsum, usum, mine, theirs):
    width = vsum.shape[1]
    pairs = mine[1].shape[0]
    args = [vsum, usum, mine[1], theirs[1], mine[0], theirs[0]]
    whole = lambda t: pl.BlockSpec(t.shape, lambda i, core: (0,) * t.ndim)
    return pl.pallas_call(
        partial(collect_kernel, devices, buckets),
        grid_spec=pltpu.PrefetchScalarGridSpec(
            num_scalar_prefetch=1,
            grid=(1,),
            in_specs=[whole(t) for t in args],
            out_specs=pl.BlockSpec((width, 128), lambda i, core: (0, 0)),
            scratch_shapes=[
                pltpu.VMEM((128, width), f32),
                pltpu.VMEM((2, pairs, 2, 128), f32),
                pltpu.VMEM((2, 2 * pairs, ROW_LEN), f32),
            ],
        ),
        out_shape=shape_of((width, 128), f32),
        compiler_params=pltpu.CompilerParams(vmem_limit_bytes=8 * MIB),
        cost_estimate=pl.CostEstimate(flops=10**6, bytes_accessed=MIB, transcendentals=0),
    )(core, *args)


def pack_kernel(core_ref, *refs):
    vectors, (table_ref, up_ref, q_ref, k_ref, v_ref, wo_ref, wu_ref, wd_ref) = refs[:8], refs[8:16]
    outs, (tall, small) = refs[16:22], refs[22:]
    rows = q_ref.shape[0]
    for i, ref in enumerate(vectors):
        tall[i : i + 1, 0:rows] = ref[...]
    small[...] = tall[...].T[0:rows, :]
    lane = lax.broadcasted_iota(jnp.int32, small.shape, 1)
    small[...] = jnp.where(lane < 8, small[...], 0.0)
    per, heads = table_ref.shape
    small[0:per, TABLE_AT : TABLE_AT + heads] = table_ref[...]
    small[0:1, UP_AT : UP_AT + up_ref.shape[1]] = up_ref[...]
    extra = small[...].astype(bf16)
    low = lambda ref, first, last: ref[:, first:last].astype(bf16)
    h, f = wo_ref.shape[1] // 2, wu_ref.shape[1] // 2

    def write(side, square, up, down):
        for g in range(h // 128):
            at = side * h + 128 * g
            for i, ref in enumerate((q_ref, k_ref, v_ref)):
                square[:, 384 * g + 128 * i : 384 * g + 128 * i + 128] = low(ref, at, at + 128)
        square[:, 3 * h : 3 * h + 128] = extra
        up[:, 0:f] = low(wu_ref, side * f, side * f + f)
        up[:, f : f + h] = low(wo_ref, side * h, side * h + h)
        down[...] = low(wd_ref, side * h, side * h + h)

    @pl.when(core_ref[0] == 0)
    def _():
        write(0, *outs[0:3])
        write(1, *outs[3:6])

    @pl.when(core_ref[0] == 1)
    def _():
        write(1, *outs[0:3])
        write(0, *outs[3:6])


def pack(core, vectors, table, up, matrices):
    rows, width = matrices[0].shape
    args = [t.reshape(1, -1) for t in vectors] + [table, up.reshape(1, -1), *matrices]
    whole = lambda s: pl.BlockSpec(s, lambda i, core: (0, 0))
    shapes = [
        (rows, 3 * width // 2 + 128),
        (rows, (matrices[4].shape[1] + width) // 2),
        (matrices[5].shape[0], width // 2),
    ] * 2
    return pl.pallas_call(
        pack_kernel,
        grid_spec=pltpu.PrefetchScalarGridSpec(
            num_scalar_prefetch=1,
            grid=(1,),
            in_specs=[whole(t.shape) for t in args],
            out_specs=[whole(s) for s in shapes],
            scratch_shapes=[pltpu.VMEM((128, 128), f32), pltpu.VMEM((rows, 128), f32)],
        ),
        out_shape=[shape_of(s, bf16) for s in shapes],
        compiler_params=pltpu.CompilerParams(vmem_limit_bytes=60 * MIB),
        cost_estimate=pl.CostEstimate(flops=10**6, bytes_accessed=2 * MIB, transcendentals=0),
    )(core, *args)


class Links:
    def __init__(self, mesh):
        wide, narrow = mesh.shape[WIDE], mesh.shape[NARROW]
        self.sizes = (wide // 2, 2, narrow // 2, 2)
        w, n = lax.axis_index(WIDE), lax.axis_index(NARROW)
        self.place = (w // 2, w % 2, n // 2, n % 2)
        self.core = self.place[CORE]
        self.chips = wide * narrow // 2

    def number(self, at):
        return ((at[Z] * self.sizes[X] + at[X]) * self.sizes[Y] + at[Y]) * 2 + at[CORE]

    def fetch(self, value, axis, step):
        pairs = []
        for z in range(self.sizes[Z]):
            for x in range(self.sizes[X]):
                for y in range(self.sizes[Y]):
                    for c in range(2):
                        here = (z, x, y, c)
                        there = list(here)
                        there[axis] = (there[axis] + step) % self.sizes[axis]
                        pairs.append((self.number(there), self.number(here)))
        return lax.ppermute(value, AXES, pairs)

    def others(self, value, axis):
        return [self.fetch(value, axis, k) for k in range(1, self.sizes[axis])]

    def swapped(self, kept, sent):
        even = self.core == 0
        got = self.fetch(sent, CORE, 1)
        return jnp.where(even, kept, got), jnp.where(even, got, kept)

    def order(self):
        chip = jnp.arange(self.chips, dtype=jnp.int32)
        sz, sx, sy = self.sizes[:3]
        kz = (chip // (sx * sy) - self.place[Z]) % sz
        kx = (chip // sy - self.place[X]) % sx
        ky = (chip - self.place[Y]) % sy
        plane = 2 * ((kz * sy + ky) * sx + kx)
        return jnp.concatenate(
            [
                (ky * sx + kx) * sz + kz,
                (kx * sy + ky) * sz + kz,
                self.core.reshape(1),
                plane,
                plane + 1,
            ]
        ).astype(jnp.int32)

    def finish(self, total):
        rows = total.shape[0] // 2
        even = self.core == 0
        own = jnp.where(even, total[:rows], total[rows:])
        got = self.fetch(jnp.where(even, total[rows:], total[:rows]), CORE, 1)
        return jnp.where(even, own, got), jnp.where(even, got, own)


def ring(me, k, size):
    at = me + k
    return jnp.where(at >= size, at - size, at)


def fold_1_kernel(halves, sizes, count, place_ref, *refs):
    kept, got, outs = refs[:count], refs[count : 2 * count], refs[2 * count :]
    split = sizes[Y]
    a_outs, b_outs = outs[:split], outs[split:]

    def write(out, at, half, x, y):
        rows, column = out.shape[2], 0
        for piece, part, first, last in half:
            source = (0, x, y, part, slice(None), slice(first, last))
            value = kept[piece][source] + got[piece][source].astype(f32)
            for row in range(0, value.shape[0], rows):
                some = value[row : row + rows, :].astype(out.dtype)
                out[0, at, :, column : column + last - first] = some
                column += last - first

    for k, out in enumerate(a_outs):
        y = ring(place_ref[Y], k, sizes[Y])
        for x in range(sizes[X]):
            write(out, x, halves[0], x, y)
    for k, out in enumerate(b_outs):
        x = ring(place_ref[X], k, sizes[X])
        for y in range(sizes[Y]):
            write(out, y, halves[1], x, y)


def fold_2_kernel(sizes, place_ref, *refs):
    sy, sx = sizes[Y], sizes[X]
    a_in, b_in, outs = refs[:sy], refs[sy : sy + sx], refs[sy + sx :]
    a_outs, b_outs = outs[:sx], outs[sx:]

    def value(ins, at):
        total = ins[0][0, at]
        for piece in ins[1:]:
            total = total + piece[0, at].astype(f32)
        return total

    for k, out in enumerate(a_outs):
        out[0] = value(a_in, ring(place_ref[X], k, sx)).astype(out.dtype)
    for k, out in enumerate(b_outs):
        out[0] = value(b_in, ring(place_ref[Y], k, sy)).astype(out.dtype)


def fold_3_kernel(sizes, place_ref, *refs):
    sy, sx = sizes[Y], sizes[X]
    a_in, b_in, outs = refs[:sx], refs[sx : sx + sy], refs[sx + sy :]
    rows, columns = a_in[0].shape[1:]
    for k, out in enumerate(outs):
        z = ring(place_ref[Z], k, sizes[Z])
        for n, ins in enumerate((a_in, b_in)):
            total = ins[0][z]
            for piece in ins[1:]:
                total = total + piece[z].astype(f32)
            first = n * columns
            out[0, :, first : first + total.shape[1]] = total.astype(out.dtype)


def fold_call(kernel, place, ins, outs, steps):
    block = lambda s: pl.BlockSpec((s[0] // steps,) + tuple(s[1:]), lambda i, place: (i,) + (0,) * (len(s) - 1))
    return pl.pallas_call(
        kernel,
        grid_spec=pltpu.PrefetchScalarGridSpec(
            num_scalar_prefetch=1,
            grid=(steps,),
            in_specs=[block(t.shape) for t in ins],
            out_specs=[block(s) for s, _ in outs],
        ),
        out_shape=[shape_of(s, t) for s, t in outs],
        compiler_params=pltpu.CompilerParams(vmem_limit_bytes=24 * MIB),
        cost_estimate=pl.CostEstimate(flops=10**6, bytes_accessed=8 * MIB, transcendentals=0),
    )(place, *ins)


class Fold:
    def __init__(self, links, halves):
        self.links, self.halves = links, halves
        self.place = jnp.stack(links.place).astype(jnp.int32)

    def to_others(self, values, axis):
        size = self.links.sizes[axis]
        return [self.links.fetch(v, axis, size - k) for k, v in enumerate(values) if k]

    def first(self, kept, got):
        sizes = self.links.sizes
        sz, sx, sy = sizes[:3]
        rows = kept[0].shape[4]
        wide = [sum((e[3] - e[2]) * kept[e[0]].shape[4] // rows for e in half) for half in self.halves]
        kinds = lambda shape, n: [(shape, f32)] + [(shape, bf16)] * (n - 1)
        outs = kinds((sz, sx, rows, wide[0]), sy) + kinds((sz, sy, rows, wide[1]), sx)
        done = fold_call(partial(fold_1_kernel, self.halves, sizes, len(kept)), self.place, [*kept, *got], outs, sz)
        a, b = done[:sy], done[sy:]
        return [a[0], b[0]], self.to_others(a, Y), self.to_others(b, X)

    def second(self, own, got_y, got_x):
        sizes = self.links.sizes
        sz, sx, sy = sizes[:3]
        kinds = lambda t, n: [((sz,) + t.shape[2:], f32)] + [((sz,) + t.shape[2:], bf16)] * (n - 1)
        outs = kinds(own[0], sx) + kinds(own[1], sy)
        done = fold_call(partial(fold_2_kernel, sizes), self.place, [own[0], *got_y, own[1], *got_x], outs, sz)
        a, b = done[:sx], done[sx:]
        return [a[0], b[0]], self.to_others(a, X), self.to_others(b, Y)

    def third(self, own, got_x, got_y):
        sizes = self.links.sizes
        rows, ca = own[0].shape[1:]
        shape = (1, rows, ca + own[1].shape[2])
        outs = [(shape, f32)] + [(shape, bf16)] * (sizes[Z] - 1)
        ins = [own[0], *got_x, own[1], *got_y]
        done = fold_call(partial(fold_3_kernel, sizes), self.place, ins, outs, 1)
        return done[0], self.to_others(done, Z)

    def last(self, own, got):
        for piece in got:
            own = own + piece.astype(f32)
        return own[0]


def segments(lengths):
    place = jnp.arange(ROW_LEN, dtype=jnp.int32)
    ending = jnp.cumsum(lengths, axis=1)
    return jnp.sum((place[None, :, None] >= ending[:, None, :]).astype(jnp.int32), axis=2)


def interleaved(q, k, v):
    rows = q.shape[0]
    return jnp.stack([t.reshape(rows, -1, 128) for t in (q, k, v)], axis=2).reshape(rows, -1)


def separate(qkv):
    rows = qkv.shape[0]
    parts = qkv.reshape(rows, -1, 3, 128)
    return [parts[:, :, i].reshape(rows, -1) for i in range(3)]


def per_device(
    mesh, tokens, cotangent, pair_lengths, w_query, w_key, w_value, w_output, w_up, w_down, b_query, b_value,
    b_output, b_up, b_down, first_gain, first_shift, second_gain, second_shift, bucket_bias,
):
    links = Links(mesh)
    devices = 2 * links.chips
    rows, width = w_query.shape
    hidden = w_up.shape[1]
    heads = bucket_bias.shape[1]
    buckets = bucket_bias.shape[0] * devices
    w_half, h_half = width // 2, hidden // 2
    low = lambda t: t.astype(bf16)
    barrier = lax.optimization_barrier
    core = links.core
    even = core == 0
    order = links.order()
    blocks = lambda a, b: [a, b]
    deep = square_blocks = lambda t: t
    if (2 * rows) % 16 or w_down.shape[0] % 16:
        found, order = order, jnp.concatenate([jnp.zeros((2,), jnp.int32), core.reshape(1), jnp.arange(2, dtype=jnp.int32)])
        n = links.chips
        sort = lambda t, first: jnp.take(t, found[first : first + n], axis=0)

        def blocks(a, b):
            return [t.reshape(1, -1, t.shape[2]) for t in (sort(a, 0), sort(b, n))]

        def square_blocks(t):
            return jnp.stack([sort(t[:n], 0), sort(t[n:], n)]).reshape(2, -1, t.shape[2])

        def deep(t):
            both = jnp.stack([sort(t, 2 * n + 1), sort(t, 3 * n + 1)], axis=1)
            return both.reshape(2, -1, t.shape[2])

    half = 3 * w_half
    cut = (half + 128) // 2
    up_cut = (h_half + w_half + 128) // 256 * 128
    packed = pack(
        core.reshape(1),
        [b_query, b_value, b_output, b_down, first_gain, first_shift, second_gain, second_shift],
        bucket_bias,
        b_up,
        [w_query, w_key, w_value, w_output, w_up, w_down],
    )
    swapped = lambda i: jnp.concatenate(links.swapped(packed[i], packed[i + 3]), axis=0)
    pair = swapped(0)
    pair_z = links.others(pair, Z)
    up_pair = swapped(1)
    down_pair = jnp.stack(links.swapped(packed[2], packed[5]))
    down_x = links.others(down_pair, X)

    def together(*groups):
        sizes = [len(g) for g in groups]
        flat = barrier(tuple(t for g in groups for t in g))
        out = []
        for size in sizes:
            out.append(list(flat[:size]))
            flat = flat[size:]
        return out

    def spans(*groups):
        leaves, tree = jax.tree.flatten(tuple(groups))
        return jax.tree.unflatten(tree, barrier(tuple(leaves)))

    def chips(value, got):
        value = jnp.stack([value] + got)
        return value.reshape((-1,) + value.shape[-2:])

    def plane_1(value, cut):
        return [value[:, :, :cut], value[:, :, cut:]], links.others(value[:, :, :cut], X), links.others(value[:, :, cut:], Y)

    def plane_2(ab, got_x, got_y):
        ab = [chips(ab[0], got_x), chips(ab[1], got_y)]
        return ab, links.others(ab[0], Y), links.others(ab[1], X)

    def plane_3(ab, got_y, got_x):
        return chips(ab[0], got_y), chips(ab[1], got_x)

    pair_z, (pair, up_pair), down_x = together(pair_z, (pair, up_pair), down_x)
    stage = plane_1(jnp.stack([pair] + pair_z), cut)
    down_pair = jnp.stack([down_pair] + down_x)
    down_y = links.others(down_pair, Y)
    got_x, got_y, (up_pair,) = together(*stage[1:], (up_pair,))
    stage = plane_2(stage[0], got_x, got_y)
    up_z = links.others(up_pair, Z)
    got_y, got_x = together(*stage[1:])
    mine = jnp.concatenate(plane_3(stage[0], got_y, got_x), axis=0)

    theirs = links.fetch(mine, CORE, 1)
    mine, theirs = square_blocks(mine), square_blocks(theirs)
    lines, vectors, up_bias, bias = spread_small(order, mine, devices, width, heads, buckets, hidden)
    segment = segments(pair_lengths)
    segc, segr = segment[:, :, None], segment[:, None, :]
    pairs = heads // 4
    first_m, first_t = (core * pairs).reshape(1), ((1 - core) * pairs).reshape(1)
    qkv_m = project(order, False, tokens, bias, mine)
    up_z, (qkv_m, bias_t, theirs), down_y = together(up_z, (qkv_m, bias, theirs), down_y)
    down_own = jnp.stack([down_pair] + down_y)
    up_stage = plane_1(jnp.stack([up_pair] + up_z), up_cut)
    down_z = links.others(down_own, Z)
    qkv_t = project(order, True, tokens, bias_t, theirs)
    o_m, p_m = attend_forward(first_m, lines, segc, segr, qkv_m)
    (o_m, qkv_t), got_x, got_y = together((o_m, qkv_t), up_stage[1], up_stage[2])

    up_stage = plane_2(up_stage[0], got_x, got_y)
    o_t, p_t = attend_forward(first_t, lines, segc, segr, qkv_t)
    (o_m, o_t), got_y, got_x = together((o_m, o_t), *up_stage[1:])
    up_a, up_b = plane_3(up_stage[0], got_y, got_x)
    up_theirs = (links.fetch(up_a, CORE, 1), links.fetch(up_b, CORE, 1))
    up_a, up_b, *down_z = barrier((up_a, up_b, *down_z))
    down_mine = jnp.stack([down_own] + down_z)
    down_mine = down_mine.reshape((-1,) + down_mine.shape[-2:])
    down_theirs = links.fetch(down_mine, CORE, 1)

    result, dh1, settled, active, do_m, do_t, dy1_m, dy1_t, dy2_m, dy2_t, dz_m, dz_t, vsum, usum = middle(
        order,
        o_m,
        o_t,
        tokens,
        cotangent,
        vectors,
        up_bias,
        blocks(up_a, up_b) + blocks(*up_theirs),
        [deep(down_mine), deep(down_theirs)],
    )

    def pieces(t, parts=1):
        return t.reshape(links.sizes[:3] + (parts, -1, t.shape[1]))

    exchange = lambda *values: [links.fetch(low(t), CORE, 1) for t in values]
    o_both = jnp.where(even, jnp.concatenate([o_m, o_t], axis=1), jnp.concatenate([o_t, o_m], axis=1))
    up_parts = lambda dz, dy1: [pieces(dot(settled, dz, TN)), pieces(dot(o_both, dy1, TN))]
    wide_fold = Fold(
        links,
        [
            [(0, 0, 0, up_cut), (2, 0, 0, w_half)],
            [(0, 0, up_cut, h_half), (1, 0, 0, w_half), (2, 1, 0, w_half)],
        ],
    )
    square_fold = Fold(links, [[(0, 0, 0, cut)], [(0, 0, cut, half), (1, 0, 0, 128)]])

    got = exchange(*up_parts(dz_t, dy1_t))
    kept = up_parts(dz_m, dy1_m)
    got, kept, (dy2_t, dy2_m) = spans(got, kept, (dy2_t, dy2_m))
    got += exchange(pieces(dot(active, dy2_t, TN), 2))
    kept += [pieces(dot(active, dy2_m, TN), 2)]
    got, kept, (do_t, do_m) = spans(got, kept, (do_t, do_m))

    wide = wide_fold.first(kept, got)
    grads_t, grads_m = attend_backward((qkv_t, do_t, o_t, p_t), (qkv_m, do_m, o_m, p_m))
    wide, grads_t, grads_m = spans(wide, grads_t, grads_m)

    wide = wide_fold.second(*wide)
    square_got = exchange(pieces(dot(tokens, grads_t[0], TN)))
    g_small = pieces(collect_small(core.reshape(1), devices, buckets, vsum, usum, grads_m[1:], grads_t[1:]))
    square_got += exchange(g_small)
    square_kept = [pieces(dot(tokens, grads_m[0], TN)), g_small]
    wide, square_kept, square_got, (d_m, d_t) = spans(wide, square_kept, square_got, (grads_m[0], grads_t[0]))

    square = square_fold.first(square_kept, square_got)
    wide_own, wide_got = wide_fold.third(*wide)
    grad_tokens = token_gradient(order, dh1, d_m, d_t, [mine, theirs])
    square, grad_tokens = spans(square, grad_tokens)

    square = square_fold.second(*square)
    square = spans(square)[0]
    square_own, square_z = square_fold.third(*square)
    wide_got, square_own = spans(wide_got, square_own)
    wide_total = wide_fold.last(wide_own, wide_got)
    square_total = square_fold.last(square_own, square_z)
    wide_a = up_cut + 2 * w_half
    up_total = jnp.concatenate([wide_total[:, :up_cut], wide_total[:, wide_a : wide_a + h_half + w_half - up_cut]], axis=1)
    groups = w_down.shape[0] // (2 * rows)
    down_total = jnp.stack(
        [
            jnp.concatenate([wide_total[:, first + w_half * i : first + w_half * (i + 1)] for i in range(groups)], axis=0)
            for first in (up_cut, wide_total.shape[1] - groups * w_half)
        ]
    ).reshape(-1, w_half)

    down_l, down_r = links.finish(down_total)
    up_l, up_r = links.finish(up_total)
    own_small = jnp.where(even, square_total[:rows, half:], square_total[rows:, half:])
    left, right = links.finish(square_total[:, :half])
    out_query, out_key, out_value = separate(jnp.concatenate([left, right], axis=1))
    flat = [own_small[:, i] for i in range(8)]
    whole = lambda start, stop: jnp.concatenate([up_l[:, start:stop], up_r[:, start:stop]], axis=1)
    table_rows = bucket_bias.shape[0]
    return (
        result,
        grad_tokens,
        out_query,
        out_key,
        out_value,
        whole(h_half, h_half + w_half),
        whole(0, h_half),
        jnp.concatenate([down_l, down_r], axis=1),
        flat[0],
        flat[1],
        flat[2],
        own_small[0, UP_AT : UP_AT + b_up.shape[0]],
        flat[3],
        flat[4],
        flat[5],
        flat[6],
        flat[7],
        own_small[:table_rows, TABLE_AT : TABLE_AT + heads],
    )


def solution(mesh):
    split, line = P(AXES, None), P(AXES)
    return jax.shard_map(
        partial(per_device, mesh),
        mesh=mesh,
        in_specs=(split,) * 9 + (line,) * 9 + (split,),
        out_specs=(split,) * 8 + (line,) * 9 + (split,),
        check_vma=False,
    )
```

```python
from functools import partial
import math

import jax
import jax.numpy as jnp
from jax import lax
from jax.experimental import pallas as pl
from jax.experimental.pallas import tpu as pltpu
from jax.sharding import PartitionSpec as P

WIDE, NARROW = "wide", "narrow"
AXES = (WIDE, NARROW)
Z, X, Y, CORE = range(4)
ROW_LEN = 512
MIB = 1 << 20
bf16, f32 = jnp.bfloat16, jnp.float32
NN = (((1,), (0,)), ((), ()))
NT = (((1,), (1,)), ((), ()))
TN = (((0,), (0,)), ((), ()))


def dot(left, right, dims=NN):
    return lax.dot_general(left, right, dims, preferred_element_type=f32)


def shape_of(shape, dtype):
    return jax.ShapeDtypeStruct(shape, dtype)


def toeplitz(line, ref, head):
    base = jnp.concatenate([pltpu.roll(line, s, 1) if s else line for s in range(8)], axis=0)
    for c in range(16):
        turned = pltpu.roll(base, 8 * c, 1) if c else base
        for b in range(ROW_LEN // 128):
            cut = ROW_LEN - 128 * b
            piece = jnp.concatenate([turned[:, cut:], turned[:, :cut]], axis=1) if b else turned
            first = 128 * b + 8 * c
            ref[head, first : first + 8, :] = piece


def diagonals(ref, head):
    total = None
    for c in range(16):
        turned = None
        for b in range(ROW_LEN // 128):
            first = 128 * b + 8 * c
            piece = ref[head, first : first + 8, :]
            if b:
                piece = jnp.concatenate([piece[:, 128 * b :], piece[:, : 128 * b]], axis=1)
            turned = piece if turned is None else turned + piece
        if c:
            turned = pltpu.roll(turned, ROW_LEN - 8 * c, 1)
        total = turned if total is None else total + turned
    out = total[0:1]
    for s in range(1, 8):
        out = out + pltpu.roll(total[s : s + 1], ROW_LEN - s, 1)
    return out


def forward_kernel(first_ref, line_ref, segc_ref, segr_ref, qkv_ref, *refs):
    o_ref, p_ref, bias, mask = refs[-4:]
    g, r = pl.program_id(0), pl.program_id(1)

    @pl.when(g == 0)
    def _():
        mask[r] = jnp.where(segc_ref[0] == segr_ref[0], 0.0, -1e30)

    @pl.when(r == 0)
    def _():
        for h in range(2):
            toeplitz(line_ref[0, h : h + 1, :], bias, h)

    q, k, v = qkv_ref[:, 0:128], qkv_ref[:, 128:256], qkv_ref[:, 256:384]
    lane = lax.broadcasted_iota(jnp.int32, (ROW_LEN, 128), 1)
    outs = []
    for h in range(2):
        mine = (lane < 64) if h == 0 else (lane >= 64)
        qh = jnp.where(mine, q.astype(f32) * 0.125, 0.0).astype(bf16)
        s = dot(qh, k, NT) + bias[h] + mask[r]
        e = jnp.exp(s - jnp.max(s, axis=1, keepdims=True))
        p = (e * (1.0 / jnp.sum(e, axis=1, keepdims=True))).astype(bf16)
        p_ref[0, h] = p
        outs.append(dot(p, v))
    o_ref[...] = jnp.where(lane < 64, outs[0], outs[1]).astype(bf16)


def attend_forward(first, lines, segc, segr, qkv, after=()):
    pairs, rows = qkv.shape[1] // 384, segc.shape[0]
    return pl.pallas_call(
        forward_kernel,
        grid_spec=pltpu.PrefetchScalarGridSpec(
            num_scalar_prefetch=1,
            grid=(pairs, rows),
            in_specs=[
                pl.BlockSpec((1, 2, ROW_LEN), lambda g, r, first: (g + first[0], 0, 0)),
                pl.BlockSpec((1, ROW_LEN, 1), lambda g, r, first: (r, 0, 0)),
                pl.BlockSpec((1, 1, ROW_LEN), lambda g, r, first: (r, 0, 0)),
                pl.BlockSpec((ROW_LEN, 384), lambda g, r, first: (r, g)),
            ]
            + [pl.BlockSpec(memory_space=pl.ANY)] * len(after),
            out_specs=[
                pl.BlockSpec((ROW_LEN, 128), lambda g, r, first: (r, g)),
                pl.BlockSpec((1, 2, ROW_LEN, ROW_LEN), lambda g, r, first: (r, g, 0, 0)),
            ],
            scratch_shapes=[pltpu.VMEM((2, ROW_LEN, ROW_LEN), f32), pltpu.VMEM((rows, ROW_LEN, ROW_LEN), f32)],
        ),
        out_shape=[
            shape_of((rows * ROW_LEN, 128 * pairs), bf16),
            shape_of((rows, 2 * pairs, ROW_LEN, ROW_LEN), bf16),
        ],
        compiler_params=pltpu.CompilerParams(vmem_limit_bytes=60 * MIB),
        cost_estimate=pl.CostEstimate(flops=pairs * rows * 2 * 10**9, bytes_accessed=pairs * rows * 2 * MIB, transcendentals=0),
    )(first, lines, segc, segr, qkv, *after)


def backward_kernel(*refs):
    ins, outs, acc = (refs[0:4], refs[4:8]), (refs[-7:-4], refs[-4:-1]), refs[-1]
    for side in range(2):

        @pl.when(pl.program_id(0) == side)
        def _():
            backward_step(*ins[side], *outs[side], acc)


def backward_step(qkv_ref, do_ref, o_ref, p_ref, d_ref, line_ref, sums_ref, acc):
    r, last = pl.program_id(2), pl.num_programs(2) - 1
    q, k, v = qkv_ref[:, 0:128], qkv_ref[:, 128:256], qkv_ref[:, 256:384]
    lane = lax.broadcasted_iota(jnp.int32, (ROW_LEN, 128), 1)
    qt = (q.astype(f32) * 0.125).T.astype(bf16)
    do = do_ref[...].astype(f32)
    dot_t = do.T.astype(bf16)
    prod = do * o_ref[...].astype(f32)
    dqs, dks, dvs = [], [], []
    for h in range(2):
        mine = (lane < 64) if h == 0 else (lane >= 64)
        doh = jnp.where(mine, do, 0.0).astype(bf16)
        delta = jnp.sum(jnp.where(mine, prod, 0.0), axis=1, keepdims=True)
        p = p_ref[0, h]
        ds = p.astype(f32) * (dot(doh, v, NT) - delta)

        @pl.when(r == 0)
        def _():
            acc[h] = ds

        @pl.when(r > 0)
        def _():
            acc[h] += ds

        dsb = ds.astype(bf16)
        half = slice(64 * h, 64 * h + 64)
        dqs.append(dot(dsb, k))
        dks.append(dot(qt[half, :], dsb))
        dvs.append(dot(dot_t[half, :], p))
    dq = jnp.where(lane < 64, dqs[0], dqs[1]) * 0.125
    dk = jnp.concatenate(dks, axis=0).T
    dv = jnp.concatenate(dvs, axis=0).T
    d_ref[:, 0:128] = dq.astype(bf16)
    d_ref[:, 128:256] = dk.astype(bf16)
    d_ref[:, 256:384] = dv.astype(bf16)
    sums = jnp.concatenate([jnp.sum(dq, axis=0, keepdims=True), jnp.sum(dv, axis=0, keepdims=True)], axis=0)

    @pl.when(r == 0)
    def _():
        sums_ref[0] = sums

    @pl.when(r > 0)
    def _():
        sums_ref[0] += sums

    @pl.when(r == last)
    def _():
        for h in range(2):
            line_ref[0, h : h + 1, :] = diagonals(acc, h)


def attend_backward(first, second, after=()):
    rows, pairs = first[3].shape[0], first[0].shape[1] // 384
    ends = ((0, 0), (pairs - 1, rows - 1))

    def block(shape, at, side):
        def index(s, g, r):
            mine = s == side
            return at(jnp.where(mine, g, ends[1 - side][0]), jnp.where(mine, r, ends[1 - side][1]))

        return pl.BlockSpec(shape, index)

    both = lambda shape, at: [block(shape, at, side) for side in range(2)]
    by_row, by_pair = lambda g, r: (r, g), lambda g, r: (g, 0, 0)
    wide, half = both((ROW_LEN, 384), by_row), both((ROW_LEN, 128), by_row)
    probs = both((1, 2, ROW_LEN, ROW_LEN), lambda g, r: (r, g, 0, 0))
    lines, sums = both((1, 2, ROW_LEN), by_pair), both((1, 2, 128), by_pair)
    shapes = [
        shape_of((rows * ROW_LEN, 384 * pairs), bf16),
        shape_of((pairs, 2, ROW_LEN), f32),
        shape_of((pairs, 2, 128), f32),
    ]
    done = pl.pallas_call(
        backward_kernel,
        grid=(2, pairs, rows),
        in_specs=[spec for i in range(2) for spec in (wide[i], half[i], half[i], probs[i])]
        + [pl.BlockSpec(memory_space=pl.ANY)] * len(after),
        out_specs=[spec for i in range(2) for spec in (wide[i], lines[i], sums[i])],
        out_shape=shapes * 2,
        scratch_shapes=[pltpu.VMEM((2, ROW_LEN, ROW_LEN), f32)],
        compiler_params=pltpu.CompilerParams(vmem_limit_bytes=60 * MIB),
        cost_estimate=pl.CostEstimate(flops=pairs * rows * 4 * 10**9, bytes_accessed=pairs * rows * 4 * MIB, transcendentals=0),
    )(*first, *second, *after)
    return done[:3], done[3:]


def normalize(value, gain, shift):
    center = value - jnp.mean(value, axis=1, keepdims=True)
    inverse = lax.rsqrt(jnp.mean(center * center, axis=1, keepdims=True) + 1e-5)
    normed = center * inverse
    return normed, inverse, normed * gain + shift


def normalize_back(upstream, normed, inverse, gain):
    scaled = upstream * gain
    return inverse * (
        scaled
        - jnp.mean(scaled, axis=1, keepdims=True)
        - normed * jnp.mean(scaled * normed, axis=1, keepdims=True)
    )


def column_sum(value):
    return jnp.sum(value, axis=0, keepdims=True)


def middle_kernel(
    blocks, order_ref,
    om_ref, ot_ref, x_ref, c_ref, vec_ref, bu_ref, uma_ref, umb_ref, uta_ref, utb_ref, dm_ref, dt_ref,
    *refs,
):
    (
        out_ref, dh1_ref, a_ref, g_ref, dom_ref, dot_ref, dy1m_ref, dy1t_ref, dy2m_ref, dy2t_ref, dzm_ref, dzt_ref,
        vsum_ref, usum_ref, wo, wu, wd, slope, dy, sems,
    ) = refs[-20:]
    step = pl.program_id(0)
    width, hidden = wu.shape
    core = order_ref[2 * blocks]
    w_half, h_half = width // 2, hidden // 2

    def cols(size, side, first=0, count=None):
        return pl.ds(pl.multiple_of(side * size + first, 128), size if count is None else count)

    up_left = uma_ref.shape[2]
    up_right = h_half - up_left
    rows, deep = uma_ref.shape[1], dm_ref.shape[1]
    sides = ((core, uma_ref, umb_ref, dm_ref), (1 - core, uta_ref, utb_ref, dt_ref))

    def out_moves(k):
        j, at = order_ref[blocks + k], place(k, rows)
        return [(ub.at[j, :, up_right : up_right + w_half], wo.at[at, cols(w_half, s)]) for s, ua, ub, d in sides]

    def up_moves(k):
        i, j, at = order_ref[k], order_ref[blocks + k], place(k, rows)
        first = [(ua.at[i], wu.at[at, cols(h_half, s, 0, up_left)]) for s, ua, ub, d in sides]
        second = [(ub.at[j, :, 0:up_right], wu.at[at, cols(h_half, s, up_left, up_right)]) for s, ua, ub, d in sides]
        return first + second

    def down_moves(k):
        found = []
        for n in range(2):
            i, at = order_ref[(2 + n) * blocks + 1 + k], place(2 * k + n, deep)
            found += [(d.at[i], wd.at[at, cols(w_half, s)]) for s, ua, ub, d in sides]
        return found

    groups = ((out_moves, 0), (up_moves, 2), (down_moves, 6))

    @pl.when(step == 0)
    def _():
        for moves, first in groups:
            copies(moves, sems, blocks, first, wait=False)

    def ready(group):
        @pl.when(step == 0)
        def _():
            copies(groups[group][0], sems, blocks, groups[group][1], start=False)

    ready(0)
    rows_of = lambda side: cols(w_half, side)
    b_out, b_down, gain1, shift1, gain2, shift2 = [vec_ref[i : i + 1, :] for i in range(2, 8)]
    first = x_ref[...].astype(f32) + dot(om_ref[...], wo[rows_of(core), :]) + dot(ot_ref[...], wo[rows_of(1 - core), :]) + b_out
    n1, r1, a = normalize(first, gain1, shift1)
    ab = a.astype(bf16)
    a_ref[...] = ab
    second = a + b_down
    chunk = h_half // 2
    ready(1)
    for f in range(0, hidden, chunk):
        at = slice(f, f + chunk)
        z = dot(ab, wu[:, at]) + bu_ref[:, at]
        mass = 0.5 * (1.0 + lax.erf(z * (1.0 / math.sqrt(2.0))))
        slope[:, at] = mass + z * jnp.exp(-0.5 * z * z) * (1.0 / math.sqrt(2.0 * math.pi))
        active = (z * mass).astype(bf16)
        g_ref[:, at] = active
        if f == 0:
            ready(2)
        second = second + dot(active, wd[at, :])
    n2, r2, out = normalize(second, gain2, shift2)
    out_ref[...] = out.astype(bf16)
    c = c_ref[...].astype(f32)
    dh2 = normalize_back(c, n2, r2, gain2)
    dy2 = dh2.astype(bf16)
    dy[...] = dy2
    dy2m_ref[...] = dy[:, cols(w_half, core)]
    dy2t_ref[...] = dy[:, cols(w_half, 1 - core)]
    da = dh2
    parts = []
    for side, dz_ref in ((core, dzm_ref), (1 - core, dzt_ref)):
        for f in range(0, h_half, chunk):
            at = cols(h_half, side, f, chunk)
            dz = dot(dy2, wd[at, :], NT) * slope[:, at]
            parts.append((at, column_sum(dz)))
            dzb = dz.astype(bf16)
            dz_ref[:, f : f + chunk] = dzb
            da = da + dot(dzb, wu[:, at], NT)
    dh1 = normalize_back(da, n1, r1, gain1)
    dh1_ref[...] = dh1
    dy1 = dh1.astype(bf16)
    dy[...] = dy1
    dy1m_ref[...] = dy[:, cols(w_half, core)]
    dy1t_ref[...] = dy[:, cols(w_half, 1 - core)]
    dom_ref[...] = dot(dy1, wo[rows_of(core), :], NT).astype(bf16)
    dot_ref[...] = dot(dy1, wo[rows_of(1 - core), :], NT).astype(bf16)
    sums = [column_sum(t) for t in (dh1, dh2, da * n1, da, c * n2, c)]
    vsum = jnp.concatenate(sums + [jnp.zeros((2, c.shape[1]), f32)], axis=0)

    @pl.when(step == 0)
    def _():
        vsum_ref[...] = vsum
        for at, part in parts:
            usum_ref[:, at] = part

    @pl.when(step > 0)
    def _():
        vsum_ref[...] += vsum
        for at, part in parts:
            usum_ref[:, at] += part


def middle(order, om, ot, x, c, vec, bu, up, down, after=(), block=256):
    tokens, width = x.shape
    hidden = bu.shape[1]
    blocks = up[0].shape[0]
    by_token = lambda n: pl.BlockSpec((block, n), lambda i, order: (i, 0))
    fixed = lambda s: pl.BlockSpec(s, lambda i, order: (0, 0))
    half, h_half = width // 2, hidden // 2
    outs = [(width, bf16), (width, f32), (width, bf16), (hidden, bf16)] + [(half, bf16)] * 6 + [(h_half, bf16)] * 2
    return pl.pallas_call(
        partial(middle_kernel, blocks),
        grid_spec=pltpu.PrefetchScalarGridSpec(
            num_scalar_prefetch=1,
            grid=(tokens // block,),
            in_specs=[by_token(half)] * 2
            + [by_token(width)] * 2
            + [fixed(vec.shape), fixed(bu.shape)]
            + [pl.BlockSpec(memory_space=pl.ANY)] * (6 + len(after)),
            out_specs=[by_token(n) for n, _ in outs] + [fixed((8, width)), fixed((1, hidden))],
            scratch_shapes=[
                pltpu.VMEM((width, width), bf16),
                pltpu.VMEM((width, hidden), bf16),
                pltpu.VMEM((hidden, width), bf16),
                pltpu.VMEM((block, hidden), f32),
                pltpu.VMEM((block, width), bf16),
                pltpu.SemaphoreType.DMA((10, blocks)),
            ],
        ),
        out_shape=[shape_of((tokens, n), t) for n, t in outs] + [shape_of((8, width), f32), shape_of((1, hidden), f32)],
        compiler_params=pltpu.CompilerParams(vmem_limit_bytes=50 * MIB),
        cost_estimate=pl.CostEstimate(flops=4 * 10**10, bytes_accessed=40 * MIB, transcendentals=0),
    )(order, om, ot, x, c, vec, bu, *up, *down, *after)


def copies(moves, sems, count, first=0, start=True, wait=True):
    def each(k, act):
        for i, (source, target) in enumerate(moves(k)):
            act(pltpu.make_async_copy(source, target, sems.at[first + i, k]))

    if start:
        lax.fori_loop(0, count, lambda k, c: (each(k, lambda copy: copy.start()), c)[1], 0)
    if wait:
        lax.fori_loop(0, count, lambda k, c: (each(k, lambda copy: copy.wait()), c)[1], 0)


def place(k, rows):
    return pl.ds(pl.multiple_of(k * rows, rows), rows)


def project_kernel(blocks, order_ref, x_ref, bias_ref, w_ref, *refs):
    out_ref, weight, sems = refs[-3:]
    rows, left = w_ref.shape[1:]
    right = weight.shape[1] - left

    @pl.when(pl.program_id(0) == 0)
    def _():
        def moves(k):
            at = place(k, rows)
            return [
                (w_ref.at[order_ref[k]], weight.at[at, 0:left]),
                (w_ref.at[blocks + order_ref[blocks + k], :, 0:right], weight.at[at, left : left + right]),
            ]

        copies(moves, sems, blocks)

    out_ref[...] = (dot(x_ref[...], weight[...]) + bias_ref[...]).astype(bf16)


def project(order, flip, x, bias, gathered, after=(), block=512):
    tokens, width = x.shape
    blocks, outs = gathered.shape[0] // 2, bias.shape[1] // 2
    half = lambda i, order: (0, 1 - order[2 * blocks] if flip else order[2 * blocks])
    return pl.pallas_call(
        partial(project_kernel, blocks),
        grid_spec=pltpu.PrefetchScalarGridSpec(
            num_scalar_prefetch=1,
            grid=(tokens // block,),
            in_specs=[
                pl.BlockSpec((block, width), lambda i, order: (i, 0)),
                pl.BlockSpec((1, outs), half),
            ]
            + [pl.BlockSpec(memory_space=pl.ANY)] * (1 + len(after)),
            out_specs=pl.BlockSpec((block, outs), lambda i, order: (i, 0)),
            scratch_shapes=[pltpu.VMEM((width, outs), bf16), pltpu.SemaphoreType.DMA((2, blocks))],
        ),
        out_shape=shape_of((tokens, outs), bf16),
        compiler_params=pltpu.CompilerParams(vmem_limit_bytes=60 * MIB),
        cost_estimate=pl.CostEstimate(flops=2 * tokens * width * outs, bytes_accessed=8 * MIB, transcendentals=0),
    )(order, x, bias, gathered, *after)


def token_kernel(blocks, order_ref, base_ref, dm_ref, dt_ref, wm_ref, wt_ref, *refs):
    out_ref, mine, theirs, sems = refs[-4:]
    rows, left = wm_ref.shape[1:]
    right = mine.shape[1] - left

    @pl.when(pl.program_id(0) == 0)
    def _():
        def moves(k):
            at, i, j = place(k, rows), order_ref[k], blocks + order_ref[blocks + k]
            return [
                (wm_ref.at[i], mine.at[at, 0:left]),
                (wm_ref.at[j, :, 0:right], mine.at[at, left : left + right]),
                (wt_ref.at[i], theirs.at[at, 0:left]),
                (wt_ref.at[j, :, 0:right], theirs.at[at, left : left + right]),
            ]

        copies(moves, sems, blocks)

    total = base_ref[...] + dot(dm_ref[...], mine[...], NT) + dot(dt_ref[...], theirs[...], NT)
    out_ref[...] = total.astype(bf16)


def token_gradient(order, base, dm, dt, gathered, after=(), block=256):
    tokens, width = base.shape
    blocks, outs = gathered[0].shape[0] // 2, dm.shape[1]
    by_token = lambda n: pl.BlockSpec((block, n), lambda i, order: (i, 0))
    return pl.pallas_call(
        partial(token_kernel, blocks),
        grid_spec=pltpu.PrefetchScalarGridSpec(
            num_scalar_prefetch=1,
            grid=(tokens // block,),
            in_specs=[by_token(width), by_token(outs), by_token(outs)]
            + [pl.BlockSpec(memory_space=pl.ANY)] * (2 + len(after)),
            out_specs=by_token(width),
            scratch_shapes=[pltpu.VMEM((width, outs), bf16)] * 2 + [pltpu.SemaphoreType.DMA((4, blocks))],
        ),
        out_shape=shape_of((tokens, width), bf16),
        compiler_params=pltpu.CompilerParams(vmem_limit_bytes=24 * MIB),
        cost_estimate=pl.CostEstimate(flops=4 * tokens * width * outs, bytes_accessed=14 * MIB, transcendentals=0),
    )(order, base, dm, dt, *gathered, *after)


TABLE_AT, UP_AT = 8, 32


def spread_kernel(devices, order_ref, b_ref, line_ref, vec_ref, up_ref, bias_ref, full, tab):
    blocks, rows = b_ref.shape[0:2]
    width, heads = vec_ref.shape[1], 2 * line_ref.shape[0]
    for k in range(blocks):
        full[rows * k : rows * k + rows, :] = b_ref[order_ref[blocks + k]].astype(f32)
    each, per, ups = width // devices, tab.shape[0] // devices, up_ref.shape[1] // devices
    vec_ref[...] = full[...].T[0:8, :]
    for d in range(devices):
        tab[per * d : per * d + per, :] = full[each * d : each * d + per, :]
        up_ref[:, ups * d : ups * d + ups] = full[each * d : each * d + 1, UP_AT : UP_AT + ups]
    table = tab[...].T[TABLE_AT : TABLE_AT + heads, :]
    buckets = table.shape[1]
    half, rest = buckets // 2, (ROW_LEN - buckets) // 2
    ends = [jnp.broadcast_to(table[:, i : i + 1], (heads, rest)) for i in (buckets - 1, 0)]
    lines = jnp.concatenate([table[:, half:], *ends, table[:, :half]], axis=1)
    for g in range(heads // 2):
        line_ref[g] = lines[2 * g : 2 * g + 2, :]
    for g in range(heads // 2):
        bias_ref[:, 384 * g : 384 * g + 128] = vec_ref[0:1, 128 * g : 128 * g + 128]
        bias_ref[:, 384 * g + 128 : 384 * g + 256] = jnp.zeros((1, 128), f32)
        bias_ref[:, 384 * g + 256 : 384 * g + 384] = vec_ref[1:2, 128 * g : 128 * g + 128]


def spread_small(order, b, devices, width, heads, buckets, hidden):
    blocks, rows = b.shape[0] // 2, b.shape[1]
    last = b.shape[2] // 128 - 1
    fixed = lambda s: pl.BlockSpec(s, lambda i, order: (0,) * len(s))
    shapes = [(heads // 2, 2, ROW_LEN), (8, width), (1, hidden), (1, 3 * width)]
    return pl.pallas_call(
        partial(spread_kernel, devices),
        grid_spec=pltpu.PrefetchScalarGridSpec(
            num_scalar_prefetch=1,
            grid=(1,),
            in_specs=[pl.BlockSpec((blocks, rows, 128), lambda i, order: (1, 0, last))],
            out_specs=[fixed(s) for s in shapes],
            scratch_shapes=[pltpu.VMEM((width, 128), f32), pltpu.VMEM((buckets, 128), f32)],
        ),
        out_shape=[shape_of(s, f32) for s in shapes],
        compiler_params=pltpu.CompilerParams(vmem_limit_bytes=8 * MIB),
        cost_estimate=pl.CostEstimate(flops=10**6, bytes_accessed=MIB, transcendentals=0),
    )(order, b)


def collect_kernel(devices, buckets, core_ref, vsum_ref, usum_ref, ms_ref, ts_ref, ml_ref, tl_ref, out_ref, tall, sums, lines):
    core = core_ref[0]
    width = vsum_ref.shape[1]
    pairs = ms_ref.shape[0]
    sums[core], sums[1 - core] = ms_ref[...], ts_ref[...]
    for g in range(pairs):
        lines[core, 2 * g : 2 * g + 2, :] = ml_ref[g]
        lines[1 - core, 2 * g : 2 * g + 2, :] = tl_ref[g]
    tall[...] = jnp.zeros_like(tall)
    tall[2:8, :] = vsum_ref[0:6, :]
    for side in range(2):
        for g in range(pairs):
            at = 128 * (side * pairs + g)
            tall[0:2, at : at + 128] = sums[side, g]
    out_ref[...] = tall[...].T
    line = jnp.concatenate([lines[0], lines[1]], axis=0)
    heads = line.shape[0]
    half, middle = buckets // 2, ROW_LEN // 2
    far = jnp.sum(line[:, half:middle], axis=1, keepdims=True)
    near = jnp.sum(line[:, middle : ROW_LEN - half], axis=1, keepdims=True)
    place = lax.broadcasted_iota(jnp.int32, (heads, half), 1)
    upper = line[:, :half] + jnp.where(place == half - 1, far, 0.0)
    lower = line[:, ROW_LEN - half :] + jnp.where(place == 0, near, 0.0)
    table = jnp.concatenate([lower, upper], axis=1)
    below = jnp.zeros((128 - TABLE_AT - heads, buckets), f32)
    table = jnp.concatenate([jnp.zeros((TABLE_AT, buckets), f32), table, below], axis=0).T
    each, per, ups = width // devices, buckets // devices, usum_ref.shape[1] // devices
    for d in range(devices):
        out_ref[each * d : each * d + per, :] += table[per * d : per * d + per, :]
        out_ref[each * d : each * d + 1, UP_AT : UP_AT + ups] = usum_ref[:, ups * d : ups * d + ups]


def collect_small(core, devices, buckets, vsum, usum, mine, theirs):
    width = vsum.shape[1]
    pairs = mine[1].shape[0]
    args = [vsum, usum, mine[1], theirs[1], mine[0], theirs[0]]
    whole = lambda t: pl.BlockSpec(t.shape, lambda i, core: (0,) * t.ndim)
    return pl.pallas_call(
        partial(collect_kernel, devices, buckets),
        grid_spec=pltpu.PrefetchScalarGridSpec(
            num_scalar_prefetch=1,
            grid=(1,),
            in_specs=[whole(t) for t in args],
            out_specs=pl.BlockSpec((width, 128), lambda i, core: (0, 0)),
            scratch_shapes=[
                pltpu.VMEM((128, width), f32),
                pltpu.VMEM((2, pairs, 2, 128), f32),
                pltpu.VMEM((2, 2 * pairs, ROW_LEN), f32),
            ],
        ),
        out_shape=shape_of((width, 128), f32),
        compiler_params=pltpu.CompilerParams(vmem_limit_bytes=8 * MIB),
        cost_estimate=pl.CostEstimate(flops=10**6, bytes_accessed=MIB, transcendentals=0),
    )(core, *args)


def pack_kernel(core_ref, *refs):
    vectors, (table_ref, up_ref, q_ref, k_ref, v_ref, wo_ref, wu_ref, wd_ref) = refs[:8], refs[8:16]
    outs, (tall, small) = refs[16:22], refs[22:]
    rows = q_ref.shape[0]
    for i, ref in enumerate(vectors):
        tall[i : i + 1, 0:rows] = ref[...]
    small[...] = tall[...].T[0:rows, :]
    lane = lax.broadcasted_iota(jnp.int32, small.shape, 1)
    small[...] = jnp.where(lane < 8, small[...], 0.0)
    per, heads = table_ref.shape
    small[0:per, TABLE_AT : TABLE_AT + heads] = table_ref[...]
    small[0:1, UP_AT : UP_AT + up_ref.shape[1]] = up_ref[...]
    extra = small[...].astype(bf16)
    low = lambda ref, first, last: ref[:, first:last].astype(bf16)
    h, f = wo_ref.shape[1] // 2, wu_ref.shape[1] // 2

    def write(side, square, up, down):
        for g in range(h // 128):
            at = side * h + 128 * g
            for i, ref in enumerate((q_ref, k_ref, v_ref)):
                square[:, 384 * g + 128 * i : 384 * g + 128 * i + 128] = low(ref, at, at + 128)
        square[:, 3 * h : 3 * h + 128] = extra
        up[:, 0:f] = low(wu_ref, side * f, side * f + f)
        up[:, f : f + h] = low(wo_ref, side * h, side * h + h)
        down[...] = low(wd_ref, side * h, side * h + h)

    @pl.when(core_ref[0] == 0)
    def _():
        write(0, *outs[0:3])
        write(1, *outs[3:6])

    @pl.when(core_ref[0] == 1)
    def _():
        write(1, *outs[0:3])
        write(0, *outs[3:6])


def pack(core, vectors, table, up, matrices):
    rows, width = matrices[0].shape
    args = [t.reshape(1, -1) for t in vectors] + [table, up.reshape(1, -1), *matrices]
    whole = lambda s: pl.BlockSpec(s, lambda i, core: (0, 0))
    shapes = [
        (rows, 3 * width // 2 + 128),
        (rows, (matrices[4].shape[1] + width) // 2),
        (matrices[5].shape[0], width // 2),
    ] * 2
    return pl.pallas_call(
        pack_kernel,
        grid_spec=pltpu.PrefetchScalarGridSpec(
            num_scalar_prefetch=1,
            grid=(1,),
            in_specs=[whole(t.shape) for t in args],
            out_specs=[whole(s) for s in shapes],
            scratch_shapes=[pltpu.VMEM((128, 128), f32), pltpu.VMEM((rows, 128), f32)],
        ),
        out_shape=[shape_of(s, bf16) for s in shapes],
        compiler_params=pltpu.CompilerParams(vmem_limit_bytes=60 * MIB),
        cost_estimate=pl.CostEstimate(flops=10**6, bytes_accessed=2 * MIB, transcendentals=0),
    )(core, *args)


class Links:
    def __init__(self, mesh):
        wide, narrow = mesh.shape[WIDE], mesh.shape[NARROW]
        self.sizes = (wide // 2, 2, narrow // 2, 2)
        w, n = lax.axis_index(WIDE), lax.axis_index(NARROW)
        self.place = (w // 2, w % 2, n // 2, n % 2)
        self.core = self.place[CORE]
        self.chips = wide * narrow // 2

    def number(self, at):
        return ((at[Z] * self.sizes[X] + at[X]) * self.sizes[Y] + at[Y]) * 2 + at[CORE]

    def fetch(self, value, axis, step):
        pairs = []
        for z in range(self.sizes[Z]):
            for x in range(self.sizes[X]):
                for y in range(self.sizes[Y]):
                    for c in range(2):
                        here = (z, x, y, c)
                        there = list(here)
                        there[axis] = (there[axis] + step) % self.sizes[axis]
                        pairs.append((self.number(there), self.number(here)))
        return lax.ppermute(value, AXES, pairs)

    def others(self, value, axis):
        return [self.fetch(value, axis, k) for k in range(1, self.sizes[axis])]

    def swapped(self, kept, sent):
        even = self.core == 0
        got = self.fetch(sent, CORE, 1)
        return jnp.where(even, kept, got), jnp.where(even, got, kept)

    def order(self):
        chip = jnp.arange(self.chips, dtype=jnp.int32)
        sz, sx, sy = self.sizes[:3]
        kz = (chip // (sx * sy) - self.place[Z]) % sz
        kx = (chip // sy - self.place[X]) % sx
        ky = (chip - self.place[Y]) % sy
        plane = 2 * ((kz * sy + ky) * sx + kx)
        return jnp.concatenate(
            [
                (ky * sx + kx) * sz + kz,
                (kx * sy + ky) * sz + kz,
                self.core.reshape(1),
                plane,
                plane + 1,
            ]
        ).astype(jnp.int32)

    def finish(self, total):
        rows = total.shape[0] // 2
        even = self.core == 0
        own = jnp.where(even, total[:rows], total[rows:])
        return own, self.fetch(jnp.where(even, total[rows:], total[:rows]), CORE, 1)


def ring(me, k, size):
    at = me + k
    return jnp.where(at >= size, at - size, at)


def fold_1_kernel(halves, sizes, count, place_ref, *refs):
    kept, got, outs = refs[:count], refs[count : 2 * count], refs[2 * count :]
    split = sizes[Y]
    a_outs, b_outs = outs[:split], outs[split:]

    def write(out, at, half, x, y):
        rows, column = out.shape[2], 0
        for piece, part, first, last in half:
            source = (0, x, y, part, slice(None), slice(first, last))
            value = kept[piece][source] + got[piece][source].astype(f32)
            for row in range(0, value.shape[0], rows):
                some = value[row : row + rows, :].astype(out.dtype)
                out[0, at, :, column : column + last - first] = some
                column += last - first

    for k, out in enumerate(a_outs):
        y = ring(place_ref[Y], k, sizes[Y])
        for x in range(sizes[X]):
            write(out, x, halves[0], x, y)
    for k, out in enumerate(b_outs):
        x = ring(place_ref[X], k, sizes[X])
        for y in range(sizes[Y]):
            write(out, y, halves[1], x, y)


def fold_2_kernel(sizes, place_ref, *refs):
    sy, sx = sizes[Y], sizes[X]
    a_in, b_in, outs = refs[:sy], refs[sy : sy + sx], refs[sy + sx :]
    a_outs, b_outs = outs[:sx], outs[sx:]

    def value(ins, at):
        total = ins[0][0, at]
        for piece in ins[1:]:
            total = total + piece[0, at].astype(f32)
        return total

    for k, out in enumerate(a_outs):
        out[0] = value(a_in, ring(place_ref[X], k, sx)).astype(out.dtype)
    for k, out in enumerate(b_outs):
        out[0] = value(b_in, ring(place_ref[Y], k, sy)).astype(out.dtype)


def fold_3_kernel(sizes, place_ref, *refs):
    sy, sx = sizes[Y], sizes[X]
    a_in, b_in, outs = refs[:sx], refs[sx : sx + sy], refs[sx + sy :]
    rows, columns = a_in[0].shape[1:]
    for k, out in enumerate(outs):
        z = ring(place_ref[Z], k, sizes[Z])
        for n, ins in enumerate((a_in, b_in)):
            total = ins[0][z]
            for piece in ins[1:]:
                total = total + piece[z].astype(f32)
            first = n * columns
            out[0, :, first : first + total.shape[1]] = total.astype(out.dtype)


def fold_call(kernel, place, ins, outs, steps):
    block = lambda s: pl.BlockSpec((s[0] // steps,) + tuple(s[1:]), lambda i, place: (i,) + (0,) * (len(s) - 1))
    return pl.pallas_call(
        kernel,
        grid_spec=pltpu.PrefetchScalarGridSpec(
            num_scalar_prefetch=1,
            grid=(steps,),
            in_specs=[block(t.shape) for t in ins],
            out_specs=[block(s) for s, _ in outs],
        ),
        out_shape=[shape_of(s, t) for s, t in outs],
        compiler_params=pltpu.CompilerParams(vmem_limit_bytes=24 * MIB),
        cost_estimate=pl.CostEstimate(flops=10**6, bytes_accessed=8 * MIB, transcendentals=0),
    )(place, *ins)


class Fold:
    def __init__(self, links, halves):
        self.links, self.halves = links, halves
        self.place = jnp.stack(links.place).astype(jnp.int32)

    def to_others(self, values, axis):
        size = self.links.sizes[axis]
        return [self.links.fetch(v, axis, size - k) for k, v in enumerate(values) if k]

    def first(self, kept, got):
        sizes = self.links.sizes
        sz, sx, sy = sizes[:3]
        rows = kept[0].shape[4]
        wide = [sum((e[3] - e[2]) * kept[e[0]].shape[4] // rows for e in half) for half in self.halves]
        kinds = lambda shape, n: [(shape, f32)] + [(shape, bf16)] * (n - 1)
        outs = kinds((sz, sx, rows, wide[0]), sy) + kinds((sz, sy, rows, wide[1]), sx)
        done = fold_call(partial(fold_1_kernel, self.halves, sizes, len(kept)), self.place, [*kept, *got], outs, sz)
        a, b = done[:sy], done[sy:]
        return [a[0], b[0]], self.to_others(a, Y), self.to_others(b, X)

    def second(self, own, got_y, got_x):
        sizes = self.links.sizes
        sz, sx, sy = sizes[:3]
        kinds = lambda t, n: [((sz,) + t.shape[2:], f32)] + [((sz,) + t.shape[2:], bf16)] * (n - 1)
        outs = kinds(own[0], sx) + kinds(own[1], sy)
        done = fold_call(partial(fold_2_kernel, sizes), self.place, [own[0], *got_y, own[1], *got_x], outs, sz)
        a, b = done[:sx], done[sx:]
        return [a[0], b[0]], self.to_others(a, X), self.to_others(b, Y)

    def third(self, own, got_x, got_y):
        sizes = self.links.sizes
        rows, ca = own[0].shape[1:]
        shape = (1, rows, ca + own[1].shape[2])
        outs = [(shape, f32)] + [(shape, bf16)] * (sizes[Z] - 1)
        ins = [own[0], *got_x, own[1], *got_y]
        done = fold_call(partial(fold_3_kernel, sizes), self.place, ins, outs, 1)
        return done[0], self.to_others(done, Z)

    def last(self, own, got):
        for piece in got:
            own = own + piece.astype(f32)
        return own[0]


def last_kernel(heads, core_ref, own_ref, *refs):
    pieces, outs = refs[: -(2 + 8 + 2)], refs[-(2 + 8 + 2) :]
    keep_ref, send_ref, vectors, table_ref, up_ref = outs[0], outs[1], outs[2:10], outs[10], outs[11]
    rows, width = keep_ref.shape
    total = own_ref[0]
    for piece in pieces:
        total = total + piece[0].astype(f32)

    def write(own, other):
        keep_ref[...] = own[:, 0:width]
        send_ref[...] = other[:, 0:width]
        small = own[:, width:]
        table_ref[...] = small[0 : table_ref.shape[0], TABLE_AT : TABLE_AT + heads]
        up_ref[...] = small[0:1, UP_AT : UP_AT + up_ref.shape[1]]
        turned = jnp.concatenate([small, jnp.zeros((128 - rows, 128), f32)], axis=0).T
        for i, ref in enumerate(vectors):
            ref[...] = turned[i : i + 1, 0:rows]

    @pl.when(core_ref[0] == 0)
    def _():
        write(total[:rows], total[rows:])

    @pl.when(core_ref[0] == 1)
    def _():
        write(total[rows:], total[:rows])


def join_kernel(core_ref, keep_ref, got_ref, *outs):
    def write(sides):
        for s, side in enumerate(sides):
            for g in range(side.shape[1] // 384):
                at = s * (side.shape[1] // 3) + 128 * g
                for i, out in enumerate(outs):
                    out[:, at : at + 128] = side[:, 384 * g + 128 * i : 384 * g + 128 * i + 128]

    @pl.when(core_ref[0] == 0)
    def _():
        write((keep_ref, got_ref))

    @pl.when(core_ref[0] == 1)
    def _():
        write((got_ref, keep_ref))


def join_wide_kernel(core_ref, keep_ref, got_ref, down_keep_ref, down_got_ref, out_ref, up_ref, down_ref):
    h, f = out_ref.shape[1] // 2, up_ref.shape[1] // 2

    def write(sides, downs):
        for s in range(2):
            up_ref[:, s * f : s * f + f] = sides[s][:, 0:f]
            out_ref[:, s * h : s * h + h] = sides[s][:, f : f + h]
            down_ref[:, s * h : s * h + h] = downs[s][...]

    @pl.when(core_ref[0] == 0)
    def _():
        write((keep_ref, got_ref), (down_keep_ref, down_got_ref))

    @pl.when(core_ref[0] == 1)
    def _():
        write((got_ref, keep_ref), (down_got_ref, down_keep_ref))


def whole_call(kernel, core, ins, outs):
    whole = lambda s: pl.BlockSpec(s, lambda i, core: (0,) * len(s))
    return pl.pallas_call(
        kernel,
        grid_spec=pltpu.PrefetchScalarGridSpec(
            num_scalar_prefetch=1,
            grid=(1,),
            in_specs=[whole(t.shape) for t in ins],
            out_specs=[whole(s) for s in outs],
        ),
        out_shape=[shape_of(s, f32) for s in outs],
        compiler_params=pltpu.CompilerParams(vmem_limit_bytes=16 * MIB),
        cost_estimate=pl.CostEstimate(flops=10**6, bytes_accessed=2 * MIB, transcendentals=0),
    )(core, *ins)


def segments(lengths):
    place = jnp.arange(ROW_LEN, dtype=jnp.int32)
    ending = jnp.cumsum(lengths, axis=1)
    return jnp.sum((place[None, :, None] >= ending[:, None, :]).astype(jnp.int32), axis=2)


def per_device(
    mesh, tokens, cotangent, pair_lengths, w_query, w_key, w_value, w_output, w_up, w_down, b_query, b_value,
    b_output, b_up, b_down, first_gain, first_shift, second_gain, second_shift, bucket_bias,
):
    links = Links(mesh)
    devices = 2 * links.chips
    rows, width = w_query.shape
    hidden = w_up.shape[1]
    heads = bucket_bias.shape[1]
    buckets = bucket_bias.shape[0] * devices
    w_half, h_half = width // 2, hidden // 2
    low = lambda t: t.astype(bf16)
    barrier = lax.optimization_barrier
    core = links.core
    even = core == 0
    order = links.order()
    blocks = lambda a, b: [a, b]
    deep = square_blocks = lambda t: t
    if (2 * rows) % 16 or w_down.shape[0] % 16:
        found, order = order, jnp.concatenate([jnp.zeros((2,), jnp.int32), core.reshape(1), jnp.arange(2, dtype=jnp.int32)])
        n = links.chips
        sort = lambda t, first: jnp.take(t, found[first : first + n], axis=0)

        def blocks(a, b):
            return [t.reshape(1, -1, t.shape[2]) for t in (sort(a, 0), sort(b, n))]

        def square_blocks(t):
            return jnp.stack([sort(t[:n], 0), sort(t[n:], n)]).reshape(2, -1, t.shape[2])

        def deep(t):
            both = jnp.stack([sort(t, 2 * n + 1), sort(t, 3 * n + 1)], axis=1)
            return both.reshape(2, -1, t.shape[2])

    half = 3 * w_half
    cut = (half + 128) // 2
    up_cut = (h_half + w_half + 128) // 256 * 128
    packed = pack(
        core.reshape(1),
        [b_query, b_value, b_output, b_down, first_gain, first_shift, second_gain, second_shift],
        bucket_bias,
        b_up,
        [w_query, w_key, w_value, w_output, w_up, w_down],
    )
    swapped = lambda i: jnp.concatenate(links.swapped(packed[i], packed[i + 3]), axis=0)
    pair = swapped(0)
    pair_z = links.others(pair, Z)
    up_pair = swapped(1)
    down_pair = jnp.stack(links.swapped(packed[2], packed[5]))
    down_x = links.others(down_pair, X)

    def together(*groups):
        sizes = [len(g) for g in groups]
        flat = barrier(tuple(t for g in groups for t in g))
        out = []
        for size in sizes:
            out.append(list(flat[:size]))
            flat = flat[size:]
        return out

    def spans(*groups):
        leaves, tree = jax.tree.flatten(tuple(groups))
        return jax.tree.unflatten(tree, barrier(tuple(leaves)))

    def chips(value, got):
        value = jnp.stack([value] + got)
        return value.reshape((-1,) + value.shape[-2:])

    def plane_1(value, cut):
        return [value[:, :, :cut], value[:, :, cut:]], links.others(value[:, :, :cut], X), links.others(value[:, :, cut:], Y)

    def plane_2(ab, got_x, got_y):
        ab = [chips(ab[0], got_x), chips(ab[1], got_y)]
        return ab, links.others(ab[0], Y), links.others(ab[1], X)

    def plane_3(ab, got_y, got_x):
        return chips(ab[0], got_y), chips(ab[1], got_x)

    pair_z, (pair, up_pair), down_x = together(pair_z, (pair, up_pair), down_x)
    stage = plane_1(jnp.stack([pair] + pair_z), cut)
    down_pair = jnp.stack([down_pair] + down_x)
    down_y = links.others(down_pair, Y)
    up_z = links.others(up_pair, Z)
    got_x, got_y, down_y, up_z, (up_pair,) = together(*stage[1:], down_y, up_z, (up_pair,))
    stage = plane_2(stage[0], got_x, got_y)
    down_own = jnp.stack([down_pair] + down_y)
    down_z = links.others(down_own, Z)
    got_y, got_x, up_z, down_z[-1:] = together(*stage[1:], up_z, down_z[-1:])
    mine = jnp.concatenate(plane_3(stage[0], got_y, got_x), axis=0)

    theirs = links.fetch(mine, CORE, 1)
    mine, theirs = square_blocks(mine), square_blocks(theirs)
    lines, vectors, up_bias, bias = spread_small(order, mine, devices, width, heads, buckets, hidden)
    segment = segments(pair_lengths)
    segc, segr = segment[:, :, None], segment[:, None, :]
    pairs = heads // 4
    first_m, first_t = (core * pairs).reshape(1), ((1 - core) * pairs).reshape(1)
    qkv_m = project(order, False, tokens, bias, mine)
    up_z, (qkv_m, bias_t, theirs) = together(up_z, (qkv_m, bias, theirs))
    up_stage = plane_1(jnp.stack([up_pair] + up_z), up_cut)
    o_m, p_m = attend_forward(first_m, lines, segc, segr, qkv_m)
    (o_m, theirs), got_x, got_y = together((o_m, theirs), up_stage[1], up_stage[2])

    up_stage = plane_2(up_stage[0], got_x, got_y)
    qkv_t = project(order, True, tokens, bias_t, theirs)
    o_t, p_t = attend_forward(first_t, lines, segc, segr, qkv_t)
    (o_m, o_t), got_y, got_x = together((o_m, o_t), *up_stage[1:])
    up_a, up_b = plane_3(up_stage[0], got_y, got_x)
    up_theirs = (links.fetch(up_a, CORE, 1), links.fetch(up_b, CORE, 1))
    up_a, up_b, *down_z = barrier((up_a, up_b, *down_z))
    down_mine = jnp.stack([down_own] + down_z)
    down_mine = down_mine.reshape((-1,) + down_mine.shape[-2:])
    down_theirs = links.fetch(down_mine, CORE, 1)

    result, dh1, settled, active, do_m, do_t, dy1_m, dy1_t, dy2_m, dy2_t, dz_m, dz_t, vsum, usum = middle(
        order,
        o_m,
        o_t,
        tokens,
        cotangent,
        vectors,
        up_bias,
        blocks(up_a, up_b) + blocks(*up_theirs),
        [deep(down_mine), deep(down_theirs)],
    )

    def pieces(t, parts=1):
        return t.reshape(links.sizes[:3] + (parts, -1, t.shape[1]))

    exchange = lambda *values: [links.fetch(low(t), CORE, 1) for t in values]
    o_both = jnp.where(even, jnp.concatenate([o_m, o_t], axis=1), jnp.concatenate([o_t, o_m], axis=1))
    up_parts = lambda dz, dy1: [pieces(dot(settled, dz, TN)), pieces(dot(o_both, dy1, TN))]
    wide_fold = Fold(
        links,
        [
            [(0, 0, 0, up_cut), (2, 0, 0, w_half)],
            [(0, 0, up_cut, h_half), (1, 0, 0, w_half), (2, 1, 0, w_half)],
        ],
    )
    square_fold = Fold(links, [[(0, 0, 0, cut)], [(0, 0, cut, half), (1, 0, 0, 128)]])

    got = exchange(*up_parts(dz_t, dy1_t))
    kept = up_parts(dz_m, dy1_m)
    got, kept, (dy2_t, dy2_m) = spans(got, kept, (dy2_t, dy2_m))
    got += exchange(pieces(dot(active, dy2_t, TN), 2))
    kept += [pieces(dot(active, dy2_m, TN), 2)]
    got, kept, (do_t, do_m) = spans(got, kept, (do_t, do_m))

    wide = wide_fold.first(kept, got)
    grads_t, grads_m = attend_backward((qkv_t, do_t, o_t, p_t), (qkv_m, do_m, o_m, p_m))
    wide, grads_t, grads_m = spans(wide, grads_t, grads_m)

    wide = wide_fold.second(*wide)
    square_got = exchange(pieces(dot(tokens, grads_t[0], TN)))
    g_small = pieces(collect_small(core.reshape(1), devices, buckets, vsum, usum, grads_m[1:], grads_t[1:]))
    square_got += exchange(g_small)
    square_kept = [pieces(dot(tokens, grads_m[0], TN)), g_small]
    wide, square_kept, square_got, (d_m, d_t) = spans(wide, square_kept, square_got, (grads_m[0], grads_t[0]))

    square = square_fold.first(square_kept, square_got)
    wide_own, wide_got = wide_fold.third(*wide)
    grad_tokens = token_gradient(order, dh1, d_m, d_t, [mine, theirs])
    square, grad_tokens = spans(square, grad_tokens)

    square = square_fold.second(*square)
    square = spans(square)[0]
    square_own, square_z = square_fold.third(*square)
    wide_got, square_own = spans(wide_got, square_own)
    wide_total = wide_fold.last(wide_own, wide_got)
    wide_a = up_cut + 2 * w_half
    up_total = jnp.concatenate([wide_total[:, :up_cut], wide_total[:, wide_a : wide_a + h_half + w_half - up_cut]], axis=1)
    groups = w_down.shape[0] // (2 * rows)
    down_total = jnp.stack(
        [
            jnp.concatenate([wide_total[:, first + w_half * i : first + w_half * (i + 1)] for i in range(groups)], axis=0)
            for first in (up_cut, wide_total.shape[1] - groups * w_half)
        ]
    ).reshape(-1, w_half)

    core_1 = core.reshape(1)
    out_output, out_up, out_down = whole_call(
        join_wide_kernel,
        core_1,
        [*links.finish(up_total), *links.finish(down_total)],
        [(rows, width), (rows, hidden), w_down.shape],
    )
    shapes = [(rows, half)] * 2 + [(1, rows)] * 8 + [bucket_bias.shape, (1, b_up.shape[0])]
    own, other, *flat = whole_call(partial(last_kernel, heads), core_1, [square_own, *square_z], shapes)
    *flat, out_table, out_b_up = flat
    flat = [t.reshape(-1) for t in flat]
    out_query, out_key, out_value = whole_call(
        join_kernel, core_1, [own, links.fetch(other, CORE, 1)], [(rows, width)] * 3
    )
    return (
        result,
        grad_tokens,
        out_query,
        out_key,
        out_value,
        out_output,
        out_up,
        out_down,
        flat[0],
        flat[1],
        flat[2],
        out_b_up.reshape(-1),
        flat[3],
        flat[4],
        flat[5],
        flat[6],
        flat[7],
        out_table,
    )


def solution(mesh):
    split, line = P(AXES, None), P(AXES)
    return jax.shard_map(
        partial(per_device, mesh),
        mesh=mesh,
        in_specs=(split,) * 9 + (line,) * 9 + (split,),
        out_specs=(split,) * 8 + (line,) * 9 + (split,),
        check_vma=False,
    )
```

```python
from functools import partial
import math

import jax
import jax.numpy as jnp
from jax import lax
from jax.experimental import pallas as pl
from jax.experimental.pallas import tpu as pltpu
from jax.sharding import PartitionSpec as P

WIDE, NARROW = "wide", "narrow"
AXES = (WIDE, NARROW)
Z, X, Y, CORE = range(4)
ROW_LEN = 512
MIB = 1 << 20
bf16, f32 = jnp.bfloat16, jnp.float32
NN = (((1,), (0,)), ((), ()))
NT = (((1,), (1,)), ((), ()))
TN = (((0,), (0,)), ((), ()))


def dot(left, right, dims=NN):
    return lax.dot_general(left, right, dims, preferred_element_type=f32)


def shape_of(shape, dtype):
    return jax.ShapeDtypeStruct(shape, dtype)


def toeplitz(line, ref, head):
    base = jnp.concatenate([pltpu.roll(line, s, 1) if s else line for s in range(8)], axis=0)
    for c in range(16):
        turned = pltpu.roll(base, 8 * c, 1) if c else base
        for b in range(ROW_LEN // 128):
            cut = ROW_LEN - 128 * b
            piece = jnp.concatenate([turned[:, cut:], turned[:, :cut]], axis=1) if b else turned
            first = 128 * b + 8 * c
            ref[head, first : first + 8, :] = piece


def diagonals(ref, head):
    total = None
    for c in range(16):
        turned = None
        for b in range(ROW_LEN // 128):
            first = 128 * b + 8 * c
            piece = ref[head, first : first + 8, :]
            if b:
                piece = jnp.concatenate([piece[:, 128 * b :], piece[:, : 128 * b]], axis=1)
            turned = piece if turned is None else turned + piece
        if c:
            turned = pltpu.roll(turned, ROW_LEN - 8 * c, 1)
        total = turned if total is None else total + turned
    out = total[0:1]
    for s in range(1, 8):
        out = out + pltpu.roll(total[s : s + 1], ROW_LEN - s, 1)
    return out


def forward_kernel(first_ref, line_ref, segc_ref, segr_ref, qkv_ref, *refs):
    o_ref, p_ref, bias, mask = refs[-4:]
    g, r = pl.program_id(0), pl.program_id(1)

    @pl.when(g == 0)
    def _():
        mask[r] = jnp.where(segc_ref[0] == segr_ref[0], 0.0, -1e30)

    @pl.when(r == 0)
    def _():
        for h in range(2):
            toeplitz(line_ref[0, h : h + 1, :], bias, h)

    q, k, v = qkv_ref[:, 0:128], qkv_ref[:, 128:256], qkv_ref[:, 256:384]
    lane = lax.broadcasted_iota(jnp.int32, (ROW_LEN, 128), 1)
    outs = []
    for h in range(2):
        mine = (lane < 64) if h == 0 else (lane >= 64)
        qh = jnp.where(mine, q.astype(f32) * 0.125, 0.0).astype(bf16)
        s = dot(qh, k, NT) + bias[h] + mask[r]
        e = jnp.exp(s - jnp.max(s, axis=1, keepdims=True))
        p = (e * (1.0 / jnp.sum(e, axis=1, keepdims=True))).astype(bf16)
        p_ref[0, h] = p
        outs.append(dot(p, v))
    o_ref[...] = jnp.where(lane < 64, outs[0], outs[1]).astype(bf16)


def attend_forward(first, lines, segc, segr, qkv, after=()):
    pairs, rows = qkv.shape[1] // 384, segc.shape[0]
    return pl.pallas_call(
        forward_kernel,
        grid_spec=pltpu.PrefetchScalarGridSpec(
            num_scalar_prefetch=1,
            grid=(pairs, rows),
            in_specs=[
                pl.BlockSpec((1, 2, ROW_LEN), lambda g, r, first: (g + first[0], 0, 0)),
                pl.BlockSpec((1, ROW_LEN, 1), lambda g, r, first: (r, 0, 0)),
                pl.BlockSpec((1, 1, ROW_LEN), lambda g, r, first: (r, 0, 0)),
                pl.BlockSpec((ROW_LEN, 384), lambda g, r, first: (r, g)),
            ]
            + [pl.BlockSpec(memory_space=pl.ANY)] * len(after),
            out_specs=[
                pl.BlockSpec((ROW_LEN, 128), lambda g, r, first: (r, g)),
                pl.BlockSpec((1, 2, ROW_LEN, ROW_LEN), lambda g, r, first: (r, g, 0, 0)),
            ],
            scratch_shapes=[pltpu.VMEM((2, ROW_LEN, ROW_LEN), f32), pltpu.VMEM((rows, ROW_LEN, ROW_LEN), f32)],
        ),
        out_shape=[
            shape_of((rows * ROW_LEN, 128 * pairs), bf16),
            shape_of((rows, 2 * pairs, ROW_LEN, ROW_LEN), bf16),
        ],
        compiler_params=pltpu.CompilerParams(vmem_limit_bytes=60 * MIB),
        cost_estimate=pl.CostEstimate(flops=pairs * rows * 2 * 10**9, bytes_accessed=pairs * rows * 2 * MIB, transcendentals=0),
    )(first, lines, segc, segr, qkv, *after)


def backward_kernel(*refs):
    ins, outs, acc = (refs[0:4], refs[4:8]), (refs[-7:-4], refs[-4:-1]), refs[-1]
    for side in range(2):

        @pl.when(pl.program_id(0) == side)
        def _():
            backward_step(*ins[side], *outs[side], acc)


def backward_step(qkv_ref, do_ref, o_ref, p_ref, d_ref, line_ref, sums_ref, acc):
    r, last = pl.program_id(2), pl.num_programs(2) - 1
    q, k, v = qkv_ref[:, 0:128], qkv_ref[:, 128:256], qkv_ref[:, 256:384]
    lane = lax.broadcasted_iota(jnp.int32, (ROW_LEN, 128), 1)
    qt = (q.astype(f32) * 0.125).T.astype(bf16)
    do = do_ref[...].astype(f32)
    dot_t = do.T.astype(bf16)
    prod = do * o_ref[...].astype(f32)
    dqs, dks, dvs = [], [], []
    for h in range(2):
        mine = (lane < 64) if h == 0 else (lane >= 64)
        doh = jnp.where(mine, do, 0.0).astype(bf16)
        delta = jnp.sum(jnp.where(mine, prod, 0.0), axis=1, keepdims=True)
        p = p_ref[0, h]
        ds = p.astype(f32) * (dot(doh, v, NT) - delta)

        @pl.when(r == 0)
        def _():
            acc[h] = ds

        @pl.when(r > 0)
        def _():
            acc[h] += ds

        dsb = ds.astype(bf16)
        half = slice(64 * h, 64 * h + 64)
        dqs.append(dot(dsb, k))
        dks.append(dot(qt[half, :], dsb))
        dvs.append(dot(dot_t[half, :], p))
    dq = jnp.where(lane < 64, dqs[0], dqs[1]) * 0.125
    dk = jnp.concatenate(dks, axis=0).T
    dv = jnp.concatenate(dvs, axis=0).T
    d_ref[:, 0:128] = dq.astype(bf16)
    d_ref[:, 128:256] = dk.astype(bf16)
    d_ref[:, 256:384] = dv.astype(bf16)
    sums = jnp.concatenate([jnp.sum(dq, axis=0, keepdims=True), jnp.sum(dv, axis=0, keepdims=True)], axis=0)

    @pl.when(r == 0)
    def _():
        sums_ref[0] = sums

    @pl.when(r > 0)
    def _():
        sums_ref[0] += sums

    @pl.when(r == last)
    def _():
        for h in range(2):
            line_ref[0, h : h + 1, :] = diagonals(acc, h)


def attend_backward(first, second, after=()):
    rows, pairs = first[3].shape[0], first[0].shape[1] // 384
    ends = ((0, 0), (pairs - 1, rows - 1))

    def block(shape, at, side):
        def index(s, g, r):
            mine = s == side
            return at(jnp.where(mine, g, ends[1 - side][0]), jnp.where(mine, r, ends[1 - side][1]))

        return pl.BlockSpec(shape, index)

    both = lambda shape, at: [block(shape, at, side) for side in range(2)]
    by_row, by_pair = lambda g, r: (r, g), lambda g, r: (g, 0, 0)
    wide, half = both((ROW_LEN, 384), by_row), both((ROW_LEN, 128), by_row)
    probs = both((1, 2, ROW_LEN, ROW_LEN), lambda g, r: (r, g, 0, 0))
    lines, sums = both((1, 2, ROW_LEN), by_pair), both((1, 2, 128), by_pair)
    shapes = [
        shape_of((rows * ROW_LEN, 384 * pairs), bf16),
        shape_of((pairs, 2, ROW_LEN), f32),
        shape_of((pairs, 2, 128), f32),
    ]
    done = pl.pallas_call(
        backward_kernel,
        grid=(2, pairs, rows),
        in_specs=[spec for i in range(2) for spec in (wide[i], half[i], half[i], probs[i])]
        + [pl.BlockSpec(memory_space=pl.ANY)] * len(after),
        out_specs=[spec for i in range(2) for spec in (wide[i], lines[i], sums[i])],
        out_shape=shapes * 2,
        scratch_shapes=[pltpu.VMEM((2, ROW_LEN, ROW_LEN), f32)],
        compiler_params=pltpu.CompilerParams(vmem_limit_bytes=50 * MIB),
        cost_estimate=pl.CostEstimate(flops=pairs * rows * 4 * 10**9, bytes_accessed=pairs * rows * 4 * MIB, transcendentals=0),
    )(*first, *second, *after)
    return done[:3], done[3:]


def normalize(value, gain, shift):
    center = value - jnp.mean(value, axis=1, keepdims=True)
    inverse = lax.rsqrt(jnp.mean(center * center, axis=1, keepdims=True) + 1e-5)
    normed = center * inverse
    return normed, inverse, normed * gain + shift


def normalize_back(upstream, normed, inverse, gain):
    scaled = upstream * gain
    return inverse * (
        scaled
        - jnp.mean(scaled, axis=1, keepdims=True)
        - normed * jnp.mean(scaled * normed, axis=1, keepdims=True)
    )


def column_sum(value):
    return jnp.sum(value, axis=0, keepdims=True)


def middle_kernel(
    blocks, order_ref,
    om_ref, ot_ref, x_ref, c_ref, vec_ref, bu_ref, uma_ref, umb_ref, uta_ref, utb_ref, dm_ref, dt_ref,
    *refs,
):
    (
        out_ref, dh1_ref, a_ref, g_ref, dom_ref, dot_ref, dy1m_ref, dy1t_ref, dy2m_ref, dy2t_ref, dzm_ref, dzt_ref,
        vsum_ref, usum_ref, wo, wu, wd, slope, dy, sems,
    ) = refs[-20:]
    step = pl.program_id(0)
    width, hidden = wu.shape
    core = order_ref[2 * blocks]
    w_half, h_half = width // 2, hidden // 2

    def cols(size, side, first=0, count=None):
        return pl.ds(pl.multiple_of(side * size + first, 128), size if count is None else count)

    up_left = uma_ref.shape[2]
    up_right = h_half - up_left
    rows, deep = uma_ref.shape[1], dm_ref.shape[1]
    sides = ((core, uma_ref, umb_ref, dm_ref), (1 - core, uta_ref, utb_ref, dt_ref))

    def out_moves(k):
        j, at = order_ref[blocks + k], place(k, rows)
        return [(ub.at[j, :, up_right : up_right + w_half], wo.at[at, cols(w_half, s)]) for s, ua, ub, d in sides]

    def up_moves(k):
        i, j, at = order_ref[k], order_ref[blocks + k], place(k, rows)
        first = [(ua.at[i], wu.at[at, cols(h_half, s, 0, up_left)]) for s, ua, ub, d in sides]
        second = [(ub.at[j, :, 0:up_right], wu.at[at, cols(h_half, s, up_left, up_right)]) for s, ua, ub, d in sides]
        return first + second

    def down_moves(k):
        found = []
        for n in range(2):
            i, at = order_ref[(2 + n) * blocks + 1 + k], place(2 * k + n, deep)
            found += [(d.at[i], wd.at[at, cols(w_half, s)]) for s, ua, ub, d in sides]
        return found

    groups = ((out_moves, 0), (up_moves, 2), (down_moves, 6))

    @pl.when(step == 0)
    def _():
        for moves, first in groups:
            copies(moves, sems, blocks, first, wait=False)

    def ready(group):
        @pl.when(step == 0)
        def _():
            copies(groups[group][0], sems, blocks, groups[group][1], start=False)

    ready(0)
    rows_of = lambda side: cols(w_half, side)
    b_out, b_down, gain1, shift1, gain2, shift2 = [vec_ref[i : i + 1, :] for i in range(2, 8)]
    first = x_ref[...].astype(f32) + dot(om_ref[...], wo[rows_of(core), :]) + dot(ot_ref[...], wo[rows_of(1 - core), :]) + b_out
    n1, r1, a = normalize(first, gain1, shift1)
    ab = a.astype(bf16)
    a_ref[...] = ab
    second = a + b_down
    chunk = h_half // 2
    ready(1)
    for f in range(0, hidden, chunk):
        at = slice(f, f + chunk)
        z = dot(ab, wu[:, at]) + bu_ref[:, at]
        mass = 0.5 * (1.0 + lax.erf(z * (1.0 / math.sqrt(2.0))))
        slope[:, at] = mass + z * jnp.exp(-0.5 * z * z) * (1.0 / math.sqrt(2.0 * math.pi))
        active = (z * mass).astype(bf16)
        g_ref[:, at] = active
        if f == 0:
            ready(2)
        second = second + dot(active, wd[at, :])
    n2, r2, out = normalize(second, gain2, shift2)
    out_ref[...] = out.astype(bf16)
    c = c_ref[...].astype(f32)
    dh2 = normalize_back(c, n2, r2, gain2)
    dy2 = dh2.astype(bf16)
    dy[...] = dy2
    dy2m_ref[...] = dy[:, cols(w_half, core)]
    dy2t_ref[...] = dy[:, cols(w_half, 1 - core)]
    da = dh2
    parts = []
    for side, dz_ref in ((core, dzm_ref), (1 - core, dzt_ref)):
        for f in range(0, h_half, chunk):
            at = cols(h_half, side, f, chunk)
            dz = dot(dy2, wd[at, :], NT) * slope[:, at]
            parts.append((at, column_sum(dz)))
            dzb = dz.astype(bf16)
            dz_ref[:, f : f + chunk] = dzb
            da = da + dot(dzb, wu[:, at], NT)
    dh1 = normalize_back(da, n1, r1, gain1)
    dh1_ref[...] = dh1
    dy1 = dh1.astype(bf16)
    dy[...] = dy1
    dy1m_ref[...] = dy[:, cols(w_half, core)]
    dy1t_ref[...] = dy[:, cols(w_half, 1 - core)]
    dom_ref[...] = dot(dy1, wo[rows_of(core), :], NT).astype(bf16)
    dot_ref[...] = dot(dy1, wo[rows_of(1 - core), :], NT).astype(bf16)
    sums = [column_sum(t) for t in (dh1, dh2, da * n1, da, c * n2, c)]
    vsum = jnp.concatenate(sums + [jnp.zeros((2, c.shape[1]), f32)], axis=0)

    @pl.when(step == 0)
    def _():
        vsum_ref[...] = vsum
        for at, part in parts:
            usum_ref[:, at] = part

    @pl.when(step > 0)
    def _():
        vsum_ref[...] += vsum
        for at, part in parts:
            usum_ref[:, at] += part


def middle(order, om, ot, x, c, vec, bu, up, down, after=(), block=256):
    tokens, width = x.shape
    hidden = bu.shape[1]
    blocks = up[0].shape[0]
    by_token = lambda n: pl.BlockSpec((block, n), lambda i, order: (i, 0))
    fixed = lambda s: pl.BlockSpec(s, lambda i, order: (0, 0))
    half, h_half = width // 2, hidden // 2
    outs = [(width, bf16), (width, f32), (width, bf16), (hidden, bf16)] + [(half, bf16)] * 6 + [(h_half, bf16)] * 2
    return pl.pallas_call(
        partial(middle_kernel, blocks),
        grid_spec=pltpu.PrefetchScalarGridSpec(
            num_scalar_prefetch=1,
            grid=(tokens // block,),
            in_specs=[by_token(half)] * 2
            + [by_token(width)] * 2
            + [fixed(vec.shape), fixed(bu.shape)]
            + [pl.BlockSpec(memory_space=pl.ANY)] * (6 + len(after)),
            out_specs=[by_token(n) for n, _ in outs] + [fixed((8, width)), fixed((1, hidden))],
            scratch_shapes=[
                pltpu.VMEM((width, width), bf16),
                pltpu.VMEM((width, hidden), bf16),
                pltpu.VMEM((hidden, width), bf16),
                pltpu.VMEM((block, hidden), f32),
                pltpu.VMEM((block, width), bf16),
                pltpu.SemaphoreType.DMA((10, blocks)),
            ],
        ),
        out_shape=[shape_of((tokens, n), t) for n, t in outs] + [shape_of((8, width), f32), shape_of((1, hidden), f32)],
        compiler_params=pltpu.CompilerParams(vmem_limit_bytes=44 * MIB),
        cost_estimate=pl.CostEstimate(flops=4 * 10**10, bytes_accessed=40 * MIB, transcendentals=0),
    )(order, om, ot, x, c, vec, bu, *up, *down, *after)


def copies(moves, sems, count, first=0, start=True, wait=True):
    def each(k, act):
        for i, (source, target) in enumerate(moves(k)):
            act(pltpu.make_async_copy(source, target, sems.at[first + i, k]))

    if start:
        lax.fori_loop(0, count, lambda k, c: (each(k, lambda copy: copy.start()), c)[1], 0)
    if wait:
        lax.fori_loop(0, count, lambda k, c: (each(k, lambda copy: copy.wait()), c)[1], 0)


def place(k, rows):
    return pl.ds(pl.multiple_of(k * rows, rows), rows)


def project_kernel(blocks, order_ref, x_ref, bias_ref, w_ref, *refs):
    out_ref, weight, sems = refs[-3:]
    rows, left = w_ref.shape[1:]
    right = weight.shape[1] - left

    @pl.when(pl.program_id(0) == 0)
    def _():
        def moves(k):
            at = place(k, rows)
            return [
                (w_ref.at[order_ref[k]], weight.at[at, 0:left]),
                (w_ref.at[blocks + order_ref[blocks + k], :, 0:right], weight.at[at, left : left + right]),
            ]

        copies(moves, sems, blocks)

    out_ref[...] = (dot(x_ref[...], weight[...]) + bias_ref[...]).astype(bf16)


def project(order, flip, x, bias, gathered, after=(), block=512):
    tokens, width = x.shape
    blocks, outs = gathered.shape[0] // 2, bias.shape[1] // 2
    half = lambda i, order: (0, 1 - order[2 * blocks] if flip else order[2 * blocks])
    return pl.pallas_call(
        partial(project_kernel, blocks),
        grid_spec=pltpu.PrefetchScalarGridSpec(
            num_scalar_prefetch=1,
            grid=(tokens // block,),
            in_specs=[
                pl.BlockSpec((block, width), lambda i, order: (i, 0)),
                pl.BlockSpec((1, outs), half),
            ]
            + [pl.BlockSpec(memory_space=pl.ANY)] * (1 + len(after)),
            out_specs=pl.BlockSpec((block, outs), lambda i, order: (i, 0)),
            scratch_shapes=[pltpu.VMEM((width, outs), bf16), pltpu.SemaphoreType.DMA((2, blocks))],
        ),
        out_shape=shape_of((tokens, outs), bf16),
        compiler_params=pltpu.CompilerParams(vmem_limit_bytes=60 * MIB),
        cost_estimate=pl.CostEstimate(flops=2 * tokens * width * outs, bytes_accessed=8 * MIB, transcendentals=0),
    )(order, x, bias, gathered, *after)


def token_kernel(blocks, order_ref, base_ref, dm_ref, dt_ref, wm_ref, wt_ref, *refs):
    out_ref, mine, theirs, sems = refs[-4:]
    rows, left = wm_ref.shape[1:]
    right = mine.shape[1] - left

    @pl.when(pl.program_id(0) == 0)
    def _():
        def moves(k):
            at, i, j = place(k, rows), order_ref[k], blocks + order_ref[blocks + k]
            return [
                (wm_ref.at[i], mine.at[at, 0:left]),
                (wm_ref.at[j, :, 0:right], mine.at[at, left : left + right]),
                (wt_ref.at[i], theirs.at[at, 0:left]),
                (wt_ref.at[j, :, 0:right], theirs.at[at, left : left + right]),
            ]

        copies(moves, sems, blocks)

    total = base_ref[...] + dot(dm_ref[...], mine[...], NT) + dot(dt_ref[...], theirs[...], NT)
    out_ref[...] = total.astype(bf16)


def token_gradient(order, base, dm, dt, gathered, after=(), block=256):
    tokens, width = base.shape
    blocks, outs = gathered[0].shape[0] // 2, dm.shape[1]
    by_token = lambda n: pl.BlockSpec((block, n), lambda i, order: (i, 0))
    return pl.pallas_call(
        partial(token_kernel, blocks),
        grid_spec=pltpu.PrefetchScalarGridSpec(
            num_scalar_prefetch=1,
            grid=(tokens // block,),
            in_specs=[by_token(width), by_token(outs), by_token(outs)]
            + [pl.BlockSpec(memory_space=pl.ANY)] * (2 + len(after)),
            out_specs=by_token(width),
            scratch_shapes=[pltpu.VMEM((width, outs), bf16)] * 2 + [pltpu.SemaphoreType.DMA((4, blocks))],
        ),
        out_shape=shape_of((tokens, width), bf16),
        compiler_params=pltpu.CompilerParams(vmem_limit_bytes=24 * MIB),
        cost_estimate=pl.CostEstimate(flops=4 * tokens * width * outs, bytes_accessed=14 * MIB, transcendentals=0),
    )(order, base, dm, dt, *gathered, *after)


TABLE_AT, UP_AT = 8, 32


def spread_kernel(devices, order_ref, b_ref, line_ref, vec_ref, up_ref, bias_ref, full, tab):
    blocks, rows = b_ref.shape[0:2]
    width, heads = vec_ref.shape[1], 2 * line_ref.shape[0]
    for k in range(blocks):
        full[rows * k : rows * k + rows, :] = b_ref[order_ref[blocks + k]].astype(f32)
    each, per, ups = width // devices, tab.shape[0] // devices, up_ref.shape[1] // devices
    vec_ref[...] = full[...].T[0:8, :]
    for d in range(devices):
        tab[per * d : per * d + per, :] = full[each * d : each * d + per, :]
        up_ref[:, ups * d : ups * d + ups] = full[each * d : each * d + 1, UP_AT : UP_AT + ups]
    table = tab[...].T[TABLE_AT : TABLE_AT + heads, :]
    buckets = table.shape[1]
    half, rest = buckets // 2, (ROW_LEN - buckets) // 2
    ends = [jnp.broadcast_to(table[:, i : i + 1], (heads, rest)) for i in (buckets - 1, 0)]
    lines = jnp.concatenate([table[:, half:], *ends, table[:, :half]], axis=1)
    for g in range(heads // 2):
        line_ref[g] = lines[2 * g : 2 * g + 2, :]
    for g in range(heads // 2):
        bias_ref[:, 384 * g : 384 * g + 128] = vec_ref[0:1, 128 * g : 128 * g + 128]
        bias_ref[:, 384 * g + 128 : 384 * g + 256] = jnp.zeros((1, 128), f32)
        bias_ref[:, 384 * g + 256 : 384 * g + 384] = vec_ref[1:2, 128 * g : 128 * g + 128]


def spread_small(order, b, devices, width, heads, buckets, hidden):
    blocks, rows = b.shape[0] // 2, b.shape[1]
    last = b.shape[2] // 128 - 1
    fixed = lambda s: pl.BlockSpec(s, lambda i, order: (0,) * len(s))
    shapes = [(heads // 2, 2, ROW_LEN), (8, width), (1, hidden), (1, 3 * width)]
    return pl.pallas_call(
        partial(spread_kernel, devices),
        grid_spec=pltpu.PrefetchScalarGridSpec(
            num_scalar_prefetch=1,
            grid=(1,),
            in_specs=[pl.BlockSpec((blocks, rows, 128), lambda i, order: (1, 0, last))],
            out_specs=[fixed(s) for s in shapes],
            scratch_shapes=[pltpu.VMEM((width, 128), f32), pltpu.VMEM((buckets, 128), f32)],
        ),
        out_shape=[shape_of(s, f32) for s in shapes],
        compiler_params=pltpu.CompilerParams(vmem_limit_bytes=8 * MIB),
        cost_estimate=pl.CostEstimate(flops=10**6, bytes_accessed=MIB, transcendentals=0),
    )(order, b)


def collect_kernel(devices, buckets, core_ref, vsum_ref, usum_ref, ms_ref, ts_ref, ml_ref, tl_ref, out_ref, tall, sums, lines):
    core = core_ref[0]
    width = vsum_ref.shape[1]
    pairs = ms_ref.shape[0]
    sums[core], sums[1 - core] = ms_ref[...], ts_ref[...]
    for g in range(pairs):
        lines[core, 2 * g : 2 * g + 2, :] = ml_ref[g]
        lines[1 - core, 2 * g : 2 * g + 2, :] = tl_ref[g]
    tall[...] = jnp.zeros_like(tall)
    tall[2:8, :] = vsum_ref[0:6, :]
    for side in range(2):
        for g in range(pairs):
            at = 128 * (side * pairs + g)
            tall[0:2, at : at + 128] = sums[side, g]
    out_ref[...] = tall[...].T
    line = jnp.concatenate([lines[0], lines[1]], axis=0)
    heads = line.shape[0]
    half, middle = buckets // 2, ROW_LEN // 2
    far = jnp.sum(line[:, half:middle], axis=1, keepdims=True)
    near = jnp.sum(line[:, middle : ROW_LEN - half], axis=1, keepdims=True)
    place = lax.broadcasted_iota(jnp.int32, (heads, half), 1)
    upper = line[:, :half] + jnp.where(place == half - 1, far, 0.0)
    lower = line[:, ROW_LEN - half :] + jnp.where(place == 0, near, 0.0)
    table = jnp.concatenate([lower, upper], axis=1)
    below = jnp.zeros((128 - TABLE_AT - heads, buckets), f32)
    table = jnp.concatenate([jnp.zeros((TABLE_AT, buckets), f32), table, below], axis=0).T
    each, per, ups = width // devices, buckets // devices, usum_ref.shape[1] // devices
    for d in range(devices):
        out_ref[each * d : each * d + per, :] += table[per * d : per * d + per, :]
        out_ref[each * d : each * d + 1, UP_AT : UP_AT + ups] = usum_ref[:, ups * d : ups * d + ups]


def collect_small(core, devices, buckets, vsum, usum, mine, theirs):
    width = vsum.shape[1]
    pairs = mine[1].shape[0]
    args = [vsum, usum, mine[1], theirs[1], mine[0], theirs[0]]
    whole = lambda t: pl.BlockSpec(t.shape, lambda i, core: (0,) * t.ndim)
    return pl.pallas_call(
        partial(collect_kernel, devices, buckets),
        grid_spec=pltpu.PrefetchScalarGridSpec(
            num_scalar_prefetch=1,
            grid=(1,),
            in_specs=[whole(t) for t in args],
            out_specs=pl.BlockSpec((width, 128), lambda i, core: (0, 0)),
            scratch_shapes=[
                pltpu.VMEM((128, width), f32),
                pltpu.VMEM((2, pairs, 2, 128), f32),
                pltpu.VMEM((2, 2 * pairs, ROW_LEN), f32),
            ],
        ),
        out_shape=shape_of((width, 128), f32),
        compiler_params=pltpu.CompilerParams(vmem_limit_bytes=8 * MIB),
        cost_estimate=pl.CostEstimate(flops=10**6, bytes_accessed=MIB, transcendentals=0),
    )(core, *args)


def pack_kernel(core_ref, *refs):
    vectors, (table_ref, up_ref, q_ref, k_ref, v_ref, wo_ref, wu_ref, wd_ref) = refs[:8], refs[8:16]
    outs, (tall, small) = refs[16:22], refs[22:]
    rows = q_ref.shape[0]
    for i, ref in enumerate(vectors):
        tall[i : i + 1, 0:rows] = ref[...]
    small[...] = tall[...].T[0:rows, :]
    lane = lax.broadcasted_iota(jnp.int32, small.shape, 1)
    small[...] = jnp.where(lane < 8, small[...], 0.0)
    per, heads = table_ref.shape
    small[0:per, TABLE_AT : TABLE_AT + heads] = table_ref[...]
    small[0:1, UP_AT : UP_AT + up_ref.shape[1]] = up_ref[...]
    extra = small[...].astype(bf16)
    low = lambda ref, first, last: ref[:, first:last].astype(bf16)
    h, f = wo_ref.shape[1] // 2, wu_ref.shape[1] // 2

    def write(side, square, up, down):
        for g in range(h // 128):
            at = side * h + 128 * g
            for i, ref in enumerate((q_ref, k_ref, v_ref)):
                square[:, 384 * g + 128 * i : 384 * g + 128 * i + 128] = low(ref, at, at + 128)
        square[:, 3 * h : 3 * h + 128] = extra
        up[:, 0:f] = low(wu_ref, side * f, side * f + f)
        up[:, f : f + h] = low(wo_ref, side * h, side * h + h)
        down[...] = low(wd_ref, side * h, side * h + h)

    @pl.when(core_ref[0] == 0)
    def _():
        write(0, *outs[0:3])
        write(1, *outs[3:6])

    @pl.when(core_ref[0] == 1)
    def _():
        write(1, *outs[0:3])
        write(0, *outs[3:6])


def pack(core, vectors, table, up, matrices):
    rows, width = matrices[0].shape
    args = [t.reshape(1, -1) for t in vectors] + [table, up.reshape(1, -1), *matrices]
    whole = lambda s: pl.BlockSpec(s, lambda i, core: (0, 0))
    shapes = [
        (rows, 3 * width // 2 + 128),
        (rows, (matrices[4].shape[1] + width) // 2),
        (matrices[5].shape[0], width // 2),
    ] * 2
    return pl.pallas_call(
        pack_kernel,
        grid_spec=pltpu.PrefetchScalarGridSpec(
            num_scalar_prefetch=1,
            grid=(1,),
            in_specs=[whole(t.shape) for t in args],
            out_specs=[whole(s) for s in shapes],
            scratch_shapes=[pltpu.VMEM((128, 128), f32), pltpu.VMEM((rows, 128), f32)],
        ),
        out_shape=[shape_of(s, bf16) for s in shapes],
        compiler_params=pltpu.CompilerParams(vmem_limit_bytes=60 * MIB),
        cost_estimate=pl.CostEstimate(flops=10**6, bytes_accessed=2 * MIB, transcendentals=0),
    )(core, *args)


class Links:
    def __init__(self, mesh):
        wide, narrow = mesh.shape[WIDE], mesh.shape[NARROW]
        self.sizes = (wide // 2, 2, narrow // 2, 2)
        w, n = lax.axis_index(WIDE), lax.axis_index(NARROW)
        self.place = (w // 2, w % 2, n // 2, n % 2)
        self.core = self.place[CORE]
        self.chips = wide * narrow // 2

    def number(self, at):
        return ((at[Z] * self.sizes[X] + at[X]) * self.sizes[Y] + at[Y]) * 2 + at[CORE]

    def fetch(self, value, axis, step):
        pairs = []
        for z in range(self.sizes[Z]):
            for x in range(self.sizes[X]):
                for y in range(self.sizes[Y]):
                    for c in range(2):
                        here = (z, x, y, c)
                        there = list(here)
                        there[axis] = (there[axis] + step) % self.sizes[axis]
                        pairs.append((self.number(there), self.number(here)))
        return lax.ppermute(value, AXES, pairs)

    def others(self, value, axis):
        return [self.fetch(value, axis, k) for k in range(1, self.sizes[axis])]

    def swapped(self, kept, sent):
        even = self.core == 0
        got = self.fetch(sent, CORE, 1)
        return jnp.where(even, kept, got), jnp.where(even, got, kept)

    def order(self):
        chip = jnp.arange(self.chips, dtype=jnp.int32)
        sz, sx, sy = self.sizes[:3]
        kz = (chip // (sx * sy) - self.place[Z]) % sz
        kx = (chip // sy - self.place[X]) % sx
        ky = (chip - self.place[Y]) % sy
        plane = 2 * ((kz * sy + ky) * sx + kx)
        return jnp.concatenate(
            [
                (ky * sx + kx) * sz + kz,
                (kx * sy + ky) * sz + kz,
                self.core.reshape(1),
                plane,
                plane + 1,
            ]
        ).astype(jnp.int32)

    def finish(self, total):
        rows = total.shape[0] // 2
        even = self.core == 0
        own = jnp.where(even, total[:rows], total[rows:])
        return own, self.fetch(jnp.where(even, total[rows:], total[:rows]), CORE, 1)


def ring(me, k, size):
    at = me + k
    return jnp.where(at >= size, at - size, at)


def fold_1_kernel(halves, sizes, count, place_ref, *refs):
    kept, got, outs = refs[:count], refs[count : 2 * count], refs[2 * count :]
    split = sizes[Y]
    a_outs, b_outs = outs[:split], outs[split:]

    def write(out, at, half, x, y):
        rows, column = out.shape[2], 0
        for piece, part, first, last in half:
            source = (0, x, y, part, slice(None), slice(first, last))
            value = kept[piece][source] + got[piece][source].astype(f32)
            for row in range(0, value.shape[0], rows):
                some = value[row : row + rows, :].astype(out.dtype)
                out[0, at, :, column : column + last - first] = some
                column += last - first

    for k, out in enumerate(a_outs):
        y = ring(place_ref[Y], k, sizes[Y])
        for x in range(sizes[X]):
            write(out, x, halves[0], x, y)
    for k, out in enumerate(b_outs):
        x = ring(place_ref[X], k, sizes[X])
        for y in range(sizes[Y]):
            write(out, y, halves[1], x, y)


def fold_2_kernel(sizes, place_ref, *refs):
    sy, sx = sizes[Y], sizes[X]
    a_in, b_in, outs = refs[:sy], refs[sy : sy + sx], refs[sy + sx :]
    a_outs, b_outs = outs[:sx], outs[sx:]

    def value(ins, at):
        total = ins[0][0, at]
        for piece in ins[1:]:
            total = total + piece[0, at].astype(f32)
        return total

    for k, out in enumerate(a_outs):
        out[0] = value(a_in, ring(place_ref[X], k, sx)).astype(out.dtype)
    for k, out in enumerate(b_outs):
        out[0] = value(b_in, ring(place_ref[Y], k, sy)).astype(out.dtype)


def fold_3_kernel(sizes, place_ref, *refs):
    sy, sx = sizes[Y], sizes[X]
    a_in, b_in, outs = refs[:sx], refs[sx : sx + sy], refs[sx + sy :]
    rows, columns = a_in[0].shape[1:]
    for k, out in enumerate(outs):
        z = ring(place_ref[Z], k, sizes[Z])
        for n, ins in enumerate((a_in, b_in)):
            total = ins[0][z]
            for piece in ins[1:]:
                total = total + piece[z].astype(f32)
            first = n * columns
            out[0, :, first : first + total.shape[1]] = total.astype(out.dtype)


def fold_call(kernel, place, ins, outs, steps):
    block = lambda s: pl.BlockSpec((s[0] // steps,) + tuple(s[1:]), lambda i, place: (i,) + (0,) * (len(s) - 1))
    return pl.pallas_call(
        kernel,
        grid_spec=pltpu.PrefetchScalarGridSpec(
            num_scalar_prefetch=1,
            grid=(steps,),
            in_specs=[block(t.shape) for t in ins],
            out_specs=[block(s) for s, _ in outs],
        ),
        out_shape=[shape_of(s, t) for s, t in outs],
        compiler_params=pltpu.CompilerParams(vmem_limit_bytes=24 * MIB),
        cost_estimate=pl.CostEstimate(flops=10**6, bytes_accessed=8 * MIB, transcendentals=0),
    )(place, *ins)


class Fold:
    def __init__(self, links, halves):
        self.links, self.halves = links, halves
        self.place = jnp.stack(links.place).astype(jnp.int32)

    def to_others(self, values, axis):
        size = self.links.sizes[axis]
        return [self.links.fetch(v, axis, size - k) for k, v in enumerate(values) if k]

    def first(self, kept, got):
        sizes = self.links.sizes
        sz, sx, sy = sizes[:3]
        rows = kept[0].shape[4]
        wide = [sum((e[3] - e[2]) * kept[e[0]].shape[4] // rows for e in half) for half in self.halves]
        kinds = lambda shape, n: [(shape, f32)] + [(shape, bf16)] * (n - 1)
        outs = kinds((sz, sx, rows, wide[0]), sy) + kinds((sz, sy, rows, wide[1]), sx)
        done = fold_call(partial(fold_1_kernel, self.halves, sizes, len(kept)), self.place, [*kept, *got], outs, sz)
        a, b = done[:sy], done[sy:]
        return [a[0], b[0]], self.to_others(a, Y), self.to_others(b, X)

    def second(self, own, got_y, got_x):
        sizes = self.links.sizes
        sz, sx, sy = sizes[:3]
        kinds = lambda t, n: [((sz,) + t.shape[2:], f32)] + [((sz,) + t.shape[2:], bf16)] * (n - 1)
        outs = kinds(own[0], sx) + kinds(own[1], sy)
        done = fold_call(partial(fold_2_kernel, sizes), self.place, [own[0], *got_y, own[1], *got_x], outs, sz)
        a, b = done[:sx], done[sx:]
        return [[a[0], b[0]], self.to_others(a, X), self.to_others(b, Y)]

    def third(self, own, got_x, got_y):
        sizes = self.links.sizes
        rows, ca = own[0].shape[1:]
        shape = (1, rows, ca + own[1].shape[2])
        outs = [(shape, f32)] + [(shape, bf16)] * (sizes[Z] - 1)
        ins = [own[0], *got_x, own[1], *got_y]
        done = fold_call(partial(fold_3_kernel, sizes), self.place, ins, outs, 1)
        return done[0], self.to_others(done, Z)

    def last(self, own, got):
        for piece in got:
            own = own + piece.astype(f32)
        return own[0]


def last_kernel(heads, core_ref, own_ref, *refs):
    pieces, outs = refs[: -(2 + 8 + 2)], refs[-(2 + 8 + 2) :]
    keep_ref, send_ref, vectors, table_ref, up_ref = outs[0], outs[1], outs[2:10], outs[10], outs[11]
    rows, width = keep_ref.shape
    total = own_ref[0]
    for piece in pieces:
        total = total + piece[0].astype(f32)

    def write(own, other):
        keep_ref[...] = own[:, 0:width]
        send_ref[...] = other[:, 0:width]
        small = own[:, width:]
        table_ref[...] = small[0 : table_ref.shape[0], TABLE_AT : TABLE_AT + heads]
        up_ref[...] = small[0:1, UP_AT : UP_AT + up_ref.shape[1]]
        turned = jnp.concatenate([small, jnp.zeros((128 - rows, 128), f32)], axis=0).T
        for i, ref in enumerate(vectors):
            ref[...] = turned[i : i + 1, 0:rows]

    @pl.when(core_ref[0] == 0)
    def _():
        write(total[:rows], total[rows:])

    @pl.when(core_ref[0] == 1)
    def _():
        write(total[rows:], total[:rows])


def join_kernel(core_ref, keep_ref, got_ref, *outs):
    def write(sides):
        for s, side in enumerate(sides):
            for g in range(side.shape[1] // 384):
                at = s * (side.shape[1] // 3) + 128 * g
                for i, out in enumerate(outs):
                    out[:, at : at + 128] = side[:, 384 * g + 128 * i : 384 * g + 128 * i + 128]

    @pl.when(core_ref[0] == 0)
    def _():
        write((keep_ref, got_ref))

    @pl.when(core_ref[0] == 1)
    def _():
        write((got_ref, keep_ref))


def join_wide_kernel(core_ref, keep_ref, got_ref, down_keep_ref, down_got_ref, out_ref, up_ref, down_ref):
    h, f = out_ref.shape[1] // 2, up_ref.shape[1] // 2

    def write(sides, downs):
        for s in range(2):
            up_ref[:, s * f : s * f + f] = sides[s][:, 0:f]
            out_ref[:, s * h : s * h + h] = sides[s][:, f : f + h]
            down_ref[:, s * h : s * h + h] = downs[s][...]

    @pl.when(core_ref[0] == 0)
    def _():
        write((keep_ref, got_ref), (down_keep_ref, down_got_ref))

    @pl.when(core_ref[0] == 1)
    def _():
        write((got_ref, keep_ref), (down_got_ref, down_keep_ref))


def whole_call(kernel, core, ins, outs):
    whole = lambda s: pl.BlockSpec(s, lambda i, core: (0,) * len(s))
    return pl.pallas_call(
        kernel,
        grid_spec=pltpu.PrefetchScalarGridSpec(
            num_scalar_prefetch=1,
            grid=(1,),
            in_specs=[whole(t.shape) for t in ins],
            out_specs=[whole(s) for s in outs],
        ),
        out_shape=[shape_of(s, f32) for s in outs],
        compiler_params=pltpu.CompilerParams(vmem_limit_bytes=16 * MIB),
        cost_estimate=pl.CostEstimate(flops=10**6, bytes_accessed=2 * MIB, transcendentals=0),
    )(core, *ins)


def segments(lengths):
    place = jnp.arange(ROW_LEN, dtype=jnp.int32)
    ending = jnp.cumsum(lengths, axis=1)
    return jnp.sum((place[None, :, None] >= ending[:, None, :]).astype(jnp.int32), axis=2)


def per_device(
    mesh, tokens, cotangent, pair_lengths, w_query, w_key, w_value, w_output, w_up, w_down, b_query, b_value,
    b_output, b_up, b_down, first_gain, first_shift, second_gain, second_shift, bucket_bias,
):
    links = Links(mesh)
    devices = 2 * links.chips
    rows, width = w_query.shape
    hidden = w_up.shape[1]
    heads = bucket_bias.shape[1]
    buckets = bucket_bias.shape[0] * devices
    w_half, h_half = width // 2, hidden // 2
    low = lambda t: t.astype(bf16)
    barrier = lax.optimization_barrier
    core = links.core
    even = core == 0
    order = links.order()
    blocks = lambda a, b: [a, b]
    deep = square_blocks = lambda t: t
    if (2 * rows) % 16 or w_down.shape[0] % 16:
        found, order = order, jnp.concatenate([jnp.zeros((2,), jnp.int32), core.reshape(1), jnp.arange(2, dtype=jnp.int32)])
        n = links.chips
        sort = lambda t, first: jnp.take(t, found[first : first + n], axis=0)

        def blocks(a, b):
            return [t.reshape(1, -1, t.shape[2]) for t in (sort(a, 0), sort(b, n))]

        def square_blocks(t):
            return jnp.stack([sort(t[:n], 0), sort(t[n:], n)]).reshape(2, -1, t.shape[2])

        def deep(t):
            both = jnp.stack([sort(t, 2 * n + 1), sort(t, 3 * n + 1)], axis=1)
            return both.reshape(2, -1, t.shape[2])

    half = 3 * w_half
    cut = (half + 128) // 2
    up_cut = (h_half + w_half + 128) // 256 * 128
    packed = pack(
        core.reshape(1),
        [b_query, b_value, b_output, b_down, first_gain, first_shift, second_gain, second_shift],
        bucket_bias,
        b_up,
        [w_query, w_key, w_value, w_output, w_up, w_down],
    )
    swapped = lambda i: jnp.concatenate(links.swapped(packed[i], packed[i + 3]), axis=0)
    pair = swapped(0)
    pair_z = links.others(pair, Z)
    up_pair = swapped(1)
    down_pair = jnp.stack(links.swapped(packed[2], packed[5]))
    down_x = links.others(down_pair, X)

    def together(*groups):
        sizes = [len(g) for g in groups]
        flat = barrier(tuple(t for g in groups for t in g))
        out = []
        for size in sizes:
            out.append(list(flat[:size]))
            flat = flat[size:]
        return out

    def spans(*groups):
        leaves, tree = jax.tree.flatten(tuple(groups))
        return jax.tree.unflatten(tree, barrier(tuple(leaves)))

    def chips(value, got):
        value = jnp.stack([value] + got)
        return value.reshape((-1,) + value.shape[-2:])

    def plane_1(value, cut):
        return [value[:, :, :cut], value[:, :, cut:]], links.others(value[:, :, :cut], X), links.others(value[:, :, cut:], Y)

    def plane_2(ab, got_x, got_y):
        ab = [chips(ab[0], got_x), chips(ab[1], got_y)]
        return ab, links.others(ab[0], Y), links.others(ab[1], X)

    def plane_3(ab, got_y, got_x):
        return chips(ab[0], got_y), chips(ab[1], got_x)

    pair_z, (pair, up_pair), down_x = together(pair_z, (pair, up_pair), down_x)
    stage = plane_1(jnp.stack([pair] + pair_z), cut)
    down_pair = jnp.stack([down_pair] + down_x)
    down_y = links.others(down_pair, Y)
    up_z = links.others(up_pair, Z)
    got_x, got_y, down_y, up_z, (up_pair,) = together(*stage[1:], down_y, up_z, (up_pair,))
    stage = plane_2(stage[0], got_x, got_y)
    down_own = jnp.stack([down_pair] + down_y)
    down_z = links.others(down_own, Z)
    got_y, got_x, up_z, down_z[-1:] = together(*stage[1:], up_z, down_z[-1:])
    mine = jnp.concatenate(plane_3(stage[0], got_y, got_x), axis=0)

    theirs = links.fetch(mine, CORE, 1)
    mine, theirs = square_blocks(mine), square_blocks(theirs)
    lines, vectors, up_bias, bias = spread_small(order, mine, devices, width, heads, buckets, hidden)
    segment = segments(pair_lengths)
    segc, segr = segment[:, :, None], segment[:, None, :]
    pairs = heads // 4
    first_m, first_t = (core * pairs).reshape(1), ((1 - core) * pairs).reshape(1)
    qkv_m = project(order, False, tokens, bias, mine)
    up_z, (qkv_m, bias_t, theirs) = together(up_z, (qkv_m, bias, theirs))
    up_stage = plane_1(jnp.stack([up_pair] + up_z), up_cut)
    o_m, p_m = attend_forward(first_m, lines, segc, segr, qkv_m)
    (o_m, theirs), got_x, got_y = together((o_m, theirs), up_stage[1], up_stage[2])

    up_stage = plane_2(up_stage[0], got_x, got_y)
    qkv_t = project(order, True, tokens, bias_t, theirs)
    o_t, p_t = attend_forward(first_t, lines, segc, segr, qkv_t)
    (o_m, o_t), got_y, got_x = together((o_m, o_t), *up_stage[1:])
    up_a, up_b = plane_3(up_stage[0], got_y, got_x)
    up_theirs = (links.fetch(up_a, CORE, 1), links.fetch(up_b, CORE, 1))
    up_a, up_b, *down_z = barrier((up_a, up_b, *down_z))
    down_mine = jnp.stack([down_own] + down_z)
    down_mine = down_mine.reshape((-1,) + down_mine.shape[-2:])
    down_theirs = links.fetch(down_mine, CORE, 1)

    result, dh1, settled, active, do_m, do_t, dy1_m, dy1_t, dy2_m, dy2_t, dz_m, dz_t, vsum, usum = middle(
        order,
        o_m,
        o_t,
        tokens,
        cotangent,
        vectors,
        up_bias,
        blocks(up_a, up_b) + blocks(*up_theirs),
        [deep(down_mine), deep(down_theirs)],
    )

    def pieces(t, parts=1):
        return t.reshape(links.sizes[:3] + (parts, -1, t.shape[1]))

    exchange = lambda *values: [links.fetch(low(t), CORE, 1) for t in values]
    o_both = jnp.where(even, jnp.concatenate([o_m, o_t], axis=1), jnp.concatenate([o_t, o_m], axis=1))
    outs = [dot(o_both, t, TN) for t in (dy1_t, dy1_m)]
    outs, (dz_t, dz_m, settled) = together(outs, (dz_t, dz_m, settled))
    up_parts = lambda dz, out: [pieces(dot(settled, dz, TN)), pieces(out)]
    wide_fold = Fold(
        links,
        [
            [(0, 0, 0, up_cut), (2, 0, 0, w_half)],
            [(0, 0, up_cut, h_half), (1, 0, 0, w_half), (2, 1, 0, w_half)],
        ],
    )
    square_fold = Fold(links, [[(0, 0, 0, cut)], [(0, 0, cut, half), (1, 0, 0, 128)]])

    got = exchange(*up_parts(dz_t, outs[0]))
    kept = up_parts(dz_m, outs[1])
    got, kept, (dy2_t, dy2_m) = spans(got, kept, (dy2_t, dy2_m))
    got += exchange(pieces(dot(active, dy2_t, TN), 2))
    kept += [pieces(dot(active, dy2_m, TN), 2)]
    got, kept, (do_t, do_m) = spans(got, kept, (do_t, do_m))

    wide = wide_fold.first(kept, got)
    grads_t, grads_m = attend_backward((qkv_t, do_t, o_t, p_t), (qkv_m, do_m, o_m, p_m))
    wide, grads_t, grads_m = spans(wide, grads_t, grads_m)

    wide = wide_fold.second(*wide)
    wide[0], grads_t, grads_m = spans(wide[0], grads_t, grads_m)
    square_got = exchange(pieces(dot(tokens, grads_t[0], TN)))
    g_small = pieces(collect_small(core.reshape(1), devices, buckets, vsum, usum, grads_m[1:], grads_t[1:]))
    square_got += exchange(g_small)
    square_kept = [pieces(dot(tokens, grads_m[0], TN)), g_small]
    wide, square_kept, square_got, (d_m, d_t) = spans(wide, square_kept, square_got, (grads_m[0], grads_t[0]))

    square = square_fold.first(square_kept, square_got)
    wide_own, wide_got = wide_fold.third(*wide)
    grad_tokens = token_gradient(order, dh1, d_m, d_t, [mine, theirs])
    square, grad_tokens = spans(square, grad_tokens)

    square = square_fold.second(*square)
    square = spans(square)[0]
    square_own, square_z = square_fold.third(*square)
    wide_got, square_own = spans(wide_got, square_own)
    wide_total = wide_fold.last(wide_own, wide_got)
    wide_a = up_cut + 2 * w_half
    up_total = jnp.concatenate([wide_total[:, :up_cut], wide_total[:, wide_a : wide_a + h_half + w_half - up_cut]], axis=1)
    groups = w_down.shape[0] // (2 * rows)
    down_total = jnp.stack(
        [
            jnp.concatenate([wide_total[:, first + w_half * i : first + w_half * (i + 1)] for i in range(groups)], axis=0)
            for first in (up_cut, wide_total.shape[1] - groups * w_half)
        ]
    ).reshape(-1, w_half)

    core_1 = core.reshape(1)
    out_output, out_up, out_down = whole_call(
        join_wide_kernel,
        core_1,
        [*links.finish(up_total), *links.finish(down_total)],
        [(rows, width), (rows, hidden), w_down.shape],
    )
    shapes = [(rows, half)] * 2 + [(1, rows)] * 8 + [bucket_bias.shape, (1, b_up.shape[0])]
    own, other, *flat = whole_call(partial(last_kernel, heads), core_1, [square_own, *square_z], shapes)
    *flat, out_table, out_b_up = flat
    flat = [t.reshape(-1) for t in flat]
    out_query, out_key, out_value = whole_call(
        join_kernel, core_1, [own, links.fetch(other, CORE, 1)], [(rows, width)] * 3
    )
    return (
        result,
        grad_tokens,
        out_query,
        out_key,
        out_value,
        out_output,
        out_up,
        out_down,
        flat[0],
        flat[1],
        flat[2],
        out_b_up.reshape(-1),
        flat[3],
        flat[4],
        flat[5],
        flat[6],
        flat[7],
        out_table,
    )


def solution(mesh):
    split, line = P(AXES, None), P(AXES)
    return jax.shard_map(
        partial(per_device, mesh),
        mesh=mesh,
        in_specs=(split,) * 9 + (line,) * 9 + (split,),
        out_specs=(split,) * 8 + (line,) * 9 + (split,),
        check_vma=False,
    )
```

```python
from functools import partial
import math

import jax
import jax.numpy as jnp
from jax import lax
from jax.experimental import pallas as pl
from jax.experimental.pallas import tpu as pltpu
from jax.sharding import PartitionSpec as P

WIDE, NARROW = "wide", "narrow"
AXES = (WIDE, NARROW)
Z, X, Y, CORE = range(4)
ROW_LEN = 512
MIB = 1 << 20
bf16, f32 = jnp.bfloat16, jnp.float32
NN = (((1,), (0,)), ((), ()))
NT = (((1,), (1,)), ((), ()))
TN = (((0,), (0,)), ((), ()))


def dot(left, right, dims=NN):
    return lax.dot_general(left, right, dims, preferred_element_type=f32)


def shape_of(shape, dtype):
    return jax.ShapeDtypeStruct(shape, dtype)


def toeplitz(line, ref, head):
    base = jnp.concatenate([pltpu.roll(line, s, 1) if s else line for s in range(8)], axis=0)
    for c in range(16):
        turned = pltpu.roll(base, 8 * c, 1) if c else base
        for b in range(ROW_LEN // 128):
            cut = ROW_LEN - 128 * b
            piece = jnp.concatenate([turned[:, cut:], turned[:, :cut]], axis=1) if b else turned
            first = 128 * b + 8 * c
            ref[head, first : first + 8, :] = piece


def diagonals(ref, head):
    total = None
    for c in range(16):
        turned = None
        for b in range(ROW_LEN // 128):
            first = 128 * b + 8 * c
            piece = ref[head, first : first + 8, :]
            if b:
                piece = jnp.concatenate([piece[:, 128 * b :], piece[:, : 128 * b]], axis=1)
            turned = piece if turned is None else turned + piece
        if c:
            turned = pltpu.roll(turned, ROW_LEN - 8 * c, 1)
        total = turned if total is None else total + turned
    out = total[0:1]
    for s in range(1, 8):
        out = out + pltpu.roll(total[s : s + 1], ROW_LEN - s, 1)
    return out


def forward_kernel(first_ref, line_ref, segc_ref, segr_ref, qkv_ref, *refs):
    o_ref, p_ref, bias, mask = refs[-4:]
    g, r = pl.program_id(0), pl.program_id(1)

    @pl.when(g == 0)
    def _():
        mask[r] = jnp.where(segc_ref[0] == segr_ref[0], 0.0, -1e30)

    @pl.when(r == 0)
    def _():
        for h in range(2):
            toeplitz(line_ref[0, h : h + 1, :], bias, h)

    q, k, v = qkv_ref[:, 0:128], qkv_ref[:, 128:256], qkv_ref[:, 256:384]
    lane = lax.broadcasted_iota(jnp.int32, (ROW_LEN, 128), 1)
    outs = []
    for h in range(2):
        mine = (lane < 64) if h == 0 else (lane >= 64)
        qh = jnp.where(mine, q.astype(f32) * 0.125, 0.0).astype(bf16)
        s = dot(qh, k, NT) + bias[h] + mask[r]
        e = jnp.exp(s - jnp.max(s, axis=1, keepdims=True))
        p = (e * (1.0 / jnp.sum(e, axis=1, keepdims=True))).astype(bf16)
        p_ref[0, h] = p
        outs.append(dot(p, v))
    o_ref[...] = jnp.where(lane < 64, outs[0], outs[1]).astype(bf16)


def attend_forward(first, lines, segc, segr, qkv, after=()):
    pairs, rows = qkv.shape[1] // 384, segc.shape[0]
    return pl.pallas_call(
        forward_kernel,
        grid_spec=pltpu.PrefetchScalarGridSpec(
            num_scalar_prefetch=1,
            grid=(pairs, rows),
            in_specs=[
                pl.BlockSpec((1, 2, ROW_LEN), lambda g, r, first: (g + first[0], 0, 0)),
                pl.BlockSpec((1, ROW_LEN, 1), lambda g, r, first: (r, 0, 0)),
                pl.BlockSpec((1, 1, ROW_LEN), lambda g, r, first: (r, 0, 0)),
                pl.BlockSpec((ROW_LEN, 384), lambda g, r, first: (r, g)),
            ]
            + [pl.BlockSpec(memory_space=pl.ANY)] * len(after),
            out_specs=[
                pl.BlockSpec((ROW_LEN, 128), lambda g, r, first: (r, g)),
                pl.BlockSpec((1, 2, ROW_LEN, ROW_LEN), lambda g, r, first: (r, g, 0, 0)),
            ],
            scratch_shapes=[pltpu.VMEM((2, ROW_LEN, ROW_LEN), f32), pltpu.VMEM((rows, ROW_LEN, ROW_LEN), f32)],
        ),
        out_shape=[
            shape_of((rows * ROW_LEN, 128 * pairs), bf16),
            shape_of((rows, 2 * pairs, ROW_LEN, ROW_LEN), bf16),
        ],
        compiler_params=pltpu.CompilerParams(vmem_limit_bytes=44 * MIB),
        cost_estimate=pl.CostEstimate(flops=pairs * rows * 2 * 10**9, bytes_accessed=pairs * rows * 2 * MIB, transcendentals=0),
    )(first, lines, segc, segr, qkv, *after)


def backward_kernel(*refs):
    ins, outs, acc = (refs[0:4], refs[4:8]), (refs[-7:-4], refs[-4:-1]), refs[-1]
    for side in range(2):

        @pl.when(pl.program_id(0) == side)
        def _():
            backward_step(*ins[side], *outs[side], acc)


def backward_step(qkv_ref, do_ref, o_ref, p_ref, d_ref, line_ref, sums_ref, acc):
    r, last = pl.program_id(2), pl.num_programs(2) - 1
    q, k, v = qkv_ref[:, 0:128], qkv_ref[:, 128:256], qkv_ref[:, 256:384]
    lane = lax.broadcasted_iota(jnp.int32, (ROW_LEN, 128), 1)
    qt = (q.astype(f32) * 0.125).T.astype(bf16)
    do = do_ref[...].astype(f32)
    dot_t = do.T.astype(bf16)
    prod = do * o_ref[...].astype(f32)
    dqs, dks, dvs = [], [], []
    for h in range(2):
        mine = (lane < 64) if h == 0 else (lane >= 64)
        doh = jnp.where(mine, do, 0.0).astype(bf16)
        delta = jnp.sum(jnp.where(mine, prod, 0.0), axis=1, keepdims=True)
        p = p_ref[0, h]
        ds = p.astype(f32) * (dot(doh, v, NT) - delta)

        @pl.when(r == 0)
        def _():
            acc[h] = ds

        @pl.when(r > 0)
        def _():
            acc[h] += ds

        dsb = ds.astype(bf16)
        half = slice(64 * h, 64 * h + 64)
        dqs.append(dot(dsb, k))
        dks.append(dot(qt[half, :], dsb))
        dvs.append(dot(dot_t[half, :], p))
    dq = jnp.where(lane < 64, dqs[0], dqs[1]) * 0.125
    dk = jnp.concatenate(dks, axis=0).T
    dv = jnp.concatenate(dvs, axis=0).T
    d_ref[:, 0:128] = dq.astype(bf16)
    d_ref[:, 128:256] = dk.astype(bf16)
    d_ref[:, 256:384] = dv.astype(bf16)
    sums = jnp.concatenate([jnp.sum(dq, axis=0, keepdims=True), jnp.sum(dv, axis=0, keepdims=True)], axis=0)

    @pl.when(r == 0)
    def _():
        sums_ref[0] = sums

    @pl.when(r > 0)
    def _():
        sums_ref[0] += sums

    @pl.when(r == last)
    def _():
        for h in range(2):
            line_ref[0, h : h + 1, :] = diagonals(acc, h)


def attend_backward(first, second, after=()):
    rows, pairs = first[3].shape[0], first[0].shape[1] // 384
    ends = ((0, 0), (pairs - 1, rows - 1))

    def block(shape, at, side):
        def index(s, g, r):
            mine = s == side
            return at(jnp.where(mine, g, ends[1 - side][0]), jnp.where(mine, r, ends[1 - side][1]))

        return pl.BlockSpec(shape, index)

    both = lambda shape, at: [block(shape, at, side) for side in range(2)]
    by_row, by_pair = lambda g, r: (r, g), lambda g, r: (g, 0, 0)
    wide, half = both((ROW_LEN, 384), by_row), both((ROW_LEN, 128), by_row)
    probs = both((1, 2, ROW_LEN, ROW_LEN), lambda g, r: (r, g, 0, 0))
    lines, sums = both((1, 2, ROW_LEN), by_pair), both((1, 2, 128), by_pair)
    shapes = [
        shape_of((rows * ROW_LEN, 384 * pairs), bf16),
        shape_of((pairs, 2, ROW_LEN), f32),
        shape_of((pairs, 2, 128), f32),
    ]
    done = pl.pallas_call(
        backward_kernel,
        grid=(2, pairs, rows),
        in_specs=[spec for i in range(2) for spec in (wide[i], half[i], half[i], probs[i])]
        + [pl.BlockSpec(memory_space=pl.ANY)] * len(after),
        out_specs=[spec for i in range(2) for spec in (wide[i], lines[i], sums[i])],
        out_shape=shapes * 2,
        scratch_shapes=[pltpu.VMEM((2, ROW_LEN, ROW_LEN), f32)],
        compiler_params=pltpu.CompilerParams(vmem_limit_bytes=50 * MIB),
        cost_estimate=pl.CostEstimate(flops=pairs * rows * 4 * 10**9, bytes_accessed=pairs * rows * 4 * MIB, transcendentals=0),
    )(*first, *second, *after)
    return done[:3], done[3:]


def normalize(value, gain, shift):
    center = value - jnp.mean(value, axis=1, keepdims=True)
    inverse = lax.rsqrt(jnp.mean(center * center, axis=1, keepdims=True) + 1e-5)
    normed = center * inverse
    return normed, inverse, normed * gain + shift


def normalize_back(upstream, normed, inverse, gain):
    scaled = upstream * gain
    return inverse * (
        scaled
        - jnp.mean(scaled, axis=1, keepdims=True)
        - normed * jnp.mean(scaled * normed, axis=1, keepdims=True)
    )


def column_sum(value):
    return jnp.sum(value, axis=0, keepdims=True)


def middle_kernel(
    blocks, order_ref,
    om_ref, ot_ref, x_ref, c_ref, vec_ref, bu_ref, uma_ref, umb_ref, uta_ref, utb_ref, dm_ref, dt_ref,
    *refs,
):
    (
        out_ref, dh1_ref, a_ref, g_ref, dom_ref, dot_ref, dy1m_ref, dy1t_ref, dy2m_ref, dy2t_ref, dzm_ref, dzt_ref,
        vsum_ref, usum_ref, wo, wu, wd, slope, dy, sems,
    ) = refs[-20:]
    step = pl.program_id(0)
    width, hidden = wu.shape
    core = order_ref[2 * blocks]
    w_half, h_half = width // 2, hidden // 2

    def cols(size, side, first=0, count=None):
        return pl.ds(pl.multiple_of(side * size + first, 128), size if count is None else count)

    up_left = uma_ref.shape[2]
    up_right = h_half - up_left
    rows, deep = uma_ref.shape[1], dm_ref.shape[1]
    sides = ((core, uma_ref, umb_ref, dm_ref), (1 - core, uta_ref, utb_ref, dt_ref))

    def out_moves(k):
        j, at = order_ref[blocks + k], place(k, rows)
        return [(ub.at[j, :, up_right : up_right + w_half], wo.at[at, cols(w_half, s)]) for s, ua, ub, d in sides]

    def up_moves(k):
        i, j, at = order_ref[k], order_ref[blocks + k], place(k, rows)
        first = [(ua.at[i], wu.at[at, cols(h_half, s, 0, up_left)]) for s, ua, ub, d in sides]
        second = [(ub.at[j, :, 0:up_right], wu.at[at, cols(h_half, s, up_left, up_right)]) for s, ua, ub, d in sides]
        return first + second

    def down_moves(k):
        found = []
        for n in range(2):
            i, at = order_ref[(2 + n) * blocks + 1 + k], place(2 * k + n, deep)
            found += [(d.at[i], wd.at[at, cols(w_half, s)]) for s, ua, ub, d in sides]
        return found

    groups = ((out_moves, 0), (up_moves, 2), (down_moves, 6))

    @pl.when(step == 0)
    def _():
        for moves, first in groups:
            copies(moves, sems, blocks, first, wait=False)

    def ready(group):
        @pl.when(step == 0)
        def _():
            copies(groups[group][0], sems, blocks, groups[group][1], start=False)

    ready(0)
    rows_of = lambda side: cols(w_half, side)
    b_out, b_down, gain1, shift1, gain2, shift2 = [vec_ref[i : i + 1, :] for i in range(2, 8)]
    first = x_ref[...].astype(f32) + dot(om_ref[...], wo[rows_of(core), :]) + dot(ot_ref[...], wo[rows_of(1 - core), :]) + b_out
    n1, r1, a = normalize(first, gain1, shift1)
    ab = a.astype(bf16)
    a_ref[...] = ab
    second = a + b_down
    chunk = h_half // 2
    ready(1)
    for f in range(0, hidden, chunk):
        at = slice(f, f + chunk)
        z = dot(ab, wu[:, at]) + bu_ref[:, at]
        mass = 0.5 * (1.0 + lax.erf(z * (1.0 / math.sqrt(2.0))))
        slope[:, at] = mass + z * jnp.exp(-0.5 * z * z) * (1.0 / math.sqrt(2.0 * math.pi))
        active = (z * mass).astype(bf16)
        g_ref[:, at] = active
        if f == 0:
            ready(2)
        second = second + dot(active, wd[at, :])
    n2, r2, out = normalize(second, gain2, shift2)
    out_ref[...] = out.astype(bf16)
    c = c_ref[...].astype(f32)
    dh2 = normalize_back(c, n2, r2, gain2)
    dy2 = dh2.astype(bf16)
    dy[...] = dy2
    dy2m_ref[...] = dy[:, cols(w_half, core)]
    dy2t_ref[...] = dy[:, cols(w_half, 1 - core)]
    da = dh2
    parts = []
    for side, dz_ref in ((core, dzm_ref), (1 - core, dzt_ref)):
        for f in range(0, h_half, chunk):
            at = cols(h_half, side, f, chunk)
            dz = dot(dy2, wd[at, :], NT) * slope[:, at]
            parts.append((at, column_sum(dz)))
            dzb = dz.astype(bf16)
            dz_ref[:, f : f + chunk] = dzb
            da = da + dot(dzb, wu[:, at], NT)
    dh1 = normalize_back(da, n1, r1, gain1)
    dh1_ref[...] = dh1
    dy1 = dh1.astype(bf16)
    dy[...] = dy1
    dy1m_ref[...] = dy[:, cols(w_half, core)]
    dy1t_ref[...] = dy[:, cols(w_half, 1 - core)]
    dom_ref[...] = dot(dy1, wo[rows_of(core), :], NT).astype(bf16)
    dot_ref[...] = dot(dy1, wo[rows_of(1 - core), :], NT).astype(bf16)
    sums = [column_sum(t) for t in (dh1, dh2, da * n1, da, c * n2, c)]
    vsum = jnp.concatenate(sums + [jnp.zeros((2, c.shape[1]), f32)], axis=0)

    @pl.when(step == 0)
    def _():
        vsum_ref[...] = vsum
        for at, part in parts:
            usum_ref[:, at] = part

    @pl.when(step > 0)
    def _():
        vsum_ref[...] += vsum
        for at, part in parts:
            usum_ref[:, at] += part


def middle(order, om, ot, x, c, vec, bu, up, down, after=(), block=256):
    tokens, width = x.shape
    hidden = bu.shape[1]
    blocks = up[0].shape[0]
    by_token = lambda n: pl.BlockSpec((block, n), lambda i, order: (i, 0))
    fixed = lambda s: pl.BlockSpec(s, lambda i, order: (0, 0))
    half, h_half = width // 2, hidden // 2
    outs = [(width, bf16), (width, f32), (width, bf16), (hidden, bf16)] + [(half, bf16)] * 6 + [(h_half, bf16)] * 2
    return pl.pallas_call(
        partial(middle_kernel, blocks),
        grid_spec=pltpu.PrefetchScalarGridSpec(
            num_scalar_prefetch=1,
            grid=(tokens // block,),
            in_specs=[by_token(half)] * 2
            + [by_token(width)] * 2
            + [fixed(vec.shape), fixed(bu.shape)]
            + [pl.BlockSpec(memory_space=pl.ANY)] * (6 + len(after)),
            out_specs=[by_token(n) for n, _ in outs] + [fixed((8, width)), fixed((1, hidden))],
            scratch_shapes=[
                pltpu.VMEM((width, width), bf16),
                pltpu.VMEM((width, hidden), bf16),
                pltpu.VMEM((hidden, width), bf16),
                pltpu.VMEM((block, hidden), f32),
                pltpu.VMEM((block, width), bf16),
                pltpu.SemaphoreType.DMA((10, blocks)),
            ],
        ),
        out_shape=[shape_of((tokens, n), t) for n, t in outs] + [shape_of((8, width), f32), shape_of((1, hidden), f32)],
        compiler_params=pltpu.CompilerParams(vmem_limit_bytes=40 * MIB),
        cost_estimate=pl.CostEstimate(flops=4 * 10**10, bytes_accessed=40 * MIB, transcendentals=0),
    )(order, om, ot, x, c, vec, bu, *up, *down, *after)


def copies(moves, sems, count, first=0, start=True, wait=True):
    def each(k, act):
        for i, (source, target) in enumerate(moves(k)):
            act(pltpu.make_async_copy(source, target, sems.at[first + i, k]))

    if start:
        lax.fori_loop(0, count, lambda k, c: (each(k, lambda copy: copy.start()), c)[1], 0)
    if wait:
        lax.fori_loop(0, count, lambda k, c: (each(k, lambda copy: copy.wait()), c)[1], 0)


def place(k, rows):
    return pl.ds(pl.multiple_of(k * rows, rows), rows)


def project_kernel(blocks, order_ref, x_ref, bias_ref, w_ref, *refs):
    out_ref, weight, sems = refs[-3:]
    rows, left = w_ref.shape[1:]
    right = weight.shape[1] - left

    @pl.when(pl.program_id(0) == 0)
    def _():
        def moves(k):
            at = place(k, rows)
            return [
                (w_ref.at[order_ref[k]], weight.at[at, 0:left]),
                (w_ref.at[blocks + order_ref[blocks + k], :, 0:right], weight.at[at, left : left + right]),
            ]

        copies(moves, sems, blocks)

    out_ref[...] = (dot(x_ref[...], weight[...]) + bias_ref[...]).astype(bf16)


def project(order, flip, x, bias, gathered, after=(), block=512):
    tokens, width = x.shape
    blocks, outs = gathered.shape[0] // 2, bias.shape[1] // 2
    half = lambda i, order: (0, 1 - order[2 * blocks] if flip else order[2 * blocks])
    return pl.pallas_call(
        partial(project_kernel, blocks),
        grid_spec=pltpu.PrefetchScalarGridSpec(
            num_scalar_prefetch=1,
            grid=(tokens // block,),
            in_specs=[
                pl.BlockSpec((block, width), lambda i, order: (i, 0)),
                pl.BlockSpec((1, outs), half),
            ]
            + [pl.BlockSpec(memory_space=pl.ANY)] * (1 + len(after)),
            out_specs=pl.BlockSpec((block, outs), lambda i, order: (i, 0)),
            scratch_shapes=[pltpu.VMEM((width, outs), bf16), pltpu.SemaphoreType.DMA((2, blocks))],
        ),
        out_shape=shape_of((tokens, outs), bf16),
        compiler_params=pltpu.CompilerParams(vmem_limit_bytes=24 * MIB),
        cost_estimate=pl.CostEstimate(flops=2 * tokens * width * outs, bytes_accessed=8 * MIB, transcendentals=0),
    )(order, x, bias, gathered, *after)


def token_kernel(blocks, order_ref, base_ref, dm_ref, dt_ref, wm_ref, wt_ref, *refs):
    out_ref, mine, theirs, sems = refs[-4:]
    rows, left = wm_ref.shape[1:]
    right = mine.shape[1] - left

    @pl.when(pl.program_id(0) == 0)
    def _():
        def moves(k):
            at, i, j = place(k, rows), order_ref[k], blocks + order_ref[blocks + k]
            return [
                (wm_ref.at[i], mine.at[at, 0:left]),
                (wm_ref.at[j, :, 0:right], mine.at[at, left : left + right]),
                (wt_ref.at[i], theirs.at[at, 0:left]),
                (wt_ref.at[j, :, 0:right], theirs.at[at, left : left + right]),
            ]

        copies(moves, sems, blocks)

    total = base_ref[...] + dot(dm_ref[...], mine[...], NT) + dot(dt_ref[...], theirs[...], NT)
    out_ref[...] = total.astype(bf16)


def token_gradient(order, base, dm, dt, gathered, after=(), block=256):
    tokens, width = base.shape
    blocks, outs = gathered[0].shape[0] // 2, dm.shape[1]
    by_token = lambda n: pl.BlockSpec((block, n), lambda i, order: (i, 0))
    return pl.pallas_call(
        partial(token_kernel, blocks),
        grid_spec=pltpu.PrefetchScalarGridSpec(
            num_scalar_prefetch=1,
            grid=(tokens // block,),
            in_specs=[by_token(width), by_token(outs), by_token(outs)]
            + [pl.BlockSpec(memory_space=pl.ANY)] * (2 + len(after)),
            out_specs=by_token(width),
            scratch_shapes=[pltpu.VMEM((width, outs), bf16)] * 2 + [pltpu.SemaphoreType.DMA((4, blocks))],
        ),
        out_shape=shape_of((tokens, width), bf16),
        compiler_params=pltpu.CompilerParams(vmem_limit_bytes=24 * MIB),
        cost_estimate=pl.CostEstimate(flops=4 * tokens * width * outs, bytes_accessed=14 * MIB, transcendentals=0),
    )(order, base, dm, dt, *gathered, *after)


TABLE_AT, UP_AT = 8, 32


def spread_kernel(devices, order_ref, b_ref, line_ref, vec_ref, up_ref, bias_ref, full, tab):
    blocks, rows = b_ref.shape[0:2]
    width, heads = vec_ref.shape[1], 2 * line_ref.shape[0]
    for k in range(blocks):
        full[rows * k : rows * k + rows, :] = b_ref[order_ref[blocks + k]].astype(f32)
    each, per, ups = width // devices, tab.shape[0] // devices, up_ref.shape[1] // devices
    vec_ref[...] = full[...].T[0:8, :]
    for d in range(devices):
        tab[per * d : per * d + per, :] = full[each * d : each * d + per, :]
        up_ref[:, ups * d : ups * d + ups] = full[each * d : each * d + 1, UP_AT : UP_AT + ups]
    table = tab[...].T[TABLE_AT : TABLE_AT + heads, :]
    buckets = table.shape[1]
    half, rest = buckets // 2, (ROW_LEN - buckets) // 2
    ends = [jnp.broadcast_to(table[:, i : i + 1], (heads, rest)) for i in (buckets - 1, 0)]
    lines = jnp.concatenate([table[:, half:], *ends, table[:, :half]], axis=1)
    for g in range(heads // 2):
        line_ref[g] = lines[2 * g : 2 * g + 2, :]
    for g in range(heads // 2):
        bias_ref[:, 384 * g : 384 * g + 128] = vec_ref[0:1, 128 * g : 128 * g + 128]
        bias_ref[:, 384 * g + 128 : 384 * g + 256] = jnp.zeros((1, 128), f32)
        bias_ref[:, 384 * g + 256 : 384 * g + 384] = vec_ref[1:2, 128 * g : 128 * g + 128]


def spread_small(order, b, devices, width, heads, buckets, hidden):
    blocks, rows = b.shape[0] // 2, b.shape[1]
    last = b.shape[2] // 128 - 1
    fixed = lambda s: pl.BlockSpec(s, lambda i, order: (0,) * len(s))
    shapes = [(heads // 2, 2, ROW_LEN), (8, width), (1, hidden), (1, 3 * width)]
    return pl.pallas_call(
        partial(spread_kernel, devices),
        grid_spec=pltpu.PrefetchScalarGridSpec(
            num_scalar_prefetch=1,
            grid=(1,),
            in_specs=[pl.BlockSpec((blocks, rows, 128), lambda i, order: (1, 0, last))],
            out_specs=[fixed(s) for s in shapes],
            scratch_shapes=[pltpu.VMEM((width, 128), f32), pltpu.VMEM((buckets, 128), f32)],
        ),
        out_shape=[shape_of(s, f32) for s in shapes],
        compiler_params=pltpu.CompilerParams(vmem_limit_bytes=8 * MIB),
        cost_estimate=pl.CostEstimate(flops=10**6, bytes_accessed=MIB, transcendentals=0),
    )(order, b)


def collect_kernel(devices, buckets, core_ref, vsum_ref, usum_ref, ms_ref, ts_ref, ml_ref, tl_ref, out_ref, tall, sums, lines):
    core = core_ref[0]
    width = vsum_ref.shape[1]
    pairs = ms_ref.shape[0]
    sums[core], sums[1 - core] = ms_ref[...], ts_ref[...]
    for g in range(pairs):
        lines[core, 2 * g : 2 * g + 2, :] = ml_ref[g]
        lines[1 - core, 2 * g : 2 * g + 2, :] = tl_ref[g]
    tall[...] = jnp.zeros_like(tall)
    tall[2:8, :] = vsum_ref[0:6, :]
    for side in range(2):
        for g in range(pairs):
            at = 128 * (side * pairs + g)
            tall[0:2, at : at + 128] = sums[side, g]
    out_ref[...] = tall[...].T
    line = jnp.concatenate([lines[0], lines[1]], axis=0)
    heads = line.shape[0]
    half, middle = buckets // 2, ROW_LEN // 2
    far = jnp.sum(line[:, half:middle], axis=1, keepdims=True)
    near = jnp.sum(line[:, middle : ROW_LEN - half], axis=1, keepdims=True)
    place = lax.broadcasted_iota(jnp.int32, (heads, half), 1)
    upper = line[:, :half] + jnp.where(place == half - 1, far, 0.0)
    lower = line[:, ROW_LEN - half :] + jnp.where(place == 0, near, 0.0)
    table = jnp.concatenate([lower, upper], axis=1)
    below = jnp.zeros((128 - TABLE_AT - heads, buckets), f32)
    table = jnp.concatenate([jnp.zeros((TABLE_AT, buckets), f32), table, below], axis=0).T
    each, per, ups = width // devices, buckets // devices, usum_ref.shape[1] // devices
    for d in range(devices):
        out_ref[each * d : each * d + per, :] += table[per * d : per * d + per, :]
        out_ref[each * d : each * d + 1, UP_AT : UP_AT + ups] = usum_ref[:, ups * d : ups * d + ups]


def collect_small(core, devices, buckets, vsum, usum, mine, theirs):
    width = vsum.shape[1]
    pairs = mine[1].shape[0]
    args = [vsum, usum, mine[1], theirs[1], mine[0], theirs[0]]
    whole = lambda t: pl.BlockSpec(t.shape, lambda i, core: (0,) * t.ndim)
    return pl.pallas_call(
        partial(collect_kernel, devices, buckets),
        grid_spec=pltpu.PrefetchScalarGridSpec(
            num_scalar_prefetch=1,
            grid=(1,),
            in_specs=[whole(t) for t in args],
            out_specs=pl.BlockSpec((width, 128), lambda i, core: (0, 0)),
            scratch_shapes=[
                pltpu.VMEM((128, width), f32),
                pltpu.VMEM((2, pairs, 2, 128), f32),
                pltpu.VMEM((2, 2 * pairs, ROW_LEN), f32),
            ],
        ),
        out_shape=shape_of((width, 128), f32),
        compiler_params=pltpu.CompilerParams(vmem_limit_bytes=8 * MIB),
        cost_estimate=pl.CostEstimate(flops=10**6, bytes_accessed=MIB, transcendentals=0),
    )(core, *args)


def pack_kernel(core_ref, *refs):
    vectors, (table_ref, up_ref, q_ref, k_ref, v_ref, wo_ref, wu_ref, wd_ref) = refs[:8], refs[8:16]
    outs, (tall, small) = refs[16:22], refs[22:]
    rows = q_ref.shape[0]
    for i, ref in enumerate(vectors):
        tall[i : i + 1, 0:rows] = ref[...]
    small[...] = tall[...].T[0:rows, :]
    lane = lax.broadcasted_iota(jnp.int32, small.shape, 1)
    small[...] = jnp.where(lane < 8, small[...], 0.0)
    per, heads = table_ref.shape
    small[0:per, TABLE_AT : TABLE_AT + heads] = table_ref[...]
    small[0:1, UP_AT : UP_AT + up_ref.shape[1]] = up_ref[...]
    extra = small[...].astype(bf16)
    low = lambda ref, first, last: ref[:, first:last].astype(bf16)
    h, f = wo_ref.shape[1] // 2, wu_ref.shape[1] // 2

    def write(side, square, up, down):
        for g in range(h // 128):
            at = side * h + 128 * g
            for i, ref in enumerate((q_ref, k_ref, v_ref)):
                square[:, 384 * g + 128 * i : 384 * g + 128 * i + 128] = low(ref, at, at + 128)
        square[:, 3 * h : 3 * h + 128] = extra
        up[:, 0:f] = low(wu_ref, side * f, side * f + f)
        up[:, f : f + h] = low(wo_ref, side * h, side * h + h)
        down[...] = low(wd_ref, side * h, side * h + h)

    @pl.when(core_ref[0] == 0)
    def _():
        write(0, *outs[0:3])
        write(1, *outs[3:6])

    @pl.when(core_ref[0] == 1)
    def _():
        write(1, *outs[0:3])
        write(0, *outs[3:6])


def pack(core, vectors, table, up, matrices):
    rows, width = matrices[0].shape
    args = [t.reshape(1, -1) for t in vectors] + [table, up.reshape(1, -1), *matrices]
    whole = lambda s: pl.BlockSpec(s, lambda i, core: (0, 0))
    shapes = [
        (rows, 3 * width // 2 + 128),
        (rows, (matrices[4].shape[1] + width) // 2),
        (matrices[5].shape[0], width // 2),
    ] * 2
    return pl.pallas_call(
        pack_kernel,
        grid_spec=pltpu.PrefetchScalarGridSpec(
            num_scalar_prefetch=1,
            grid=(1,),
            in_specs=[whole(t.shape) for t in args],
            out_specs=[whole(s) for s in shapes],
            scratch_shapes=[pltpu.VMEM((128, 128), f32), pltpu.VMEM((rows, 128), f32)],
        ),
        out_shape=[shape_of(s, bf16) for s in shapes],
        compiler_params=pltpu.CompilerParams(vmem_limit_bytes=60 * MIB),
        cost_estimate=pl.CostEstimate(flops=10**6, bytes_accessed=2 * MIB, transcendentals=0),
    )(core, *args)


class Links:
    def __init__(self, mesh):
        wide, narrow = mesh.shape[WIDE], mesh.shape[NARROW]
        self.sizes = (wide // 2, 2, narrow // 2, 2)
        w, n = lax.axis_index(WIDE), lax.axis_index(NARROW)
        self.place = (w // 2, w % 2, n // 2, n % 2)
        self.core = self.place[CORE]
        self.chips = wide * narrow // 2

    def number(self, at):
        return ((at[Z] * self.sizes[X] + at[X]) * self.sizes[Y] + at[Y]) * 2 + at[CORE]

    def fetch(self, value, axis, step):
        pairs = []
        for z in range(self.sizes[Z]):
            for x in range(self.sizes[X]):
                for y in range(self.sizes[Y]):
                    for c in range(2):
                        here = (z, x, y, c)
                        there = list(here)
                        there[axis] = (there[axis] + step) % self.sizes[axis]
                        pairs.append((self.number(there), self.number(here)))
        return lax.ppermute(value, AXES, pairs)

    def others(self, value, axis):
        return [self.fetch(value, axis, k) for k in range(1, self.sizes[axis])]

    def swapped(self, kept, sent):
        even = self.core == 0
        got = self.fetch(sent, CORE, 1)
        return jnp.where(even, kept, got), jnp.where(even, got, kept)

    def order(self):
        chip = jnp.arange(self.chips, dtype=jnp.int32)
        sz, sx, sy = self.sizes[:3]
        kz = (chip // (sx * sy) - self.place[Z]) % sz
        kx = (chip // sy - self.place[X]) % sx
        ky = (chip - self.place[Y]) % sy
        plane = 2 * ((kz * sy + ky) * sx + kx)
        return jnp.concatenate(
            [
                (ky * sx + kx) * sz + kz,
                (kx * sy + ky) * sz + kz,
                self.core.reshape(1),
                plane,
                plane + 1,
            ]
        ).astype(jnp.int32)

    def finish(self, total):
        rows = total.shape[0] // 2
        even = self.core == 0
        own = jnp.where(even, total[:rows], total[rows:])
        return own, self.fetch(jnp.where(even, total[rows:], total[:rows]), CORE, 1)


def ring(me, k, size):
    at = me + k
    return jnp.where(at >= size, at - size, at)


def fold_1_kernel(halves, sizes, count, place_ref, *refs):
    kept, got, outs = refs[:count], refs[count : 2 * count], refs[2 * count :]
    split = sizes[Y]
    a_outs, b_outs = outs[:split], outs[split:]

    def write(out, at, half, x, y):
        rows, column = out.shape[2], 0
        for piece, part, first, last in half:
            source = (0, x, y, part, slice(None), slice(first, last))
            value = kept[piece][source] + got[piece][source].astype(f32)
            for row in range(0, value.shape[0], rows):
                some = value[row : row + rows, :].astype(out.dtype)
                out[0, at, :, column : column + last - first] = some
                column += last - first

    for k, out in enumerate(a_outs):
        y = ring(place_ref[Y], k, sizes[Y])
        for x in range(sizes[X]):
            write(out, x, halves[0], x, y)
    for k, out in enumerate(b_outs):
        x = ring(place_ref[X], k, sizes[X])
        for y in range(sizes[Y]):
            write(out, y, halves[1], x, y)


def fold_2_kernel(sizes, place_ref, *refs):
    sy, sx = sizes[Y], sizes[X]
    a_in, b_in, outs = refs[:sy], refs[sy : sy + sx], refs[sy + sx :]
    a_outs, b_outs = outs[:sx], outs[sx:]

    def value(ins, at):
        total = ins[0][0, at]
        for piece in ins[1:]:
            total = total + piece[0, at].astype(f32)
        return total

    for k, out in enumerate(a_outs):
        out[0] = value(a_in, ring(place_ref[X], k, sx)).astype(out.dtype)
    for k, out in enumerate(b_outs):
        out[0] = value(b_in, ring(place_ref[Y], k, sy)).astype(out.dtype)


def fold_3_kernel(sizes, place_ref, *refs):
    sy, sx = sizes[Y], sizes[X]
    a_in, b_in, outs = refs[:sx], refs[sx : sx + sy], refs[sx + sy :]
    rows, columns = a_in[0].shape[1:]
    for k, out in enumerate(outs):
        z = ring(place_ref[Z], k, sizes[Z])
        for n, ins in enumerate((a_in, b_in)):
            total = ins[0][z]
            for piece in ins[1:]:
                total = total + piece[z].astype(f32)
            first = n * columns
            out[0, :, first : first + total.shape[1]] = total.astype(out.dtype)


def fold_call(kernel, place, ins, outs, steps):
    block = lambda s: pl.BlockSpec((s[0] // steps,) + tuple(s[1:]), lambda i, place: (i,) + (0,) * (len(s) - 1))
    return pl.pallas_call(
        kernel,
        grid_spec=pltpu.PrefetchScalarGridSpec(
            num_scalar_prefetch=1,
            grid=(steps,),
            in_specs=[block(t.shape) for t in ins],
            out_specs=[block(s) for s, _ in outs],
        ),
        out_shape=[shape_of(s, t) for s, t in outs],
        compiler_params=pltpu.CompilerParams(vmem_limit_bytes=24 * MIB),
        cost_estimate=pl.CostEstimate(flops=10**6, bytes_accessed=8 * MIB, transcendentals=0),
    )(place, *ins)


class Fold:
    def __init__(self, links, halves):
        self.links, self.halves = links, halves
        self.place = jnp.stack(links.place).astype(jnp.int32)

    def to_others(self, values, axis):
        size = self.links.sizes[axis]
        return [self.links.fetch(v, axis, size - k) for k, v in enumerate(values) if k]

    def first(self, kept, got):
        sizes = self.links.sizes
        sz, sx, sy = sizes[:3]
        rows = kept[0].shape[4]
        wide = [sum((e[3] - e[2]) * kept[e[0]].shape[4] // rows for e in half) for half in self.halves]
        kinds = lambda shape, n: [(shape, f32)] + [(shape, bf16)] * (n - 1)
        outs = kinds((sz, sx, rows, wide[0]), sy) + kinds((sz, sy, rows, wide[1]), sx)
        done = fold_call(partial(fold_1_kernel, self.halves, sizes, len(kept)), self.place, [*kept, *got], outs, sz)
        a, b = done[:sy], done[sy:]
        return [a[0], b[0]], self.to_others(a, Y), self.to_others(b, X)

    def second(self, own, got_y, got_x):
        sizes = self.links.sizes
        sz, sx, sy = sizes[:3]
        kinds = lambda t, n: [((sz,) + t.shape[2:], f32)] + [((sz,) + t.shape[2:], bf16)] * (n - 1)
        outs = kinds(own[0], sx) + kinds(own[1], sy)
        done = fold_call(partial(fold_2_kernel, sizes), self.place, [own[0], *got_y, own[1], *got_x], outs, sz)
        a, b = done[:sx], done[sx:]
        return [[a[0], b[0]], self.to_others(a, X), self.to_others(b, Y)]

    def third(self, own, got_x, got_y):
        sizes = self.links.sizes
        rows, ca = own[0].shape[1:]
        shape = (1, rows, ca + own[1].shape[2])
        outs = [(shape, f32)] + [(shape, bf16)] * (sizes[Z] - 1)
        ins = [own[0], *got_x, own[1], *got_y]
        done = fold_call(partial(fold_3_kernel, sizes), self.place, ins, outs, 1)
        return done[0], self.to_others(done, Z)

    def last(self, own, got):
        for piece in got:
            own = own + piece.astype(f32)
        return own[0]


def last_kernel(heads, core_ref, own_ref, *refs):
    pieces, outs = refs[: -(2 + 8 + 2)], refs[-(2 + 8 + 2) :]
    keep_ref, send_ref, vectors, table_ref, up_ref = outs[0], outs[1], outs[2:10], outs[10], outs[11]
    rows, width = keep_ref.shape
    total = own_ref[0]
    for piece in pieces:
        total = total + piece[0].astype(f32)

    def write(own, other):
        keep_ref[...] = own[:, 0:width]
        send_ref[...] = other[:, 0:width]
        small = own[:, width:]
        table_ref[...] = small[0 : table_ref.shape[0], TABLE_AT : TABLE_AT + heads]
        up_ref[...] = small[0:1, UP_AT : UP_AT + up_ref.shape[1]]
        turned = jnp.concatenate([small, jnp.zeros((128 - rows, 128), f32)], axis=0).T
        for i, ref in enumerate(vectors):
            ref[...] = turned[i : i + 1, 0:rows]

    @pl.when(core_ref[0] == 0)
    def _():
        write(total[:rows], total[rows:])

    @pl.when(core_ref[0] == 1)
    def _():
        write(total[rows:], total[:rows])


def join_kernel(core_ref, keep_ref, got_ref, *outs):
    def write(sides):
        for s, side in enumerate(sides):
            for g in range(side.shape[1] // 384):
                at = s * (side.shape[1] // 3) + 128 * g
                for i, out in enumerate(outs):
                    out[:, at : at + 128] = side[:, 384 * g + 128 * i : 384 * g + 128 * i + 128]

    @pl.when(core_ref[0] == 0)
    def _():
        write((keep_ref, got_ref))

    @pl.when(core_ref[0] == 1)
    def _():
        write((got_ref, keep_ref))


def join_wide_kernel(core_ref, keep_ref, got_ref, down_keep_ref, down_got_ref, out_ref, up_ref, down_ref):
    h, f = out_ref.shape[1] // 2, up_ref.shape[1] // 2

    def write(sides, downs):
        for s in range(2):
            up_ref[:, s * f : s * f + f] = sides[s][:, 0:f]
            out_ref[:, s * h : s * h + h] = sides[s][:, f : f + h]
            down_ref[:, s * h : s * h + h] = downs[s][...]

    @pl.when(core_ref[0] == 0)
    def _():
        write((keep_ref, got_ref), (down_keep_ref, down_got_ref))

    @pl.when(core_ref[0] == 1)
    def _():
        write((got_ref, keep_ref), (down_got_ref, down_keep_ref))


def whole_call(kernel, core, ins, outs):
    whole = lambda s: pl.BlockSpec(s, lambda i, core: (0,) * len(s))
    return pl.pallas_call(
        kernel,
        grid_spec=pltpu.PrefetchScalarGridSpec(
            num_scalar_prefetch=1,
            grid=(1,),
            in_specs=[whole(t.shape) for t in ins],
            out_specs=[whole(s) for s in outs],
        ),
        out_shape=[shape_of(s, f32) for s in outs],
        compiler_params=pltpu.CompilerParams(vmem_limit_bytes=16 * MIB),
        cost_estimate=pl.CostEstimate(flops=10**6, bytes_accessed=2 * MIB, transcendentals=0),
    )(core, *ins)


def segments(lengths):
    place = jnp.arange(ROW_LEN, dtype=jnp.int32)
    ending = jnp.cumsum(lengths, axis=1)
    return jnp.sum((place[None, :, None] >= ending[:, None, :]).astype(jnp.int32), axis=2)


def per_device(
    mesh, tokens, cotangent, pair_lengths, w_query, w_key, w_value, w_output, w_up, w_down, b_query, b_value,
    b_output, b_up, b_down, first_gain, first_shift, second_gain, second_shift, bucket_bias,
):
    links = Links(mesh)
    devices = 2 * links.chips
    rows, width = w_query.shape
    hidden = w_up.shape[1]
    heads = bucket_bias.shape[1]
    buckets = bucket_bias.shape[0] * devices
    w_half, h_half = width // 2, hidden // 2
    low = lambda t: t.astype(bf16)
    barrier = lax.optimization_barrier
    core = links.core
    even = core == 0
    order = links.order()
    blocks = lambda a, b: [a, b]
    deep = square_blocks = lambda t: t
    if (2 * rows) % 16 or w_down.shape[0] % 16:
        found, order = order, jnp.concatenate([jnp.zeros((2,), jnp.int32), core.reshape(1), jnp.arange(2, dtype=jnp.int32)])
        n = links.chips
        sort = lambda t, first: jnp.take(t, found[first : first + n], axis=0)

        def blocks(a, b):
            return [t.reshape(1, -1, t.shape[2]) for t in (sort(a, 0), sort(b, n))]

        def square_blocks(t):
            return jnp.stack([sort(t[:n], 0), sort(t[n:], n)]).reshape(2, -1, t.shape[2])

        def deep(t):
            both = jnp.stack([sort(t, 2 * n + 1), sort(t, 3 * n + 1)], axis=1)
            return both.reshape(2, -1, t.shape[2])

    half = 3 * w_half
    cut = (half + 128) // 2
    up_cut = (h_half + w_half + 128) // 256 * 128
    packed = pack(
        core.reshape(1),
        [b_query, b_value, b_output, b_down, first_gain, first_shift, second_gain, second_shift],
        bucket_bias,
        b_up,
        [w_query, w_key, w_value, w_output, w_up, w_down],
    )
    swapped = lambda i: jnp.concatenate(links.swapped(packed[i], packed[i + 3]), axis=0)
    pair = swapped(0)
    pair_z = links.others(pair, Z)
    up_pair = swapped(1)
    down_pair = jnp.stack(links.swapped(packed[2], packed[5]))
    down_x = links.others(down_pair, X)

    def together(*groups):
        sizes = [len(g) for g in groups]
        flat = barrier(tuple(t for g in groups for t in g))
        out = []
        for size in sizes:
            out.append(list(flat[:size]))
            flat = flat[size:]
        return out

    def spans(*groups):
        leaves, tree = jax.tree.flatten(tuple(groups))
        return jax.tree.unflatten(tree, barrier(tuple(leaves)))

    def chips(value, got):
        value = jnp.stack([value] + got)
        return value.reshape((-1,) + value.shape[-2:])

    def plane_1(value, cut):
        return [value[:, :, :cut], value[:, :, cut:]], links.others(value[:, :, :cut], X), links.others(value[:, :, cut:], Y)

    def plane_2(ab, got_x, got_y):
        ab = [chips(ab[0], got_x), chips(ab[1], got_y)]
        return ab, links.others(ab[0], Y), links.others(ab[1], X)

    def plane_3(ab, got_y, got_x):
        return chips(ab[0], got_y), chips(ab[1], got_x)

    pair_z, (pair, up_pair), down_x = together(pair_z, (pair, up_pair), down_x)
    stage = plane_1(jnp.stack([pair] + pair_z), cut)
    down_pair = jnp.stack([down_pair] + down_x)
    down_y = links.others(down_pair, Y)
    up_z = links.others(up_pair, Z)
    got_x, got_y, down_y, up_z, (up_pair,) = together(*stage[1:], down_y, up_z, (up_pair,))
    stage = plane_2(stage[0], got_x, got_y)
    down_own = jnp.stack([down_pair] + down_y)
    down_z = links.others(down_own, Z)
    got_y, got_x, up_z, down_z[-1:] = together(*stage[1:], up_z, down_z[-1:])
    mine = jnp.concatenate(plane_3(stage[0], got_y, got_x), axis=0)

    theirs = links.fetch(mine, CORE, 1)
    mine, theirs = square_blocks(mine), square_blocks(theirs)
    lines, vectors, up_bias, bias = spread_small(order, mine, devices, width, heads, buckets, hidden)
    segment = segments(pair_lengths)
    segc, segr = segment[:, :, None], segment[:, None, :]
    pairs = heads // 4
    first_m, first_t = (core * pairs).reshape(1), ((1 - core) * pairs).reshape(1)
    qkv_m = project(order, False, tokens, bias, mine)
    up_z, (qkv_m, bias_t, theirs) = together(up_z, (qkv_m, bias, theirs))
    up_stage = plane_1(jnp.stack([up_pair] + up_z), up_cut)
    o_m, p_m = attend_forward(first_m, lines, segc, segr, qkv_m)
    (o_m, theirs), got_x, got_y = together((o_m, theirs), up_stage[1], up_stage[2])

    up_stage = plane_2(up_stage[0], got_x, got_y)
    qkv_t = project(order, True, tokens, bias_t, theirs)
    o_t, p_t = attend_forward(first_t, lines, segc, segr, qkv_t)
    (o_m, o_t), got_y, got_x = together((o_m, o_t), *up_stage[1:])
    up_a, up_b = plane_3(up_stage[0], got_y, got_x)
    up_theirs = (links.fetch(up_a, CORE, 1), links.fetch(up_b, CORE, 1))
    up_a, up_b, *down_z = barrier((up_a, up_b, *down_z))
    down_mine = jnp.stack([down_own] + down_z)
    down_mine = down_mine.reshape((-1,) + down_mine.shape[-2:])
    down_theirs = links.fetch(down_mine, CORE, 1)

    result, dh1, settled, active, do_m, do_t, dy1_m, dy1_t, dy2_m, dy2_t, dz_m, dz_t, vsum, usum = middle(
        order,
        o_m,
        o_t,
        tokens,
        cotangent,
        vectors,
        up_bias,
        blocks(up_a, up_b) + blocks(*up_theirs),
        [deep(down_mine), deep(down_theirs)],
    )

    def pieces(t, parts=1):
        return t.reshape(links.sizes[:3] + (parts, -1, t.shape[1]))

    exchange = lambda *values: [links.fetch(low(t), CORE, 1) for t in values]
    o_both = jnp.where(even, jnp.concatenate([o_m, o_t], axis=1), jnp.concatenate([o_t, o_m], axis=1))
    outs = [dot(o_both, t, TN) for t in (dy1_t, dy1_m)]
    outs, (dz_t, dz_m, settled) = together(outs, (dz_t, dz_m, settled))
    up_parts = lambda dz, out: [pieces(dot(settled, dz, TN)), pieces(out)]
    wide_fold = Fold(
        links,
        [
            [(0, 0, 0, up_cut), (2, 0, 0, w_half)],
            [(0, 0, up_cut, h_half), (1, 0, 0, w_half), (2, 1, 0, w_half)],
        ],
    )
    square_fold = Fold(links, [[(0, 0, 0, cut)], [(0, 0, cut, half), (1, 0, 0, 128)]])

    got = exchange(*up_parts(dz_t, outs[0]))
    kept = up_parts(dz_m, outs[1])
    got, kept, (dy2_t, dy2_m) = spans(got, kept, (dy2_t, dy2_m))
    got += exchange(pieces(dot(active, dy2_t, TN), 2))
    kept += [pieces(dot(active, dy2_m, TN), 2)]
    got, kept, (do_t, do_m) = spans(got, kept, (do_t, do_m))

    wide = wide_fold.first(kept, got)
    grads_t, grads_m = attend_backward((qkv_t, do_t, o_t, p_t), (qkv_m, do_m, o_m, p_m))
    wide, grads_t, grads_m = spans(wide, grads_t, grads_m)

    wide = wide_fold.second(*wide)
    wide[0], grads_t, grads_m = spans(wide[0], grads_t, grads_m)
    square_got = exchange(pieces(dot(tokens, grads_t[0], TN)))
    g_small = pieces(collect_small(core.reshape(1), devices, buckets, vsum, usum, grads_m[1:], grads_t[1:]))
    square_got += exchange(g_small)
    square_kept = [pieces(dot(tokens, grads_m[0], TN)), g_small]
    wide, square_kept, square_got, (d_m, d_t) = spans(wide, square_kept, square_got, (grads_m[0], grads_t[0]))

    square = square_fold.first(square_kept, square_got)
    wide_own, wide_got = wide_fold.third(*wide)
    grad_tokens = token_gradient(order, dh1, d_m, d_t, [mine, theirs])
    square, grad_tokens = spans(square, grad_tokens)

    square = square_fold.second(*square)
    square = spans(square)[0]
    square_own, square_z = square_fold.third(*square)
    wide_got, square_own = spans(wide_got, square_own)
    wide_total = wide_fold.last(wide_own, wide_got)
    wide_a = up_cut + 2 * w_half
    up_total = jnp.concatenate([wide_total[:, :up_cut], wide_total[:, wide_a : wide_a + h_half + w_half - up_cut]], axis=1)
    groups = w_down.shape[0] // (2 * rows)
    down_total = jnp.stack(
        [
            jnp.concatenate([wide_total[:, first + w_half * i : first + w_half * (i + 1)] for i in range(groups)], axis=0)
            for first in (up_cut, wide_total.shape[1] - groups * w_half)
        ]
    ).reshape(-1, w_half)

    core_1 = core.reshape(1)
    out_output, out_up, out_down = whole_call(
        join_wide_kernel,
        core_1,
        [*links.finish(up_total), *links.finish(down_total)],
        [(rows, width), (rows, hidden), w_down.shape],
    )
    shapes = [(rows, half)] * 2 + [(1, rows)] * 8 + [bucket_bias.shape, (1, b_up.shape[0])]
    own, other, *flat = whole_call(partial(last_kernel, heads), core_1, [square_own, *square_z], shapes)
    *flat, out_table, out_b_up = flat
    flat = [t.reshape(-1) for t in flat]
    out_query, out_key, out_value = whole_call(
        join_kernel, core_1, [own, links.fetch(other, CORE, 1)], [(rows, width)] * 3
    )
    return (
        result,
        grad_tokens,
        out_query,
        out_key,
        out_value,
        out_output,
        out_up,
        out_down,
        flat[0],
        flat[1],
        flat[2],
        out_b_up.reshape(-1),
        flat[3],
        flat[4],
        flat[5],
        flat[6],
        flat[7],
        out_table,
    )


def solution(mesh):
    split, line = P(AXES, None), P(AXES)
    return jax.shard_map(
        partial(per_device, mesh),
        mesh=mesh,
        in_specs=(split,) * 9 + (line,) * 9 + (split,),
        out_specs=(split,) * 8 + (line,) * 9 + (split,),
        check_vma=False,
    )
```

```python
from functools import partial
import math

import jax
import jax.numpy as jnp
from jax import lax
from jax.experimental import pallas as pl
from jax.experimental.pallas import tpu as pltpu
from jax.sharding import PartitionSpec as P

WIDE, NARROW = "wide", "narrow"
AXES = (WIDE, NARROW)
Z, X, Y, CORE = range(4)
ROW_LEN = 512
MIB = 1 << 20
bf16, f32 = jnp.bfloat16, jnp.float32
NN = (((1,), (0,)), ((), ()))
NT = (((1,), (1,)), ((), ()))
TN = (((0,), (0,)), ((), ()))


def dot(left, right, dims=NN):
    return lax.dot_general(left, right, dims, preferred_element_type=f32)


def shape_of(shape, dtype):
    return jax.ShapeDtypeStruct(shape, dtype)


def toeplitz(line, ref, head):
    base = jnp.concatenate([pltpu.roll(line, s, 1) if s else line for s in range(8)], axis=0)
    for c in range(16):
        turned = pltpu.roll(base, 8 * c, 1) if c else base
        for b in range(ROW_LEN // 128):
            cut = ROW_LEN - 128 * b
            piece = jnp.concatenate([turned[:, cut:], turned[:, :cut]], axis=1) if b else turned
            first = 128 * b + 8 * c
            ref[head, first : first + 8, :] = piece


def diagonals(ref, head):
    total = None
    for c in range(16):
        turned = None
        for b in range(ROW_LEN // 128):
            first = 128 * b + 8 * c
            piece = ref[head, first : first + 8, :]
            if b:
                piece = jnp.concatenate([piece[:, 128 * b :], piece[:, : 128 * b]], axis=1)
            turned = piece if turned is None else turned + piece
        if c:
            turned = pltpu.roll(turned, ROW_LEN - 8 * c, 1)
        total = turned if total is None else total + turned
    out = total[0:1]
    for s in range(1, 8):
        out = out + pltpu.roll(total[s : s + 1], ROW_LEN - s, 1)
    return out


def forward_kernel(first_ref, line_ref, segc_ref, segr_ref, qkv_ref, *refs):
    o_ref, p_ref, bias, mask = refs[-4:]
    g, r = pl.program_id(0), pl.program_id(1)

    @pl.when(g == 0)
    def _():
        mask[r] = jnp.where(segc_ref[0] == segr_ref[0], 0.0, -1e30)

    @pl.when(r == 0)
    def _():
        for h in range(2):
            toeplitz(line_ref[0, h : h + 1, :], bias, h)

    q, k, v = qkv_ref[:, 0:128], qkv_ref[:, 128:256], qkv_ref[:, 256:384]
    lane = lax.broadcasted_iota(jnp.int32, (ROW_LEN, 128), 1)
    outs = []
    for h in range(2):
        mine = (lane < 64) if h == 0 else (lane >= 64)
        qh = jnp.where(mine, q.astype(f32) * 0.125, 0.0).astype(bf16)
        s = dot(qh, k, NT) + bias[h] + mask[r]
        e = jnp.exp(s - jnp.max(s, axis=1, keepdims=True))
        p = (e * (1.0 / jnp.sum(e, axis=1, keepdims=True))).astype(bf16)
        p_ref[0, h] = p
        outs.append(dot(p, v))
    o_ref[...] = jnp.where(lane < 64, outs[0], outs[1]).astype(bf16)


def attend_forward(first, lines, segc, segr, qkv, after=()):
    pairs, rows = qkv.shape[1] // 384, segc.shape[0]
    return pl.pallas_call(
        forward_kernel,
        grid_spec=pltpu.PrefetchScalarGridSpec(
            num_scalar_prefetch=1,
            grid=(pairs, rows),
            in_specs=[
                pl.BlockSpec((1, 2, ROW_LEN), lambda g, r, first: (g + first[0], 0, 0)),
                pl.BlockSpec((1, ROW_LEN, 1), lambda g, r, first: (r, 0, 0)),
                pl.BlockSpec((1, 1, ROW_LEN), lambda g, r, first: (r, 0, 0)),
                pl.BlockSpec((ROW_LEN, 384), lambda g, r, first: (r, g)),
            ]
            + [pl.BlockSpec(memory_space=pl.ANY)] * len(after),
            out_specs=[
                pl.BlockSpec((ROW_LEN, 128), lambda g, r, first: (r, g)),
                pl.BlockSpec((1, 2, ROW_LEN, ROW_LEN), lambda g, r, first: (r, g, 0, 0)),
            ],
            scratch_shapes=[pltpu.VMEM((2, ROW_LEN, ROW_LEN), f32), pltpu.VMEM((rows, ROW_LEN, ROW_LEN), f32)],
        ),
        out_shape=[
            shape_of((rows * ROW_LEN, 128 * pairs), bf16),
            shape_of((rows, 2 * pairs, ROW_LEN, ROW_LEN), bf16),
        ],
        compiler_params=pltpu.CompilerParams(vmem_limit_bytes=44 * MIB),
        cost_estimate=pl.CostEstimate(flops=pairs * rows * 2 * 10**9, bytes_accessed=pairs * rows * 2 * MIB, transcendentals=0),
    )(first, lines, segc, segr, qkv, *after)


def backward_kernel(*refs):
    ins, outs, acc = (refs[0:4], refs[4:8]), (refs[-7:-4], refs[-4:-1]), refs[-1]
    for side in range(2):

        @pl.when(pl.program_id(0) == side)
        def _():
            backward_step(*ins[side], *outs[side], acc)


def backward_step(qkv_ref, do_ref, o_ref, p_ref, d_ref, line_ref, sums_ref, acc):
    r, last = pl.program_id(2), pl.num_programs(2) - 1
    q, k, v = qkv_ref[:, 0:128], qkv_ref[:, 128:256], qkv_ref[:, 256:384]
    lane = lax.broadcasted_iota(jnp.int32, (ROW_LEN, 128), 1)
    qt = (q.astype(f32) * 0.125).T.astype(bf16)
    do = do_ref[...].astype(f32)
    dot_t = do.T.astype(bf16)
    prod = do * o_ref[...].astype(f32)
    dqs, dks, dvs = [], [], []
    for h in range(2):
        mine = (lane < 64) if h == 0 else (lane >= 64)
        doh = jnp.where(mine, do, 0.0).astype(bf16)
        delta = jnp.sum(jnp.where(mine, prod, 0.0), axis=1, keepdims=True)
        p = p_ref[0, h]
        ds = p.astype(f32) * (dot(doh, v, NT) - delta)

        @pl.when(r == 0)
        def _():
            acc[h] = ds

        @pl.when(r > 0)
        def _():
            acc[h] += ds

        dsb = ds.astype(bf16)
        half = slice(64 * h, 64 * h + 64)
        dqs.append(dot(dsb, k))
        dks.append(dot(qt[half, :], dsb))
        dvs.append(dot(dot_t[half, :], p))
    dq = jnp.where(lane < 64, dqs[0], dqs[1]) * 0.125
    dk = jnp.concatenate(dks, axis=0).T
    dv = jnp.concatenate(dvs, axis=0).T
    d_ref[:, 0:128] = dq.astype(bf16)
    d_ref[:, 128:256] = dk.astype(bf16)
    d_ref[:, 256:384] = dv.astype(bf16)
    sums = jnp.concatenate([jnp.sum(dq, axis=0, keepdims=True), jnp.sum(dv, axis=0, keepdims=True)], axis=0)

    @pl.when(r == 0)
    def _():
        sums_ref[0] = sums

    @pl.when(r > 0)
    def _():
        sums_ref[0] += sums

    @pl.when(r == last)
    def _():
        for h in range(2):
            line_ref[0, h : h + 1, :] = diagonals(acc, h)


def attend_backward(first, second, after=()):
    rows, pairs = first[3].shape[0], first[0].shape[1] // 384
    ends = ((0, 0), (pairs - 1, rows - 1))

    def block(shape, at, side):
        def index(s, g, r):
            mine = s == side
            return at(jnp.where(mine, g, ends[1 - side][0]), jnp.where(mine, r, ends[1 - side][1]))

        return pl.BlockSpec(shape, index)

    both = lambda shape, at: [block(shape, at, side) for side in range(2)]
    by_row, by_pair = lambda g, r: (r, g), lambda g, r: (g, 0, 0)
    wide, half = both((ROW_LEN, 384), by_row), both((ROW_LEN, 128), by_row)
    probs = both((1, 2, ROW_LEN, ROW_LEN), lambda g, r: (r, g, 0, 0))
    lines, sums = both((1, 2, ROW_LEN), by_pair), both((1, 2, 128), by_pair)
    shapes = [
        shape_of((rows * ROW_LEN, 384 * pairs), bf16),
        shape_of((pairs, 2, ROW_LEN), f32),
        shape_of((pairs, 2, 128), f32),
    ]
    done = pl.pallas_call(
        backward_kernel,
        grid=(2, pairs, rows),
        in_specs=[spec for i in range(2) for spec in (wide[i], half[i], half[i], probs[i])]
        + [pl.BlockSpec(memory_space=pl.ANY)] * len(after),
        out_specs=[spec for i in range(2) for spec in (wide[i], lines[i], sums[i])],
        out_shape=shapes * 2,
        scratch_shapes=[pltpu.VMEM((2, ROW_LEN, ROW_LEN), f32)],
        compiler_params=pltpu.CompilerParams(vmem_limit_bytes=50 * MIB),
        cost_estimate=pl.CostEstimate(flops=pairs * rows * 4 * 10**9, bytes_accessed=pairs * rows * 4 * MIB, transcendentals=0),
    )(*first, *second, *after)
    return done[:3], done[3:]


def normalize(value, gain, shift):
    center = value - jnp.mean(value, axis=1, keepdims=True)
    inverse = lax.rsqrt(jnp.mean(center * center, axis=1, keepdims=True) + 1e-5)
    normed = center * inverse
    return normed, inverse, normed * gain + shift


def normalize_back(upstream, normed, inverse, gain):
    scaled = upstream * gain
    return inverse * (
        scaled
        - jnp.mean(scaled, axis=1, keepdims=True)
        - normed * jnp.mean(scaled * normed, axis=1, keepdims=True)
    )


def column_sum(value):
    return jnp.sum(value, axis=0, keepdims=True)


def middle_kernel(
    blocks, order_ref,
    om_ref, ot_ref, x_ref, c_ref, vec_ref, bu_ref, uma_ref, umb_ref, uta_ref, utb_ref, dm_ref, dt_ref,
    *refs,
):
    (
        out_ref, dh1_ref, a_ref, g_ref, dom_ref, dot_ref, dy1m_ref, dy1t_ref, dy2m_ref, dy2t_ref, dzm_ref, dzt_ref,
        vsum_ref, usum_ref, wo, wu, wd, slope, dy, sems,
    ) = refs[-20:]
    step = pl.program_id(0)
    width, hidden = wu.shape
    core = order_ref[2 * blocks]
    w_half, h_half = width // 2, hidden // 2

    def cols(size, side, first=0, count=None):
        return pl.ds(pl.multiple_of(side * size + first, 128), size if count is None else count)

    up_left = uma_ref.shape[2]
    up_right = h_half - up_left
    rows, deep = uma_ref.shape[1], dm_ref.shape[1]
    sides = ((core, uma_ref, umb_ref, dm_ref), (1 - core, uta_ref, utb_ref, dt_ref))

    def out_moves(k):
        j, at = order_ref[blocks + k], place(k, rows)
        return [(ub.at[j, :, up_right : up_right + w_half], wo.at[at, cols(w_half, s)]) for s, ua, ub, d in sides]

    def up_moves(k):
        i, j, at = order_ref[k], order_ref[blocks + k], place(k, rows)
        first = [(ua.at[i], wu.at[at, cols(h_half, s, 0, up_left)]) for s, ua, ub, d in sides]
        second = [(ub.at[j, :, 0:up_right], wu.at[at, cols(h_half, s, up_left, up_right)]) for s, ua, ub, d in sides]
        return first + second

    def down_moves(k):
        found = []
        for n in range(2):
            i, at = order_ref[(2 + n) * blocks + 1 + k], place(2 * k + n, deep)
            found += [(d.at[i], wd.at[at, cols(w_half, s)]) for s, ua, ub, d in sides]
        return found

    groups = ((out_moves, 0), (up_moves, 2), (down_moves, 6))

    @pl.when(step == 0)
    def _():
        for moves, first in groups:
            copies(moves, sems, blocks, first, wait=False)

    def ready(group):
        @pl.when(step == 0)
        def _():
            copies(groups[group][0], sems, blocks, groups[group][1], start=False)

    ready(0)
    rows_of = lambda side: cols(w_half, side)
    b_out, b_down, gain1, shift1, gain2, shift2 = [vec_ref[i : i + 1, :] for i in range(2, 8)]
    first = x_ref[...].astype(f32) + dot(om_ref[...], wo[rows_of(core), :]) + dot(ot_ref[...], wo[rows_of(1 - core), :]) + b_out
    n1, r1, a = normalize(first, gain1, shift1)
    ab = a.astype(bf16)
    a_ref[...] = ab
    second = a + b_down
    chunk = h_half // 2
    ready(1)
    for f in range(0, hidden, chunk):
        at = slice(f, f + chunk)
        z = dot(ab, wu[:, at]) + bu_ref[:, at]
        mass = 0.5 * (1.0 + lax.erf(z * (1.0 / math.sqrt(2.0))))
        slope[:, at] = mass + z * jnp.exp(-0.5 * z * z) * (1.0 / math.sqrt(2.0 * math.pi))
        active = (z * mass).astype(bf16)
        g_ref[:, at] = active
        if f == 0:
            ready(2)
        second = second + dot(active, wd[at, :])
    n2, r2, out = normalize(second, gain2, shift2)
    out_ref[...] = out.astype(bf16)
    c = c_ref[...].astype(f32)
    dh2 = normalize_back(c, n2, r2, gain2)
    dy2 = dh2.astype(bf16)
    dy[...] = dy2
    dy2m_ref[...] = dy[:, cols(w_half, core)]
    dy2t_ref[...] = dy[:, cols(w_half, 1 - core)]
    da = dh2
    parts = []
    for side, dz_ref in ((core, dzm_ref), (1 - core, dzt_ref)):
        for f in range(0, h_half, chunk):
            at = cols(h_half, side, f, chunk)
            dz = dot(dy2, wd[at, :], NT) * slope[:, at]
            parts.append((at, column_sum(dz)))
            dzb = dz.astype(bf16)
            dz_ref[:, f : f + chunk] = dzb
            da = da + dot(dzb, wu[:, at], NT)
    dh1 = normalize_back(da, n1, r1, gain1)
    dh1_ref[...] = dh1
    dy1 = dh1.astype(bf16)
    dy[...] = dy1
    dy1m_ref[...] = dy[:, cols(w_half, core)]
    dy1t_ref[...] = dy[:, cols(w_half, 1 - core)]
    dom_ref[...] = dot(dy1, wo[rows_of(core), :], NT).astype(bf16)
    dot_ref[...] = dot(dy1, wo[rows_of(1 - core), :], NT).astype(bf16)
    sums = [column_sum(t) for t in (dh1, dh2, da * n1, da, c * n2, c)]
    vsum = jnp.concatenate(sums + [jnp.zeros((2, c.shape[1]), f32)], axis=0)

    @pl.when(step == 0)
    def _():
        vsum_ref[...] = vsum
        for at, part in parts:
            usum_ref[:, at] = part

    @pl.when(step > 0)
    def _():
        vsum_ref[...] += vsum
        for at, part in parts:
            usum_ref[:, at] += part


def middle(order, om, ot, x, c, vec, bu, up, down, after=(), block=256):
    tokens, width = x.shape
    hidden = bu.shape[1]
    blocks = up[0].shape[0]
    by_token = lambda n: pl.BlockSpec((block, n), lambda i, order: (i, 0))
    fixed = lambda s: pl.BlockSpec(s, lambda i, order: (0, 0))
    half, h_half = width // 2, hidden // 2
    outs = [(width, bf16), (width, f32), (width, bf16), (hidden, bf16)] + [(half, bf16)] * 6 + [(h_half, bf16)] * 2
    return pl.pallas_call(
        partial(middle_kernel, blocks),
        grid_spec=pltpu.PrefetchScalarGridSpec(
            num_scalar_prefetch=1,
            grid=(tokens // block,),
            in_specs=[by_token(half)] * 2
            + [by_token(width)] * 2
            + [fixed(vec.shape), fixed(bu.shape)]
            + [pl.BlockSpec(memory_space=pl.ANY)] * (6 + len(after)),
            out_specs=[by_token(n) for n, _ in outs] + [fixed((8, width)), fixed((1, hidden))],
            scratch_shapes=[
                pltpu.VMEM((width, width), bf16),
                pltpu.VMEM((width, hidden), bf16),
                pltpu.VMEM((hidden, width), bf16),
                pltpu.VMEM((block, hidden), f32),
                pltpu.VMEM((block, width), bf16),
                pltpu.SemaphoreType.DMA((10, blocks)),
            ],
        ),
        out_shape=[shape_of((tokens, n), t) for n, t in outs] + [shape_of((8, width), f32), shape_of((1, hidden), f32)],
        compiler_params=pltpu.CompilerParams(vmem_limit_bytes=40 * MIB),
        cost_estimate=pl.CostEstimate(flops=4 * 10**10, bytes_accessed=40 * MIB, transcendentals=0),
    )(order, om, ot, x, c, vec, bu, *up, *down, *after)


def copies(moves, sems, count, first=0, start=True, wait=True):
    def each(k, act):
        for i, (source, target) in enumerate(moves(k)):
            act(pltpu.make_async_copy(source, target, sems.at[first + i, k]))

    if start:
        lax.fori_loop(0, count, lambda k, c: (each(k, lambda copy: copy.start()), c)[1], 0)
    if wait:
        lax.fori_loop(0, count, lambda k, c: (each(k, lambda copy: copy.wait()), c)[1], 0)


def place(k, rows):
    return pl.ds(pl.multiple_of(k * rows, rows), rows)


def project_kernel(blocks, order_ref, x_ref, bias_ref, w_ref, *refs):
    out_ref, weight, sems = refs[-3:]
    rows, left = w_ref.shape[1:]
    right = weight.shape[1] - left

    @pl.when(pl.program_id(0) == 0)
    def _():
        def moves(k):
            at = place(k, rows)
            return [
                (w_ref.at[order_ref[k]], weight.at[at, 0:left]),
                (w_ref.at[blocks + order_ref[blocks + k], :, 0:right], weight.at[at, left : left + right]),
            ]

        copies(moves, sems, blocks)

    out_ref[...] = (dot(x_ref[...], weight[...]) + bias_ref[...]).astype(bf16)


def project(order, flip, x, bias, gathered, after=(), block=512):
    tokens, width = x.shape
    blocks, outs = gathered.shape[0] // 2, bias.shape[1] // 2
    half = lambda i, order: (0, 1 - order[2 * blocks] if flip else order[2 * blocks])
    return pl.pallas_call(
        partial(project_kernel, blocks),
        grid_spec=pltpu.PrefetchScalarGridSpec(
            num_scalar_prefetch=1,
            grid=(tokens // block,),
            in_specs=[
                pl.BlockSpec((block, width), lambda i, order: (i, 0)),
                pl.BlockSpec((1, outs), half),
            ]
            + [pl.BlockSpec(memory_space=pl.ANY)] * (1 + len(after)),
            out_specs=pl.BlockSpec((block, outs), lambda i, order: (i, 0)),
            scratch_shapes=[pltpu.VMEM((width, outs), bf16), pltpu.SemaphoreType.DMA((2, blocks))],
        ),
        out_shape=shape_of((tokens, outs), bf16),
        compiler_params=pltpu.CompilerParams(vmem_limit_bytes=24 * MIB),
        cost_estimate=pl.CostEstimate(flops=2 * tokens * width * outs, bytes_accessed=8 * MIB, transcendentals=0),
    )(order, x, bias, gathered, *after)


def token_kernel(blocks, order_ref, base_ref, dm_ref, dt_ref, wm_ref, wt_ref, *refs):
    out_ref, mine, theirs, sems = refs[-4:]
    rows, left = wm_ref.shape[1:]
    right = mine.shape[1] - left

    @pl.when(pl.program_id(0) == 0)
    def _():
        def moves(k):
            at, i, j = place(k, rows), order_ref[k], blocks + order_ref[blocks + k]
            return [
                (wm_ref.at[i], mine.at[at, 0:left]),
                (wm_ref.at[j, :, 0:right], mine.at[at, left : left + right]),
                (wt_ref.at[i], theirs.at[at, 0:left]),
                (wt_ref.at[j, :, 0:right], theirs.at[at, left : left + right]),
            ]

        copies(moves, sems, blocks)

    total = base_ref[...] + dot(dm_ref[...], mine[...], NT) + dot(dt_ref[...], theirs[...], NT)
    out_ref[...] = total.astype(bf16)


def token_gradient(order, base, dm, dt, gathered, after=(), block=256):
    tokens, width = base.shape
    blocks, outs = gathered[0].shape[0] // 2, dm.shape[1]
    by_token = lambda n: pl.BlockSpec((block, n), lambda i, order: (i, 0))
    return pl.pallas_call(
        partial(token_kernel, blocks),
        grid_spec=pltpu.PrefetchScalarGridSpec(
            num_scalar_prefetch=1,
            grid=(tokens // block,),
            in_specs=[by_token(width), by_token(outs), by_token(outs)]
            + [pl.BlockSpec(memory_space=pl.ANY)] * (2 + len(after)),
            out_specs=by_token(width),
            scratch_shapes=[pltpu.VMEM((width, outs), bf16)] * 2 + [pltpu.SemaphoreType.DMA((4, blocks))],
        ),
        out_shape=shape_of((tokens, width), bf16),
        compiler_params=pltpu.CompilerParams(vmem_limit_bytes=24 * MIB),
        cost_estimate=pl.CostEstimate(flops=4 * tokens * width * outs, bytes_accessed=14 * MIB, transcendentals=0),
    )(order, base, dm, dt, *gathered, *after)


TABLE_AT, UP_AT = 8, 32


def spread_kernel(devices, order_ref, b_ref, line_ref, vec_ref, up_ref, bias_ref, full, tab):
    blocks, rows = b_ref.shape[0:2]
    width, heads = vec_ref.shape[1], 2 * line_ref.shape[0]
    for k in range(blocks):
        full[rows * k : rows * k + rows, :] = b_ref[order_ref[blocks + k]].astype(f32)
    each, per, ups = width // devices, tab.shape[0] // devices, up_ref.shape[1] // devices
    vec_ref[...] = full[...].T[0:8, :]
    for d in range(devices):
        tab[per * d : per * d + per, :] = full[each * d : each * d + per, :]
        up_ref[:, ups * d : ups * d + ups] = full[each * d : each * d + 1, UP_AT : UP_AT + ups]
    table = tab[...].T[TABLE_AT : TABLE_AT + heads, :]
    buckets = table.shape[1]
    half, rest = buckets // 2, (ROW_LEN - buckets) // 2
    ends = [jnp.broadcast_to(table[:, i : i + 1], (heads, rest)) for i in (buckets - 1, 0)]
    lines = jnp.concatenate([table[:, half:], *ends, table[:, :half]], axis=1)
    for g in range(heads // 2):
        line_ref[g] = lines[2 * g : 2 * g + 2, :]
    for g in range(heads // 2):
        bias_ref[:, 384 * g : 384 * g + 128] = vec_ref[0:1, 128 * g : 128 * g + 128]
        bias_ref[:, 384 * g + 128 : 384 * g + 256] = jnp.zeros((1, 128), f32)
        bias_ref[:, 384 * g + 256 : 384 * g + 384] = vec_ref[1:2, 128 * g : 128 * g + 128]


def spread_small(order, b, devices, width, heads, buckets, hidden):
    blocks, rows = b.shape[0] // 2, b.shape[1]
    last = b.shape[2] // 128 - 1
    fixed = lambda s: pl.BlockSpec(s, lambda i, order: (0,) * len(s))
    shapes = [(heads // 2, 2, ROW_LEN), (8, width), (1, hidden), (1, 3 * width)]
    return pl.pallas_call(
        partial(spread_kernel, devices),
        grid_spec=pltpu.PrefetchScalarGridSpec(
            num_scalar_prefetch=1,
            grid=(1,),
            in_specs=[pl.BlockSpec((blocks, rows, 128), lambda i, order: (1, 0, last))],
            out_specs=[fixed(s) for s in shapes],
            scratch_shapes=[pltpu.VMEM((width, 128), f32), pltpu.VMEM((buckets, 128), f32)],
        ),
        out_shape=[shape_of(s, f32) for s in shapes],
        compiler_params=pltpu.CompilerParams(vmem_limit_bytes=8 * MIB),
        cost_estimate=pl.CostEstimate(flops=10**6, bytes_accessed=MIB, transcendentals=0),
    )(order, b)


def collect_kernel(devices, buckets, core_ref, vsum_ref, usum_ref, ms_ref, ts_ref, ml_ref, tl_ref, out_ref, tall, sums, lines):
    core = core_ref[0]
    width = vsum_ref.shape[1]
    pairs = ms_ref.shape[0]
    sums[core], sums[1 - core] = ms_ref[...], ts_ref[...]
    for g in range(pairs):
        lines[core, 2 * g : 2 * g + 2, :] = ml_ref[g]
        lines[1 - core, 2 * g : 2 * g + 2, :] = tl_ref[g]
    tall[...] = jnp.zeros_like(tall)
    tall[2:8, :] = vsum_ref[0:6, :]
    for side in range(2):
        for g in range(pairs):
            at = 128 * (side * pairs + g)
            tall[0:2, at : at + 128] = sums[side, g]
    out_ref[...] = tall[...].T
    line = jnp.concatenate([lines[0], lines[1]], axis=0)
    heads = line.shape[0]
    half, middle = buckets // 2, ROW_LEN // 2
    far = jnp.sum(line[:, half:middle], axis=1, keepdims=True)
    near = jnp.sum(line[:, middle : ROW_LEN - half], axis=1, keepdims=True)
    place = lax.broadcasted_iota(jnp.int32, (heads, half), 1)
    upper = line[:, :half] + jnp.where(place == half - 1, far, 0.0)
    lower = line[:, ROW_LEN - half :] + jnp.where(place == 0, near, 0.0)
    table = jnp.concatenate([lower, upper], axis=1)
    below = jnp.zeros((128 - TABLE_AT - heads, buckets), f32)
    table = jnp.concatenate([jnp.zeros((TABLE_AT, buckets), f32), table, below], axis=0).T
    each, per, ups = width // devices, buckets // devices, usum_ref.shape[1] // devices
    for d in range(devices):
        out_ref[each * d : each * d + per, :] += table[per * d : per * d + per, :]
        out_ref[each * d : each * d + 1, UP_AT : UP_AT + ups] = usum_ref[:, ups * d : ups * d + ups]


def collect_small(core, devices, buckets, vsum, usum, mine, theirs):
    width = vsum.shape[1]
    pairs = mine[1].shape[0]
    args = [vsum, usum, mine[1], theirs[1], mine[0], theirs[0]]
    whole = lambda t: pl.BlockSpec(t.shape, lambda i, core: (0,) * t.ndim)
    return pl.pallas_call(
        partial(collect_kernel, devices, buckets),
        grid_spec=pltpu.PrefetchScalarGridSpec(
            num_scalar_prefetch=1,
            grid=(1,),
            in_specs=[whole(t) for t in args],
            out_specs=pl.BlockSpec((width, 128), lambda i, core: (0, 0)),
            scratch_shapes=[
                pltpu.VMEM((128, width), f32),
                pltpu.VMEM((2, pairs, 2, 128), f32),
                pltpu.VMEM((2, 2 * pairs, ROW_LEN), f32),
            ],
        ),
        out_shape=shape_of((width, 128), f32),
        compiler_params=pltpu.CompilerParams(vmem_limit_bytes=8 * MIB),
        cost_estimate=pl.CostEstimate(flops=10**6, bytes_accessed=MIB, transcendentals=0),
    )(core, *args)


def pack_kernel(core_ref, *refs):
    vectors, (table_ref, up_ref, q_ref, k_ref, v_ref, wo_ref, wu_ref, wd_ref) = refs[:8], refs[8:16]
    outs, (tall, small) = refs[16:22], refs[22:]
    rows = q_ref.shape[0]
    for i, ref in enumerate(vectors):
        tall[i : i + 1, 0:rows] = ref[...]
    small[...] = tall[...].T[0:rows, :]
    lane = lax.broadcasted_iota(jnp.int32, small.shape, 1)
    small[...] = jnp.where(lane < 8, small[...], 0.0)
    per, heads = table_ref.shape
    small[0:per, TABLE_AT : TABLE_AT + heads] = table_ref[...]
    small[0:1, UP_AT : UP_AT + up_ref.shape[1]] = up_ref[...]
    extra = small[...].astype(bf16)
    low = lambda ref, first, last: ref[:, first:last].astype(bf16)
    h, f = wo_ref.shape[1] // 2, wu_ref.shape[1] // 2

    def write(side, square, up, down):
        for g in range(h // 128):
            at = side * h + 128 * g
            for i, ref in enumerate((q_ref, k_ref, v_ref)):
                square[:, 384 * g + 128 * i : 384 * g + 128 * i + 128] = low(ref, at, at + 128)
        square[:, 3 * h : 3 * h + 128] = extra
        up[:, 0:f] = low(wu_ref, side * f, side * f + f)
        up[:, f : f + h] = low(wo_ref, side * h, side * h + h)
        down[...] = low(wd_ref, side * h, side * h + h)

    @pl.when(core_ref[0] == 0)
    def _():
        write(0, *outs[0:3])
        write(1, *outs[3:6])

    @pl.when(core_ref[0] == 1)
    def _():
        write(1, *outs[0:3])
        write(0, *outs[3:6])


def pack(core, vectors, table, up, matrices):
    rows, width = matrices[0].shape
    args = [t.reshape(1, -1) for t in vectors] + [table, up.reshape(1, -1), *matrices]
    whole = lambda s: pl.BlockSpec(s, lambda i, core: (0, 0))
    shapes = [
        (rows, 3 * width // 2 + 128),
        (rows, (matrices[4].shape[1] + width) // 2),
        (matrices[5].shape[0], width // 2),
    ] * 2
    return pl.pallas_call(
        pack_kernel,
        grid_spec=pltpu.PrefetchScalarGridSpec(
            num_scalar_prefetch=1,
            grid=(1,),
            in_specs=[whole(t.shape) for t in args],
            out_specs=[whole(s) for s in shapes],
            scratch_shapes=[pltpu.VMEM((128, 128), f32), pltpu.VMEM((rows, 128), f32)],
        ),
        out_shape=[shape_of(s, bf16) for s in shapes],
        compiler_params=pltpu.CompilerParams(vmem_limit_bytes=60 * MIB),
        cost_estimate=pl.CostEstimate(flops=10**6, bytes_accessed=2 * MIB, transcendentals=0),
    )(core, *args)


class Links:
    def __init__(self, mesh):
        wide, narrow = mesh.shape[WIDE], mesh.shape[NARROW]
        self.sizes = (wide // 2, 2, narrow // 2, 2)
        w, n = lax.axis_index(WIDE), lax.axis_index(NARROW)
        self.place = (w // 2, w % 2, n // 2, n % 2)
        self.core = self.place[CORE]
        self.chips = wide * narrow // 2

    def number(self, at):
        return ((at[Z] * self.sizes[X] + at[X]) * self.sizes[Y] + at[Y]) * 2 + at[CORE]

    def fetch(self, value, axis, step):
        pairs = []
        for z in range(self.sizes[Z]):
            for x in range(self.sizes[X]):
                for y in range(self.sizes[Y]):
                    for c in range(2):
                        here = (z, x, y, c)
                        there = list(here)
                        there[axis] = (there[axis] + step) % self.sizes[axis]
                        pairs.append((self.number(there), self.number(here)))
        return lax.ppermute(value, AXES, pairs)

    def others(self, value, axis):
        return [self.fetch(value, axis, k) for k in range(1, self.sizes[axis])]

    def swapped(self, kept, sent):
        even = self.core == 0
        got = self.fetch(sent, CORE, 1)
        return jnp.where(even, kept, got), jnp.where(even, got, kept)

    def order(self):
        chip = jnp.arange(self.chips, dtype=jnp.int32)
        sz, sx, sy = self.sizes[:3]
        kz = (chip // (sx * sy) - self.place[Z]) % sz
        kx = (chip // sy - self.place[X]) % sx
        ky = (chip - self.place[Y]) % sy
        plane = 2 * ((kz * sy + ky) * sx + kx)
        return jnp.concatenate(
            [
                (ky * sx + kx) * sz + kz,
                (kx * sy + ky) * sz + kz,
                self.core.reshape(1),
                plane,
                plane + 1,
            ]
        ).astype(jnp.int32)

    def finish(self, total):
        rows = total.shape[0] // 2
        even = self.core == 0
        own = jnp.where(even, total[:rows], total[rows:])
        return own, self.fetch(jnp.where(even, total[rows:], total[:rows]), CORE, 1)


def ring(me, k, size):
    at = me + k
    return jnp.where(at >= size, at - size, at)


def fold_1_kernel(halves, sizes, count, place_ref, *refs):
    kept, got, outs = refs[:count], refs[count : 2 * count], refs[2 * count :]
    split = sizes[Y]
    a_outs, b_outs = outs[:split], outs[split:]

    def write(out, at, half, x, y):
        rows, column = out.shape[2], 0
        for piece, part, first, last in half:
            source = (0, x, y, part, slice(None), slice(first, last))
            value = kept[piece][source] + got[piece][source].astype(f32)
            for row in range(0, value.shape[0], rows):
                some = value[row : row + rows, :].astype(out.dtype)
                out[0, at, :, column : column + last - first] = some
                column += last - first

    for k, out in enumerate(a_outs):
        y = ring(place_ref[Y], k, sizes[Y])
        for x in range(sizes[X]):
            write(out, x, halves[0], x, y)
    for k, out in enumerate(b_outs):
        x = ring(place_ref[X], k, sizes[X])
        for y in range(sizes[Y]):
            write(out, y, halves[1], x, y)


def fold_2_kernel(sizes, place_ref, *refs):
    sy, sx = sizes[Y], sizes[X]
    a_in, b_in, outs = refs[:sy], refs[sy : sy + sx], refs[sy + sx :]
    a_outs, b_outs = outs[:sx], outs[sx:]

    def value(ins, at):
        total = ins[0][0, at]
        for piece in ins[1:]:
            total = total + piece[0, at].astype(f32)
        return total

    for k, out in enumerate(a_outs):
        out[0] = value(a_in, ring(place_ref[X], k, sx)).astype(out.dtype)
    for k, out in enumerate(b_outs):
        out[0] = value(b_in, ring(place_ref[Y], k, sy)).astype(out.dtype)


def fold_3_kernel(sizes, place_ref, *refs):
    sy, sx = sizes[Y], sizes[X]
    a_in, b_in, outs = refs[:sx], refs[sx : sx + sy], refs[sx + sy :]
    rows, columns = a_in[0].shape[1:]
    for k, out in enumerate(outs):
        z = ring(place_ref[Z], k, sizes[Z])
        for n, ins in enumerate((a_in, b_in)):
            total = ins[0][z]
            for piece in ins[1:]:
                total = total + piece[z].astype(f32)
            first = n * columns
            out[0, :, first : first + total.shape[1]] = total.astype(out.dtype)


def fold_call(kernel, place, ins, outs, steps):
    block = lambda s: pl.BlockSpec((s[0] // steps,) + tuple(s[1:]), lambda i, place: (i,) + (0,) * (len(s) - 1))
    return pl.pallas_call(
        kernel,
        grid_spec=pltpu.PrefetchScalarGridSpec(
            num_scalar_prefetch=1,
            grid=(steps,),
            in_specs=[block(t.shape) for t in ins],
            out_specs=[block(s) for s, _ in outs],
        ),
        out_shape=[shape_of(s, t) for s, t in outs],
        compiler_params=pltpu.CompilerParams(vmem_limit_bytes=16 * MIB),
        cost_estimate=pl.CostEstimate(flops=10**6, bytes_accessed=8 * MIB, transcendentals=0),
    )(place, *ins)


class Fold:
    def __init__(self, links, halves):
        self.links, self.halves = links, halves
        self.place = jnp.stack(links.place).astype(jnp.int32)

    def to_others(self, values, axis):
        size = self.links.sizes[axis]
        return [self.links.fetch(v, axis, size - k) for k, v in enumerate(values) if k]

    def first(self, kept, got):
        sizes = self.links.sizes
        sz, sx, sy = sizes[:3]
        rows = kept[0].shape[4]
        wide = [sum((e[3] - e[2]) * kept[e[0]].shape[4] // rows for e in half) for half in self.halves]
        kinds = lambda shape, n: [(shape, f32)] + [(shape, bf16)] * (n - 1)
        outs = kinds((sz, sx, rows, wide[0]), sy) + kinds((sz, sy, rows, wide[1]), sx)
        done = fold_call(partial(fold_1_kernel, self.halves, sizes, len(kept)), self.place, [*kept, *got], outs, sz)
        a, b = done[:sy], done[sy:]
        return [a[0], b[0]], self.to_others(a, Y), self.to_others(b, X)

    def second(self, own, got_y, got_x):
        sizes = self.links.sizes
        sz, sx, sy = sizes[:3]
        kinds = lambda t, n: [((sz,) + t.shape[2:], f32)] + [((sz,) + t.shape[2:], bf16)] * (n - 1)
        outs = kinds(own[0], sx) + kinds(own[1], sy)
        done = fold_call(partial(fold_2_kernel, sizes), self.place, [own[0], *got_y, own[1], *got_x], outs, sz)
        a, b = done[:sx], done[sx:]
        return [[a[0], b[0]], self.to_others(a, X), self.to_others(b, Y)]

    def third(self, own, got_x, got_y):
        sizes = self.links.sizes
        rows, ca = own[0].shape[1:]
        shape = (1, rows, ca + own[1].shape[2])
        outs = [(shape, f32)] + [(shape, bf16)] * (sizes[Z] - 1)
        ins = [own[0], *got_x, own[1], *got_y]
        done = fold_call(partial(fold_3_kernel, sizes), self.place, ins, outs, 1)
        return done[0], self.to_others(done, Z)

    def last(self, own, got):
        for piece in got:
            own = own + piece.astype(f32)
        return own[0]


def last_kernel(heads, core_ref, own_ref, *refs):
    pieces, outs = refs[: -(2 + 8 + 2)], refs[-(2 + 8 + 2) :]
    keep_ref, send_ref, vectors, table_ref, up_ref = outs[0], outs[1], outs[2:10], outs[10], outs[11]
    rows, width = keep_ref.shape
    total = own_ref[0]
    for piece in pieces:
        total = total + piece[0].astype(f32)

    def write(own, other):
        keep_ref[...] = own[:, 0:width]
        send_ref[...] = other[:, 0:width]
        small = own[:, width:]
        table_ref[...] = small[0 : table_ref.shape[0], TABLE_AT : TABLE_AT + heads]
        up_ref[...] = small[0:1, UP_AT : UP_AT + up_ref.shape[1]]
        turned = jnp.concatenate([small, jnp.zeros((128 - rows, 128), f32)], axis=0).T
        for i, ref in enumerate(vectors):
            ref[...] = turned[i : i + 1, 0:rows]

    @pl.when(core_ref[0] == 0)
    def _():
        write(total[:rows], total[rows:])

    @pl.when(core_ref[0] == 1)
    def _():
        write(total[rows:], total[:rows])


def join_kernel(core_ref, keep_ref, got_ref, *outs):
    def write(sides):
        for s, side in enumerate(sides):
            for g in range(side.shape[1] // 384):
                at = s * (side.shape[1] // 3) + 128 * g
                for i, out in enumerate(outs):
                    out[:, at : at + 128] = side[:, 384 * g + 128 * i : 384 * g + 128 * i + 128]

    @pl.when(core_ref[0] == 0)
    def _():
        write((keep_ref, got_ref))

    @pl.when(core_ref[0] == 1)
    def _():
        write((got_ref, keep_ref))


def join_wide_kernel(core_ref, keep_ref, got_ref, down_keep_ref, down_got_ref, out_ref, up_ref, down_ref):
    h, f = out_ref.shape[1] // 2, up_ref.shape[1] // 2

    def write(sides, downs):
        for s in range(2):
            up_ref[:, s * f : s * f + f] = sides[s][:, 0:f]
            out_ref[:, s * h : s * h + h] = sides[s][:, f : f + h]
            down_ref[:, s * h : s * h + h] = downs[s][...]

    @pl.when(core_ref[0] == 0)
    def _():
        write((keep_ref, got_ref), (down_keep_ref, down_got_ref))

    @pl.when(core_ref[0] == 1)
    def _():
        write((got_ref, keep_ref), (down_got_ref, down_keep_ref))


def whole_call(kernel, core, ins, outs):
    whole = lambda s: pl.BlockSpec(s, lambda i, core: (0,) * len(s))
    return pl.pallas_call(
        kernel,
        grid_spec=pltpu.PrefetchScalarGridSpec(
            num_scalar_prefetch=1,
            grid=(1,),
            in_specs=[whole(t.shape) for t in ins],
            out_specs=[whole(s) for s in outs],
        ),
        out_shape=[shape_of(s, f32) for s in outs],
        compiler_params=pltpu.CompilerParams(vmem_limit_bytes=16 * MIB),
        cost_estimate=pl.CostEstimate(flops=10**6, bytes_accessed=2 * MIB, transcendentals=0),
    )(core, *ins)


def segments(lengths):
    place = jnp.arange(ROW_LEN, dtype=jnp.int32)
    ending = jnp.cumsum(lengths, axis=1)
    return jnp.sum((place[None, :, None] >= ending[:, None, :]).astype(jnp.int32), axis=2)


def per_device(
    mesh, tokens, cotangent, pair_lengths, w_query, w_key, w_value, w_output, w_up, w_down, b_query, b_value,
    b_output, b_up, b_down, first_gain, first_shift, second_gain, second_shift, bucket_bias,
):
    links = Links(mesh)
    devices = 2 * links.chips
    rows, width = w_query.shape
    hidden = w_up.shape[1]
    heads = bucket_bias.shape[1]
    buckets = bucket_bias.shape[0] * devices
    w_half, h_half = width // 2, hidden // 2
    low = lambda t: t.astype(bf16)
    barrier = lax.optimization_barrier
    core = links.core
    even = core == 0
    order = links.order()
    blocks = lambda a, b: [a, b]
    deep = square_blocks = lambda t: t
    if (2 * rows) % 16 or w_down.shape[0] % 16:
        found, order = order, jnp.concatenate([jnp.zeros((2,), jnp.int32), core.reshape(1), jnp.arange(2, dtype=jnp.int32)])
        n = links.chips
        sort = lambda t, first: jnp.take(t, found[first : first + n], axis=0)

        def blocks(a, b):
            return [t.reshape(1, -1, t.shape[2]) for t in (sort(a, 0), sort(b, n))]

        def square_blocks(t):
            return jnp.stack([sort(t[:n], 0), sort(t[n:], n)]).reshape(2, -1, t.shape[2])

        def deep(t):
            both = jnp.stack([sort(t, 2 * n + 1), sort(t, 3 * n + 1)], axis=1)
            return both.reshape(2, -1, t.shape[2])

    half = 3 * w_half
    cut = (half + 128) // 2
    up_cut = (h_half + w_half + 128) // 256 * 128
    packed = pack(
        core.reshape(1),
        [b_query, b_value, b_output, b_down, first_gain, first_shift, second_gain, second_shift],
        bucket_bias,
        b_up,
        [w_query, w_key, w_value, w_output, w_up, w_down],
    )
    swapped = lambda i: jnp.concatenate(links.swapped(packed[i], packed[i + 3]), axis=0)
    pair = swapped(0)
    pair_z = links.others(pair, Z)
    up_pair = swapped(1)
    down_pair = jnp.stack(links.swapped(packed[2], packed[5]))
    down_x = links.others(down_pair, X)

    def together(*groups):
        sizes = [len(g) for g in groups]
        flat = barrier(tuple(t for g in groups for t in g))
        out = []
        for size in sizes:
            out.append(list(flat[:size]))
            flat = flat[size:]
        return out

    def spans(*groups):
        leaves, tree = jax.tree.flatten(tuple(groups))
        return jax.tree.unflatten(tree, barrier(tuple(leaves)))

    def chips(value, got):
        value = jnp.stack([value] + got)
        return value.reshape((-1,) + value.shape[-2:])

    def plane_1(value, cut):
        return [value[:, :, :cut], value[:, :, cut:]], links.others(value[:, :, :cut], X), links.others(value[:, :, cut:], Y)

    def plane_2(ab, got_x, got_y):
        ab = [chips(ab[0], got_x), chips(ab[1], got_y)]
        return ab, links.others(ab[0], Y), links.others(ab[1], X)

    def plane_3(ab, got_y, got_x):
        return chips(ab[0], got_y), chips(ab[1], got_x)

    pair_z, (pair, up_pair), down_x = together(pair_z, (pair, up_pair), down_x)
    stage = plane_1(jnp.stack([pair] + pair_z), cut)
    down_pair = jnp.stack([down_pair] + down_x)
    down_y = links.others(down_pair, Y)
    up_z = links.others(up_pair, Z)
    got_x, got_y, down_y, up_z, (up_pair,) = together(*stage[1:], down_y, up_z, (up_pair,))
    stage = plane_2(stage[0], got_x, got_y)
    down_own = jnp.stack([down_pair] + down_y)
    down_z = links.others(down_own, Z)
    got_y, got_x, up_z, down_z[-1:] = together(*stage[1:], up_z, down_z[-1:])
    mine = jnp.concatenate(plane_3(stage[0], got_y, got_x), axis=0)

    theirs = links.fetch(mine, CORE, 1)
    mine, theirs = square_blocks(mine), square_blocks(theirs)
    lines, vectors, up_bias, bias = spread_small(order, mine, devices, width, heads, buckets, hidden)
    segment = segments(pair_lengths)
    segc, segr = segment[:, :, None], segment[:, None, :]
    pairs = heads // 4
    first_m, first_t = (core * pairs).reshape(1), ((1 - core) * pairs).reshape(1)
    qkv_m = project(order, False, tokens, bias, mine)
    up_z, (qkv_m, bias_t, theirs) = together(up_z, (qkv_m, bias, theirs))
    up_stage = plane_1(jnp.stack([up_pair] + up_z), up_cut)
    o_m, p_m = attend_forward(first_m, lines, segc, segr, qkv_m)
    (o_m, theirs), got_x, got_y = together((o_m, theirs), up_stage[1], up_stage[2])

    up_stage = plane_2(up_stage[0], got_x, got_y)
    qkv_t = project(order, True, tokens, bias_t, theirs)
    o_t, p_t = attend_forward(first_t, lines, segc, segr, qkv_t)
    (o_m, o_t), got_y, got_x = together((o_m, o_t), *up_stage[1:])
    up_a, up_b = plane_3(up_stage[0], got_y, got_x)
    up_theirs = (links.fetch(up_a, CORE, 1), links.fetch(up_b, CORE, 1))
    up_a, up_b, *down_z = barrier((up_a, up_b, *down_z))
    down_mine = jnp.stack([down_own] + down_z)
    down_mine = down_mine.reshape((-1,) + down_mine.shape[-2:])
    down_theirs = links.fetch(down_mine, CORE, 1)

    result, dh1, settled, active, do_m, do_t, dy1_m, dy1_t, dy2_m, dy2_t, dz_m, dz_t, vsum, usum = middle(
        order,
        o_m,
        o_t,
        tokens,
        cotangent,
        vectors,
        up_bias,
        blocks(up_a, up_b) + blocks(*up_theirs),
        [deep(down_mine), deep(down_theirs)],
    )

    def pieces(t, parts=1):
        return t.reshape(links.sizes[:3] + (parts, -1, t.shape[1]))

    exchange = lambda *values: [links.fetch(low(t), CORE, 1) for t in values]
    o_both = jnp.where(even, jnp.concatenate([o_m, o_t], axis=1), jnp.concatenate([o_t, o_m], axis=1))
    outs = [dot(o_both, t, TN) for t in (dy1_t, dy1_m)]
    outs, (dz_t, dz_m, settled) = together(outs, (dz_t, dz_m, settled))
    up_parts = lambda dz, out: [pieces(dot(settled, dz, TN)), pieces(out)]
    wide_fold = Fold(
        links,
        [
            [(0, 0, 0, up_cut), (2, 0, 0, w_half)],
            [(0, 0, up_cut, h_half), (1, 0, 0, w_half), (2, 1, 0, w_half)],
        ],
    )
    square_fold = Fold(links, [[(0, 0, 0, cut)], [(0, 0, cut, half), (1, 0, 0, 128)]])

    got = exchange(*up_parts(dz_t, outs[0]))
    kept = up_parts(dz_m, outs[1])
    got, kept, (dy2_t, dy2_m) = spans(got, kept, (dy2_t, dy2_m))
    got += exchange(pieces(dot(active, dy2_t, TN), 2))
    kept += [pieces(dot(active, dy2_m, TN), 2)]
    got, kept, (do_t, do_m) = spans(got, kept, (do_t, do_m))

    wide = wide_fold.first(kept, got)
    grads_t, grads_m = attend_backward((qkv_t, do_t, o_t, p_t), (qkv_m, do_m, o_m, p_m))
    wide, grads_t, grads_m = spans(wide, grads_t, grads_m)

    wide = wide_fold.second(*wide)
    wide[0], grads_t, grads_m = spans(wide[0], grads_t, grads_m)
    square_got = exchange(pieces(dot(tokens, grads_t[0], TN)))
    g_small = pieces(collect_small(core.reshape(1), devices, buckets, vsum, usum, grads_m[1:], grads_t[1:]))
    square_got += exchange(g_small)
    square_kept = [pieces(dot(tokens, grads_m[0], TN)), g_small]
    wide, square_kept, square_got, (d_m, d_t) = spans(wide, square_kept, square_got, (grads_m[0], grads_t[0]))

    square = square_fold.first(square_kept, square_got)
    wide_own, wide_got = wide_fold.third(*wide)
    grad_tokens = token_gradient(order, dh1, d_m, d_t, [mine, theirs])
    square, grad_tokens = spans(square, grad_tokens)

    square = square_fold.second(*square)
    square = spans(square)[0]
    square_own, square_z = square_fold.third(*square)
    wide_got, square_own = spans(wide_got, square_own)
    wide_total = wide_fold.last(wide_own, wide_got)
    wide_a = up_cut + 2 * w_half
    up_total = jnp.concatenate([wide_total[:, :up_cut], wide_total[:, wide_a : wide_a + h_half + w_half - up_cut]], axis=1)
    groups = w_down.shape[0] // (2 * rows)
    down_total = jnp.stack(
        [
            jnp.concatenate([wide_total[:, first + w_half * i : first + w_half * (i + 1)] for i in range(groups)], axis=0)
            for first in (up_cut, wide_total.shape[1] - groups * w_half)
        ]
    ).reshape(-1, w_half)

    core_1 = core.reshape(1)
    out_output, out_up, out_down = whole_call(
        join_wide_kernel,
        core_1,
        [*links.finish(up_total), *links.finish(down_total)],
        [(rows, width), (rows, hidden), w_down.shape],
    )
    shapes = [(rows, half)] * 2 + [(1, rows)] * 8 + [bucket_bias.shape, (1, b_up.shape[0])]
    own, other, *flat = whole_call(partial(last_kernel, heads), core_1, [square_own, *square_z], shapes)
    *flat, out_table, out_b_up = flat
    flat = [t.reshape(-1) for t in flat]
    out_query, out_key, out_value = whole_call(
        join_kernel, core_1, [own, links.fetch(other, CORE, 1)], [(rows, width)] * 3
    )
    return (
        result,
        grad_tokens,
        out_query,
        out_key,
        out_value,
        out_output,
        out_up,
        out_down,
        flat[0],
        flat[1],
        flat[2],
        out_b_up.reshape(-1),
        flat[3],
        flat[4],
        flat[5],
        flat[6],
        flat[7],
        out_table,
    )


def solution(mesh):
    split, line = P(AXES, None), P(AXES)
    return jax.shard_map(
        partial(per_device, mesh),
        mesh=mesh,
        in_specs=(split,) * 9 + (line,) * 9 + (split,),
        out_specs=(split,) * 8 + (line,) * 9 + (split,),
        check_vma=False,
    )
```
